32 devices in a mesh: dp: 4 (over y, x), mp: 8 (over z, core).
Axes of the slice: x: 2, y: 2, z: 4, core: 2. Of those that a mesh axis runs over, the one named last changes fastest.
Arguments:
- source_ids: int32 [8, 1024], P('dp'), may hold values from 0 to 32127
- target_ids: int32 [8, 1024], P('dp'), may hold values from 0 to 32127
- prefix: int32 [8], replicated, may hold values from 192 to 832
- attn_in: float32 [3, 1024, 2048], P(None, ('dp', 'mp')), may hold values from -0.1875 to 0.1875
- attn_out: float32 [3, 1024, 1024], P(None, ('dp', 'mp')), may hold values from -6 to 6
- ff_in: float32 [2, 1024, 5632], P(None, ('dp', 'mp')), may hold values from -0.1875 to 0.1875
- ff_out: float32 [2, 2816, 1024], P(None, ('dp', 'mp')), may hold values from -0.109375 to 0.109375
- table: float32 [32128, 1024], P('mp', 'dp')
- gains: float32 [7, 1024], P(None, ('dp', 'mp'))
- attn_in_mom: float32 [3, 1024, 2048], P(None, ('dp', 'mp')), may hold values from -1.4901161e-08 to 1.4901161e-08
- attn_out_mom: float32 [3, 1024, 1024], P(None, ('dp', 'mp')), may hold values from -1.4901161e-08 to 1.4901161e-08
- ff_in_mom: float32 [2, 1024, 5632], P(None, ('dp', 'mp')), may hold values from -1.4901161e-08 to 1.4901161e-08
- ff_out_mom: float32 [2, 2816, 1024], P(None, ('dp', 'mp')), may hold values from -1.4901161e-08 to 1.4901161e-08
- table_mom: float32 [32128, 1024], P('mp', 'dp'), may hold values from -7.450581e-09 to 7.450581e-09
- gains_mom: float32 [7, 1024], P(None, ('dp', 'mp')), may hold values from -8.940697e-08 to 8.940697e-08
- attn_in_avg: float32 [3, 1024, 2048], P(None, ('dp', 'mp')), may hold values from -0.1875 to 0.1875
- attn_out_avg: float32 [3, 1024, 1024], P(None, ('dp', 'mp')), may hold values from -6 to 6
- ff_in_avg: float32 [2, 1024, 5632], P(None, ('dp', 'mp')), may hold values from -0.1875 to 0.1875
- ff_out_avg: float32 [2, 2816, 1024], P(None, ('dp', 'mp')), may hold values from -0.109375 to 0.109375
- table_avg: float32 [32128, 1024], P('mp', 'dp'), may hold values from -8 to 8
- gains_avg: float32 [7, 1024], P(None, ('dp', 'mp')), may hold values from 0.5 to 1.5
Outputs:
- loss_sum: float32 [], replicated
- scored_count: float32 [], replicated
- grad_norm: float32 [], replicated
- new_attn_in: float32 [3, 1024, 2048], P(None, ('dp', 'mp'))
- new_attn_out: float32 [3, 1024, 1024], P(None, ('dp', 'mp'))
- new_ff_in: float32 [2, 1024, 5632], P(None, ('dp', 'mp'))
- new_ff_out: float32 [2, 2816, 1024], P(None, ('dp', 'mp'))
- new_table: float32 [32128, 1024], P('mp', 'dp')
- new_gains: float32 [7, 1024], P(None, ('dp', 'mp'))
- mom_attn_in: float32 [3, 1024, 2048], P(None, ('dp', 'mp'))
- mom_attn_out: float32 [3, 1024, 1024], P(None, ('dp', 'mp'))
- mom_ff_in: float32 [2, 1024, 5632], P(None, ('dp', 'mp'))
- mom_ff_out: float32 [2, 2816, 1024], P(None, ('dp', 'mp'))
- mom_table: float32 [32128, 1024], P('mp', 'dp')
- mom_gains: float32 [7, 1024], P(None, ('dp', 'mp'))
- avg_attn_in: float32 [3, 1024, 2048], P(None, ('dp', 'mp'))
- avg_attn_out: float32 [3, 1024, 1024], P(None, ('dp', 'mp'))
- avg_ff_in: float32 [2, 1024, 5632], P(None, ('dp', 'mp'))
- avg_ff_out: float32 [2, 2816, 1024], P(None, ('dp', 'mp'))
- avg_table: float32 [32128, 1024], P('mp', 'dp')
- avg_gains: float32 [7, 1024], P(None, ('dp', 'mp'))
The draws below stay inside these ranges and needn't reach their ends.
All inputs are finite; a program needn't handle non-finite values.
Results may differ from the reference program's by a relative error of at most 0.0095.
The reference program's roundings to bfloat16 on the way count: a program that leaves them out, or rounds other values in their place, can miss the bound.
Values may be sent and summed in bfloat16 or wider, within the bound.
A program may use at most 384 MiB of HBM per device.

```python
import math
from functools import partial
import jax
import jax.numpy as jnp
import numpy as np
from jax import lax

D = 1024
HQ = 16
HK = 8
HD = 64
FF = 2816
VOCAB = 32128
LEN = 1024
SEQ_GRP = 2
ITEMS = 8
QW = 1024
KW = 512
PARAMS = 59644928


def draw_prefix(key, part):
    key = jax.random.fold_in(key, 11)
    high_key, low_key, jitter_key = jax.random.split(key, 3)
    groups = ITEMS // SEQ_GRP
    positions = jnp.arange(ITEMS, dtype=jnp.int32)
    group_of = positions // SEQ_GRP
    scored_base = LEN * (groups - 1 + 2 * group_of) // (4 * (groups - 1))
    reach = LEN // 16
    jitter = jax.random.randint(jitter_key, (ITEMS,), -reach, reach + 1)
    high_item = jax.random.randint(high_key, (), 0, SEQ_GRP)
    low_item = ITEMS - SEQ_GRP + jax.random.randint(low_key, (), 0, SEQ_GRP)
    jitter = jnp.where(positions == high_item, -reach, jitter)
    jitter = jnp.where(positions == low_item, reach, jitter)
    return jnp.clip(LEN - scored_base - jitter, 1, LEN - 1).astype(jnp.int32)


def draw_table(key, part):
    key = jax.random.fold_in(key, 12)
    placed = jnp.arange(VOCAB, dtype=jnp.float32)[:, None] / VOCAB
    values = jax.random.normal(key, (VOCAB, D), jnp.float32) * (1.0 + 2.0 * placed)
    return values


def draw_gains(key, part):
    key = jax.random.fold_in(key, 13)
    placed = jnp.arange(D, dtype=jnp.float32)[None, :] / D
    values = (1.0 + 0.1 * jax.random.normal(key, (7, D), jnp.float32)) * (0.5 + placed)
    return values


def touch_ends(entries, own_key, low, top_value):
    dims = entries.shape
    index_at = [jax.random.randint(jax.random.fold_in(own_key, axis), (), 0, dims[axis]) for axis in range(len(dims))]
    entries = entries.at[tuple(index_at)].set(low)
    longest = dims.index(max(dims))
    index_at[longest] = (index_at[longest] + 1) % dims[longest]
    return entries.at[tuple(index_at)].set(top_value)


def level_of(stream_key, extent, pieces, low, largest):
    def one(dim, parts):
        draws = jax.random.uniform(jax.random.fold_in(jax.random.fold_in(stream_key, 6), dim), (parts,), jnp.float32, low / len(pieces), largest / len(pieces))
        return jnp.repeat(jnp.exp(draws), extent[dim] // parts).reshape((-1,) + (1,) * (len(extent) - dim - 1))

    factor_of = one(*pieces[0])
    for cut in pieces[1:]:
        factor_of = factor_of * one(*cut)
    return factor_of


def rank_bounds(count, skew):
    loads = [(1 << 20) // math.isqrt(grade ** skew) + 1 for grade in range(1, count + 1)]
    spread = 1 + sum(loads) // (1 << 30)
    return np.cumsum(np.array([max(1, weight // spread) for weight in loads]))


def ranked(own_key, extent, number_of, lean):
    grid = rank_bounds(number_of, lean)
    lot = jax.random.randint(jax.random.fold_in(own_key, 1), extent, 0, int(grid[number_of - 1]))
    standing = jnp.searchsorted(jnp.asarray(grid, jnp.int32), lot, side="right")
    return jax.random.permutation(jax.random.fold_in(own_key, 2), number_of)[standing].astype(jnp.int32)


def normal_values(key, extent, deviation, limit, cuts=(), held_as=jnp.bfloat16):
    entries = deviation * jax.random.normal(key, extent, jnp.float32)
    if cuts:
        entries = entries * level_of(key, extent, cuts, -0.22, 0.18)
    return jnp.clip(entries, -limit, limit).astype(held_as)


def setup_inputs(seed: int = 0) -> dict:
    arg_keys = jax.random.split(jax.random.key(seed), 22)
    source_ids = touch_ends(ranked(arg_keys[0], (ITEMS, LEN), VOCAB, 2), jax.random.fold_in(arg_keys[0], 3), 0, VOCAB - 1).astype(jnp.int32)
    target_ids = touch_ends(ranked(arg_keys[1], (ITEMS, LEN), VOCAB, 2), jax.random.fold_in(arg_keys[1], 3), 0, VOCAB - 1).astype(jnp.int32)
    prefix = draw_prefix(jax.random.fold_in(arg_keys[21], 71), 0)
    attn_in = normal_values(arg_keys[3], (3, D, QW + 2 * KW), D ** -0.5, 0.1875, ((1, 32),), jnp.float32)
    attn_out = normal_values(arg_keys[4], (3, QW, D), (max(QW // LEN, 1)) ** -0.5, 6.0, ((1, 32),), jnp.float32)
    ff_in = normal_values(arg_keys[5], (2, D, 2 * FF), D ** -0.5, 0.1875, ((1, 32),), jnp.float32)
    ff_out = normal_values(arg_keys[6], (2, FF, D), FF ** -0.5, 0.109375, ((1, 32),), jnp.float32)
    table = draw_table(jax.random.fold_in(arg_keys[21], 71), 0)
    gains = draw_gains(jax.random.fold_in(arg_keys[21], 71), 0)
    attn_in_mom = normal_values(arg_keys[9], (3, D, QW + 2 * KW), (0.000022 * PARAMS ** -0.5), 1.4901161193847656e-08, ((1, 32),), jnp.float32)
    attn_out_mom = normal_values(arg_keys[10], (3, QW, D), (0.000022 * PARAMS ** -0.5), 1.4901161193847656e-08, ((1, 32),), jnp.float32)
    ff_in_mom = normal_values(arg_keys[11], (2, D, 2 * FF), (0.000022 * PARAMS ** -0.5), 1.4901161193847656e-08, ((1, 32),), jnp.float32)
    ff_out_mom = normal_values(arg_keys[12], (2, FF, D), (0.000022 * PARAMS ** -0.5), 1.4901161193847656e-08, ((1, 32),), jnp.float32)
    table_mom = normal_values(arg_keys[13], (VOCAB, D), (0.000011 * PARAMS ** -0.5), 7.450580596923828e-09, ((0, 8), (1, 4)), jnp.float32)
    gains_mom = normal_values(arg_keys[14], (7, D), (0.00011 * PARAMS ** -0.5), 8.940696716308594e-08, ((1, 32),), jnp.float32)
    attn_in_avg = normal_values(arg_keys[15], (3, D, QW + 2 * KW), D ** -0.5, 0.1875, ((1, 32),), jnp.float32)
    attn_out_avg = normal_values(arg_keys[16], (3, QW, D), (max(QW // LEN, 1)) ** -0.5, 6.0, ((1, 32),), jnp.float32)
    ff_in_avg = normal_values(arg_keys[17], (2, D, 2 * FF), D ** -0.5, 0.1875, ((1, 32),), jnp.float32)
    ff_out_avg = normal_values(arg_keys[18], (2, FF, D), FF ** -0.5, 0.109375, ((1, 32),), jnp.float32)
    table_avg = normal_values(arg_keys[19], (VOCAB, D), 1.5, 8.0, ((0, 8), (1, 4)), jnp.float32)
    gains_avg = jnp.clip(1.0 + 0.1 * jax.random.normal(arg_keys[20], (7, D), jnp.float32), 0.5, 1.5)
    return dict(source_ids=source_ids, target_ids=target_ids, prefix=prefix, attn_in=attn_in, attn_out=attn_out, ff_in=ff_in, ff_out=ff_out, table=table, gains=gains, attn_in_mom=attn_in_mom, attn_out_mom=attn_out_mom, ff_in_mom=ff_in_mom, ff_out_mom=ff_out_mom, table_mom=table_mom, gains_mom=gains_mom, attn_in_avg=attn_in_avg, attn_out_avg=attn_out_avg, ff_in_avg=ff_in_avg, ff_out_avg=ff_out_avg, table_avg=table_avg, gains_avg=gains_avg)


@jax.custom_vjp
def low(v):
    return lax.optimization_barrier(v.astype(jnp.bfloat16)).astype(jnp.float32)

@jax.custom_vjp
def low_back(v):
    return v

def low_keep(v):
    return (low(v), None)

def low_pass(kept, grad):
    return (grad,)

def back_keep(v):
    return (v, None)

def back_low(kept, grad):
    return (low(grad),)
low.defvjp(low_keep, low_pass)
low_back.defvjp(back_keep, back_low)
HIGH = lax.Precision.HIGHEST
MOMENTUM = 0.9
AVERAGE = 0.9
CLIP = 0.0002
EPS = 1e-06

def step_rates():
    base_rate = 3.5 * PARAMS ** 0.5 / CLIP
    return (base_rate * D ** (-0.5), base_rate * max(QW // LEN, 1) ** (-0.5), base_rate * D ** (-0.5), base_rate * FF ** (-0.5), base_rate * 2.0, base_rate * 0.3)

def matmul(left, right):
    return jnp.matmul(left, right, precision=HIGH)

def rms_norm(stream, gain_row):
    return stream * lax.rsqrt(lax.optimization_barrier(jnp.mean(stream * stream, axis=-1, keepdims=True)) + EPS) * gain_row

def attend_one(causal, item_pair):
    queries, keyvals = item_pair
    length = queries.shape[0]
    key_length = keyvals.shape[0]
    query_heads = queries.reshape(length, HK, HQ // HK, HD)
    key_heads = keyvals[:, :KW].reshape(key_length, HK, HD)
    value_heads = keyvals[:, KW:].reshape(key_length, HK, HD)
    scores = low_back(jnp.einsum('qhgd,khd->hgqk', query_heads, key_heads, precision=HIGH) * HD ** (-0.5))
    if causal:
        allowed = jnp.arange(length)[:, None] >= jnp.arange(key_length)[None, :]
        scores = jnp.where(allowed, scores, -1000000000.0)
    attn_probs = low(jax.nn.softmax(scores, axis=-1))
    mixed = jnp.einsum('hgqk,khd->qhgd', attn_probs, value_heads, precision=HIGH)
    return low_back(low(mixed.reshape(length, QW)))

def attention_block(stream, source, weight_in, weight_out, gain_row, causal):
    normed = low(rms_norm(stream, gain_row))
    anchor = normed if source is None else source
    queries = low_back(low(matmul(normed, weight_in[:, :QW])))
    keyvals = low_back(low(matmul(anchor, weight_in[:, QW:])))
    mixed = lax.map(jax.checkpoint(partial(attend_one, causal)), (queries, keyvals))
    return stream + low_back(matmul(mixed, weight_out))

def feed_forward(stream, weight_in, weight_out, gain_row):
    normed = low(rms_norm(stream, gain_row))
    both = low_back(matmul(normed, weight_in))
    hidden_act = low(jax.nn.gelu(both[..., :FF], approximate=True) * both[..., FF:])
    return stream + low_back(matmul(hidden_act, weight_out))

def row_loss(table_low, item_triple):
    hidden, target_row, weight_row = item_triple
    logits = low_back(matmul(hidden, table_low.T) * D ** (-0.5))
    log_norm = jax.nn.logsumexp(logits, axis=-1)
    picked = jnp.take_along_axis(logits, target_row[:, None], axis=1)[:, 0]
    return jnp.sum((log_norm - picked) * weight_row)

def forward(attn_in, attn_out, ff_in, ff_out, table, gains, source_ids, decoder_ids, target_ids, scored):
    a_in, a_out, f_in, f_out = (low(attn_in), low(attn_out), low(ff_in), low(ff_out))
    table_low, gain_low = (low(table), low(gains))
    stream = low_back(table_low[source_ids])
    stream = attention_block(stream, None, a_in[0], a_out[0], gain_low[0], False)
    stream = feed_forward(stream, f_in[0], f_out[0], gain_low[1])
    encoded = low(rms_norm(stream, gain_low[2]))
    decoded = low_back(table_low[decoder_ids])
    decoded = attention_block(decoded, None, a_in[1], a_out[1], gain_low[3], True)
    decoded = attention_block(decoded, encoded, a_in[2], a_out[2], gain_low[4], False)
    decoded = feed_forward(decoded, f_in[1], f_out[1], gain_low[5])
    hidden = low(rms_norm(decoded, gain_low[6]))
    losses = lax.map(jax.checkpoint(partial(row_loss, table_low)), (hidden, target_ids, scored))
    loss_total = jnp.sum(losses)
    return (loss_total / jnp.sum(scored), loss_total)

def update(weight, gradient, moment, average, rate, factor):
    clipped = gradient * factor
    moment_new = MOMENTUM * moment + (1 - MOMENTUM) * clipped
    weight_new = weight - rate * ((1 - MOMENTUM) * clipped + MOMENTUM * moment_new)
    average_new = AVERAGE * average + (1 - AVERAGE) * weight_new
    return (weight_new, moment_new, average_new)

def reference(source_ids, target_ids, prefix, attn_in, attn_out, ff_in, ff_out, table, gains, attn_in_mom, attn_out_mom, ff_in_mom, ff_out_mom, table_mom, gains_mom, attn_in_avg, attn_out_avg, ff_in_avg, ff_out_avg, table_avg, gains_avg):
    decoder_ids = jnp.concatenate([jnp.zeros((ITEMS, 1), jnp.int32), target_ids[:, :-1]], axis=1)
    scored = (jnp.arange(LEN)[None, :] >= prefix[:, None]).astype(jnp.float32)
    weights = (attn_in, attn_out, ff_in, ff_out, table, gains)

    def objective(*params):
        return forward(*params, source_ids, decoder_ids, target_ids, scored)
    mean_loss, pull_back, loss_total = jax.vjp(objective, *weights, has_aux=True)
    gradients = pull_back(jnp.ones_like(mean_loss))
    squares = sum((jnp.sum(gradient * gradient) for gradient in gradients))
    grad_norm = jnp.sqrt(squares)
    factor = jnp.minimum(1.0, CLIP / grad_norm)
    moments = (attn_in_mom, attn_out_mom, ff_in_mom, ff_out_mom, table_mom, gains_mom)
    averages = (attn_in_avg, attn_out_avg, ff_in_avg, ff_out_avg, table_avg, gains_avg)
    results = [update(weight, gradient, moment, average, rate, factor) for weight, gradient, moment, average, rate in zip(weights, gradients, moments, averages, step_rates())]
    return (loss_total, jnp.sum(scored), grad_norm, results[0][0], results[1][0], results[2][0], results[3][0], results[4][0], results[5][0], results[0][1], results[1][1], results[2][1], results[3][1], results[4][1], results[5][1], results[0][2], results[1][2], results[2][2], results[3][2], results[4][2], results[5][2])
```

```python
from functools import partial

import jax
import jax.numpy as jnp
from jax import lax
from jax.sharding import Mesh
from jax.sharding import PartitionSpec as P

D = 1024
HQ = 16
HK = 8
HD = 64
FF = 2816
LEN = 1024
QW = 1024
KW = 512
PARAMS = 59644928

MOMENTUM = 0.9
AVERAGE = 0.9
CLIP = 0.0002
EPS = 1e-06

BF = jnp.bfloat16
F32 = jnp.float32


def step_rates():
    base_rate = 3.5 * PARAMS**0.5 / CLIP
    return (
        base_rate * D ** (-0.5),
        base_rate * max(QW // LEN, 1) ** (-0.5),
        base_rate * D ** (-0.5),
        base_rate * FF ** (-0.5),
        base_rate * 2.0,
        base_rate * 0.3,
    )


def swap(value, axis):
    return lax.ppermute(value, axis, [(0, 1), (1, 0)])


def take_bit(value, bit, position):
    return lax.dynamic_index_in_dim(value, bit, position, keepdims=False)


def gather_blocks(block, layout, order):
    have = []
    held = block
    for axis in order:
        received = swap(held, axis)
        position = sum(layout.index(other) < layout.index(axis) for other in have)
        bit = lax.axis_index(axis)
        shape = held.shape
        joined = jnp.zeros(shape[:position] + (2,) + shape[position:], held.dtype)
        joined = lax.dynamic_update_index_in_dim(joined, held, bit, position)
        held = lax.dynamic_update_index_in_dim(joined, received, 1 - bit, position)
        have.append(axis)
    return held


def sum_blocks(terms, layout, order, last=F32):
    left = list(layout)
    held = terms
    for axis in order:
        position = left.index(axis)
        bit = lax.axis_index(axis)
        received = swap(take_bit(held, 1 - bit, position), axis)
        held = take_bit(held, bit, position).astype(F32) + received.astype(F32)
        left.remove(axis)
        if left:
            held = held.astype(terms.dtype)
    return held.astype(last)


def mm(left, right):
    return jnp.dot(left, right, preferred_element_type=F32)


def mm_nt(left, right):
    return lax.dot_general(left, right, (((1,), (1,)), ((), ())), preferred_element_type=F32)


def mm_tn(left, right):
    return lax.dot_general(left, right, (((0,), (0,)), ((), ())), preferred_element_type=F32)


def norm_forward(stream, gain_row):
    inverse = lax.rsqrt(jnp.mean(stream * stream, axis=-1, keepdims=True) + EPS)
    return stream * inverse * gain_row


def norm_backward(stream, gain_row, grad_out):
    inverse = lax.rsqrt(jnp.mean(stream * stream, axis=-1, keepdims=True) + EPS)
    scaled = grad_out * gain_row
    d_input = inverse * scaled - stream * inverse**3 * jnp.mean(
        stream * scaled, axis=-1, keepdims=True
    )
    return (d_input, jnp.sum(grad_out * stream * inverse, axis=0))


def head_split(queries, keyvals):
    rows, length = queries.shape[0], keyvals.shape[0]
    query_heads = queries.reshape(rows, HK, HQ // HK, HD)
    key_heads = keyvals[:, :KW].reshape(length, HK, HD)
    value_heads = keyvals[:, KW:].reshape(length, HK, HD)
    return (query_heads, key_heads, value_heads)


def scores_of(query_heads, key_heads, first_row):
    scores = jnp.einsum(
        "rhgd,khd->hgrk", query_heads, key_heads, preferred_element_type=F32
    ) * HD ** (-0.5)
    if first_row is not None:
        rows, length = query_heads.shape[0], key_heads.shape[0]
        allowed = (first_row + jnp.arange(rows))[:, None] >= jnp.arange(length)[None, :]
        scores = jnp.where(allowed, scores, -1000000000.0)
    return scores


def attend_forward(queries, keyvals, first_row):
    query_heads, key_heads, value_heads = head_split(queries, keyvals)
    scores = scores_of(query_heads, key_heads, first_row)
    row_max = jnp.max(scores, axis=-1, keepdims=True)
    expo_terms = jnp.exp(scores - row_max)
    row_total = jnp.sum(expo_terms, axis=-1, keepdims=True)
    attn_probs = (expo_terms / row_total).astype(BF)
    mixed = jnp.einsum("hgrk,khd->rhgd", attn_probs, value_heads, preferred_element_type=F32)
    return (mixed.reshape(queries.shape[0], QW).astype(BF), row_max + jnp.log(row_total))


def attend_backward(queries, keyvals, first_row, log_total, d_mixed):
    rows, length = queries.shape[0], keyvals.shape[0]
    query_heads, key_heads, value_heads = head_split(queries, keyvals)
    attn_probs = jnp.exp(scores_of(query_heads, key_heads, first_row) - log_total)
    d_heads = d_mixed.reshape(rows, HK, HQ // HK, HD)
    d_probs = jnp.einsum("rhgd,khd->hgrk", d_heads, value_heads, preferred_element_type=F32)
    d_scores = attn_probs * (d_probs - jnp.sum(attn_probs * d_probs, axis=-1, keepdims=True))
    d_scores = d_scores.astype(BF)
    d_queries = jnp.einsum(
        "hgrk,khd->rhgd", d_scores, key_heads, preferred_element_type=F32
    ) * HD ** (-0.5)
    d_keys = jnp.einsum(
        "hgrk,rhgd->khd", d_scores, query_heads, preferred_element_type=F32
    ) * HD ** (-0.5)
    d_values = jnp.einsum(
        "hgrk,rhgd->khd", attn_probs.astype(BF), d_heads, preferred_element_type=F32
    )
    d_keyvals = jnp.concatenate(
        [d_keys.reshape(length, KW).astype(BF), d_values.reshape(length, KW).astype(BF)], axis=-1
    )
    return (d_queries.reshape(rows, QW).astype(BF), d_keyvals)


def update(weight, gradient, moment, average, rate, factor):
    clipped = gradient * factor
    moment_new = MOMENTUM * moment + (1 - MOMENTUM) * clipped
    weight_new = weight - rate * ((1 - MOMENTUM) * clipped + MOMENTUM * moment_new)
    average_new = AVERAGE * average + (1 - AVERAGE) * weight_new
    return (weight_new, moment_new, average_new)


def on_device(
    dp_axes,
    mp_axes,
    source_ids,
    target_ids,
    prefix,
    attn_in,
    attn_out,
    ff_in,
    ff_out,
    table,
    gains,
    attn_in_mom,
    attn_out_mom,
    ff_in_mom,
    ff_out_mom,
    table_mom,
    gains_mom,
    attn_in_avg,
    attn_out_avg,
    ff_in_avg,
    ff_out_avg,
    table_avg,
    gains_avg,
):
    every = dp_axes + mp_axes
    core = mp_axes[-1]
    row_axes = mp_axes[1:]
    line = mp_axes[:-1]
    gather_orders = (
        line + dp_axes + (core,),
        line + dp_axes[::-1] + (core,),
        dp_axes + line + (core,),
    )
    sum_orders = tuple(order[::-1] for order in gather_orders)
    two_dp, two_mp, two_rows = (2,) * len(dp_axes), (2,) * len(mp_axes), (2,) * len(row_axes)

    seq_count, length = source_ids.shape
    rows = length // 2 ** len(row_axes)
    first_row = lax.axis_index(row_axes) * rows

    def whole(shard, kind):
        got = gather_blocks(shard.astype(BF), every, gather_orders[kind])
        return got.reshape((-1,) + shard.shape[1:])

    gain_all = gather_blocks(gains.astype(BF).T, every, gather_orders[0])
    gain_all = gain_all.reshape(-1, gains.shape[0]).T.astype(F32)

    a_in = [None] * 3
    a_out = [None] * 3
    gate = [None] * 2
    up = [None] * 2
    down = [None] * 2
    a_in[0] = whole(attn_in[0], 0)
    a_out[0] = whole(attn_out[0], 1)
    a_in[1] = whole(attn_in[1], 2)
    gate[0] = whole(ff_in[0, :, :FF], 0)
    up[0] = whole(ff_in[0, :, FF:], 1)
    down[0] = whole(ff_out[0], 2)
    a_out[1] = whole(attn_out[1], 0)
    a_in[2] = whole(attn_in[2], 1)
    a_out[2] = whole(attn_out[2], 2)
    gate[1] = whole(ff_in[1, :, :FF], 0)
    up[1] = whole(ff_in[1, :, FF:], 1)
    down[1] = whole(ff_out[1], 2)

    vocab_part = table.shape[0]
    offset = lax.axis_index(mp_axes) * vocab_part
    table_bf = table.astype(BF)
    decoder_ids = jnp.concatenate(
        [jnp.zeros((seq_count, 1), jnp.int32), target_ids[:, :-1]], axis=1
    )
    ids_all = gather_blocks(jnp.stack([source_ids, decoder_ids]), dp_axes, dp_axes)
    ids_all = jnp.moveaxis(ids_all, len(dp_axes), 0).reshape(2, -1)
    local_ids = ids_all - offset
    inside = (local_ids >= 0) & (local_ids < vocab_part)

    def embed(which):
        found = jnp.where(
            inside[which][:, None],
            table_bf[jnp.clip(local_ids[which], 0, vocab_part - 1)],
            jnp.zeros((), BF),
        )
        width = found.shape[-1]
        found = found.reshape(two_dp + two_mp + (rows, width))
        found = sum_blocks(found, dp_axes + mp_axes, mp_axes[::-1], BF)
        for position, axis in enumerate(dp_axes):
            bit = lax.axis_index(axis)
            received = swap(take_bit(found, 1 - bit, position), axis)
            kept = take_bit(found, bit, position)
            found = jnp.stack(
                [jnp.where(bit == 0, kept, received), jnp.where(bit == 0, received, kept)],
                axis=position,
            )
        found = found.reshape(-1, rows, width)
        return jnp.moveaxis(found, 0, 1).reshape(rows, -1).astype(F32)

    stream_e = embed(0)
    stream_d = embed(1)

    table_rows = gather_blocks(table_bf, dp_axes, dp_axes[::-1]).reshape(-1, *table.shape)
    table_rows = jnp.moveaxis(table_rows, 0, 1).reshape(vocab_part, -1)

    def spread_keys(own):
        return gather_blocks(own, row_axes, row_axes).reshape(length, -1)

    def attention_forward(stream, source, block, gain_row, start):
        normed = norm_forward(stream, gain_row).astype(BF)
        anchor = normed if source is None else source
        keyvals = spread_keys(mm(anchor, a_in[block][:, QW:]).astype(BF))
        queries = mm(normed, a_in[block][:, :QW]).astype(BF)
        mixed, log_total = attend_forward(queries, keyvals, start)
        out = stream + mm(mixed, a_out[block])
        return (out, (stream, normed, anchor, queries, keyvals, mixed, log_total))

    def ffn_forward(stream, which, gain_row):
        normed = norm_forward(stream, gain_row).astype(BF)
        gate_part = mm(normed, gate[which])
        up_part = mm(normed, up[which])
        hidden_act = (jax.nn.gelu(gate_part, approximate=True) * up_part).astype(BF)
        return (stream + mm(hidden_act, down[which]), (stream, normed, gate_part, up_part))

    stream_e, enc_attn = attention_forward(stream_e, None, 0, gain_all[0], None)
    stream_d, dec_self = attention_forward(stream_d, None, 1, gain_all[3], first_row)
    stream_e, enc_ffn = ffn_forward(stream_e, 0, gain_all[1])
    encoded = norm_forward(stream_e, gain_all[2]).astype(BF)
    stream_d, dec_cross = attention_forward(stream_d, encoded, 2, gain_all[4], None)
    stream_d, dec_ffn = ffn_forward(stream_d, 1, gain_all[5])
    hidden = norm_forward(stream_d, gain_all[6]).astype(BF)

    hidden_all = gather_blocks(hidden, mp_axes, mp_axes).reshape(-1, hidden.shape[-1])
    targets = target_ids.reshape(-1)
    vocab_ids = offset + jnp.arange(vocab_part)
    hits = vocab_ids[None, :] == targets[:, None]
    logits = mm_nt(hidden_all, table_rows) * D ** (-0.5)
    own_max = jnp.max(logits, axis=-1)
    expo = jnp.exp(logits - own_max[:, None])
    stats = jnp.stack(
        [own_max, jnp.sum(expo, axis=-1), jnp.sum(jnp.where(hits, logits, 0.0), axis=-1)]
    )
    expo = expo.astype(BF)
    for axis in mp_axes[::-1]:
        other = swap(stats, axis)
        joint = jnp.maximum(stats[0], other[0])
        stats = jnp.stack(
            [
                joint,
                stats[1] * jnp.exp(stats[0] - joint) + other[1] * jnp.exp(other[0] - joint),
                stats[2] + other[2],
            ]
        )
    log_norm = stats[0] + jnp.log(stats[1])
    prefix_group = lax.dynamic_slice_in_dim(prefix, lax.axis_index(dp_axes) * seq_count, seq_count)
    scored = (jnp.arange(length)[None, :] >= prefix_group[:, None]).astype(F32).reshape(-1)
    scored_count = jnp.sum((length - prefix).astype(F32))
    scale = jnp.exp(own_max - log_norm)
    d_logits = (
        (expo.astype(F32) * scale[:, None] - hits.astype(F32)) * (scored / scored_count)[:, None]
    ).astype(BF)
    d_final = (mm(d_logits, table_rows) * D ** (-0.5)).astype(BF)
    d_final = sum_blocks(d_final.reshape(two_mp + (rows, -1)), mp_axes, mp_axes[::-1])

    head_table = (mm_tn(d_logits, hidden_all) * D ** (-0.5)).astype(BF)
    half = vocab_part // 2
    width = table.shape[1]

    def table_sum(part, order):
        stacked = jnp.stack(jnp.split(part, 2 ** len(dp_axes), axis=1))
        return sum_blocks(stacked.reshape(two_dp + part.shape[:1] + (width,)), dp_axes, order)

    grad_table = jnp.concatenate(
        [table_sum(head_table[:half], dp_axes), table_sum(head_table[half:], dp_axes[::-1])], axis=0
    )

    def own_sum(gradient, kind):
        blocks = gradient.astype(BF).reshape((2,) * len(every) + (-1,) + gradient.shape[1:])
        return sum_blocks(blocks, every, sum_orders[kind])

    def ffn_backward(saved, which, gain_row, d_stream):
        stream, normed, gate_part, up_part = saved
        activated, gelu_pull = jax.vjp(partial(jax.nn.gelu, approximate=True), gate_part)
        hidden_act = (activated * up_part).astype(BF)
        d_branch = d_stream.astype(BF)
        d_hidden = mm_nt(d_branch, down[which])
        d_gate = gelu_pull(d_hidden * up_part)[0].astype(BF)
        d_up = (d_hidden * activated).astype(BF)
        d_normed = mm_nt(d_gate, gate[which]) + mm_nt(d_up, up[which])
        grads = (
            own_sum(mm_tn(normed, d_gate), 0),
            own_sum(mm_tn(normed, d_up), 1),
            own_sum(mm_tn(hidden_act, d_branch), 2),
        )
        d_input, grad_gain = norm_backward(stream, gain_row, d_normed)
        return (d_stream + d_input, grads, grad_gain)

    def attention_backward(saved, cross, block, gain_row, start, d_stream, kinds):
        stream, normed, anchor, queries, keyvals, mixed, log_total = saved
        d_branch = d_stream.astype(BF)
        d_mixed = mm_nt(d_branch, a_out[block]).astype(BF)
        d_queries, d_keyvals = attend_backward(queries, keyvals, start, log_total, d_mixed)
        d_keyvals = sum_blocks(
            d_keyvals.reshape(two_rows + (rows, -1)), row_axes, row_axes[::-1], BF
        )
        d_normed = mm_nt(d_queries, a_in[block][:, :QW])
        d_anchor = mm_nt(d_keyvals, a_in[block][:, QW:])
        if not cross:
            d_normed = d_normed + d_anchor
        grads = (
            own_sum(mm_tn(normed, d_queries), kinds[0]),
            own_sum(mm_tn(anchor, d_keyvals), kinds[1]),
            own_sum(mm_tn(mixed, d_branch), kinds[2]),
        )
        d_input, grad_gain = norm_backward(stream, gain_row, d_normed)
        return (d_stream + d_input, d_anchor, grads, grad_gain)

    d_y, gain6 = norm_backward(stream_d, gain_all[6], d_final)
    d_y, ffn_grads1, gain5 = ffn_backward(dec_ffn, 1, gain_all[5], d_y)
    d_y, d_encoded, attn_grads2, gain4 = attention_backward(
        dec_cross, True, 2, gain_all[4], None, d_y, (0, 1, 2)
    )
    d_y, _, attn_grads1, gain3 = attention_backward(
        dec_self, False, 1, gain_all[3], first_row, d_y, (1, 2, 0)
    )
    d_x, gain2 = norm_backward(stream_e, gain_all[2], d_encoded)
    d_x, ffn_grads0, gain1 = ffn_backward(enc_ffn, 0, gain_all[1], d_x)
    d_x, _, attn_grads0, gain0 = attention_backward(
        enc_attn, False, 0, gain_all[0], None, d_x, (0, 1, 2)
    )

    def spread_rows(d_rows):
        width = table.shape[1]
        piece = jnp.moveaxis(d_rows.astype(BF).reshape(rows, -1, width), 1, 0)
        piece = piece.reshape(two_dp + (rows, width))
        for position, axis in enumerate(dp_axes):
            bit = lax.axis_index(axis)
            received = swap(take_bit(piece, 1 - bit, position), axis)
            kept = take_bit(piece, bit, position)
            piece = jnp.stack(
                [jnp.where(bit == 0, kept, received), jnp.where(bit == 0, received, kept)],
                axis=position,
            )
        piece = piece.reshape((-1, rows, width))
        everyone = gather_blocks(piece, mp_axes, mp_axes)
        everyone = everyone.reshape((2 ** len(mp_axes), -1, rows, width))
        return jnp.moveaxis(everyone, 0, 1).reshape(-1, width)

    def look_back(which, d_rows):
        segment_ids = jnp.where(inside[which], local_ids[which], vocab_part)
        return jax.ops.segment_sum(
            spread_rows(d_rows).astype(F32), segment_ids, num_segments=vocab_part + 1
        )[:vocab_part]

    grad_table = grad_table + look_back(1, d_y) + look_back(0, d_x)

    gain_grads = jnp.stack([gain0, gain1, gain2, gain3, gain4, gain5, gain6])
    gain_blocks = jnp.moveaxis(gain_grads.reshape(gains.shape[0], -1, gains.shape[1]), 1, 0)
    grad_gains = sum_blocks(
        gain_blocks.reshape((2,) * len(every) + gains.shape), every, sum_orders[0]
    )

    attn_grads = (attn_grads0, attn_grads1, attn_grads2)
    gradients = (
        jnp.stack([jnp.concatenate([g[0], g[1]], axis=1) for g in attn_grads]),
        jnp.stack([g[2] for g in attn_grads]),
        jnp.stack([jnp.concatenate([g[0], g[1]], axis=1) for g in (ffn_grads0, ffn_grads1)]),
        jnp.stack([g[2] for g in (ffn_grads0, ffn_grads1)]),
        grad_table,
        grad_gains,
    )

    own_losses = ((log_norm - stats[2]) * scored).reshape(2 ** len(mp_axes), rows)
    loss_part = jnp.sum(take_bit(own_losses, lax.axis_index(mp_axes), 0))
    squares = sum((jnp.sum(gradient * gradient) for gradient in gradients))
    totals = jnp.stack([loss_part, squares])
    for axis in every[::-1]:
        totals = totals + swap(totals, axis)
    loss_sum = totals[0]
    grad_norm = jnp.sqrt(totals[1])
    factor = jnp.minimum(1.0, CLIP / grad_norm)
    weights = (attn_in, attn_out, ff_in, ff_out, table, gains)
    moments = (attn_in_mom, attn_out_mom, ff_in_mom, ff_out_mom, table_mom, gains_mom)
    averages = (attn_in_avg, attn_out_avg, ff_in_avg, ff_out_avg, table_avg, gains_avg)
    results = [
        update(weight, gradient, moment, average, rate, factor)
        for weight, gradient, moment, average, rate in zip(
            weights, gradients, moments, averages, step_rates()
        )
    ]
    return (loss_sum, scored_count, grad_norm) + tuple(
        results[array][kind] for kind in range(3) for array in range(6)
    )


def solution(mesh):
    dp_count, mp_count = mesh.shape["dp"], mesh.shape["mp"]
    dp_axes = tuple(f"d{k}" for k in range(dp_count.bit_length() - 1))
    mp_axes = tuple(f"m{k}" for k in range(mp_count.bit_length() - 1))
    every = dp_axes + mp_axes
    fine = Mesh(mesh.devices.reshape((2,) * len(every)), every)
    rows_split = P(None, every, None)
    params = (rows_split,) * 4 + (P(mp_axes, dp_axes), P(None, every))
    in_specs = (P(dp_axes, None), P(dp_axes, None), P()) + params * 3
    out_specs = (P(), P(), P()) + params * 3
    return jax.shard_map(
        partial(on_device, dp_axes, mp_axes),
        mesh=fine,
        in_specs=in_specs,
        out_specs=out_specs,
        check_vma=False,
    )
```

```python
from functools import partial

import jax
import jax.numpy as jnp
from jax import lax
from jax.experimental import pallas as pl
from jax.experimental.pallas import tpu as pltpu
from jax.sharding import Mesh
from jax.sharding import PartitionSpec as P

D = 1024
HQ = 16
HK = 8
HD = 64
FF = 2816
LEN = 1024
QW = 1024
KW = 512
PARAMS = 59644928

MOMENTUM = 0.9
AVERAGE = 0.9
CLIP = 0.0002
EPS = 1e-06

BF = jnp.bfloat16
F32 = jnp.float32
MESH = pl.DeviceIdType.MESH
CHUNK = 256
LANES = 3


def step_rates():
    base_rate = 3.5 * PARAMS**0.5 / CLIP
    return (
        base_rate * D ** (-0.5),
        base_rate * max(QW // LEN, 1) ** (-0.5),
        base_rate * D ** (-0.5),
        base_rate * FF ** (-0.5),
        base_rate * 2.0,
        base_rate * 0.3,
    )


def swap(value, axis):
    return lax.ppermute(value, axis, [(0, 1), (1, 0)])


def take_bit(value, bit, position):
    return lax.dynamic_index_in_dim(value, bit, position, keepdims=False)


def gather_blocks(block, layout, order):
    have = []
    held = block
    for axis in order:
        received = swap(held, axis)
        position = sum(layout.index(other) < layout.index(axis) for other in have)
        bit = lax.axis_index(axis)
        shape = held.shape
        joined = jnp.zeros(shape[:position] + (2,) + shape[position:], held.dtype)
        joined = lax.dynamic_update_index_in_dim(joined, held, bit, position)
        held = lax.dynamic_update_index_in_dim(joined, received, 1 - bit, position)
        have.append(axis)
    return held


def sum_blocks(terms, layout, order, last=F32):
    left = list(layout)
    held = terms
    for axis in order:
        position = left.index(axis)
        bit = lax.axis_index(axis)
        received = swap(take_bit(held, 1 - bit, position), axis)
        held = take_bit(held, bit, position).astype(F32) + received.astype(F32)
        left.remove(axis)
        if left:
            held = held.astype(terms.dtype)
    return held.astype(last)


def greet(axes):
    barrier = pltpu.get_barrier_semaphore()
    for axis in axes:
        pl.semaphore_signal(
            barrier, inc=1, device_id={axis: 1 - lax.axis_index(axis)}, device_id_type=MESH
        )
    pl.semaphore_wait(barrier, len(axes))


def gather_kernel(layout, units, lanes, count, *refs):
    ins, outs = refs[:count], refs[count : 2 * count]
    own_sem, send_sem, recv_sem = refs[2 * count :]
    bits = {axis: lax.axis_index(axis) for axis in layout}
    depth = len(layout)

    def region(unit, have):
        tensor, start, size, _ = units[unit]
        blocks = tuple(pl.ds(0, 2) if axis in have else bits[axis] for axis in layout)
        return outs[tensor].at[blocks + (slice(None), pl.ds(start, size))]

    own = [
        pltpu.make_async_copy(
            ins[k], outs[k].at[tuple(bits[axis] for axis in layout)], own_sem.at[k]
        )
        for k in range(count)
    ]
    for copy in own:
        copy.start()
    greet(layout)
    for copy in own:
        copy.wait()
    copies = {}
    groups = -(-len(units) // lanes)
    for turn in range(groups + depth - 1):
        for step in reversed(range(depth)):
            first = (turn - step) * lanes
            for unit in range(max(first, 0), min(first + lanes, len(units))):
                order = units[unit][3]
                if step:
                    copies[unit, step - 1].wait_recv()
                source = region(unit, order[:step])
                copy = pltpu.make_async_remote_copy(
                    src_ref=source,
                    dst_ref=source,
                    send_sem=send_sem.at[unit, step],
                    recv_sem=recv_sem.at[unit, step],
                    device_id={order[step]: 1 - bits[order[step]]},
                    device_id_type=MESH,
                )
                copy.start()
                copies[unit, step] = copy
    for unit in range(len(units)):
        copies[unit, depth - 1].wait_recv()
    for copy in copies.values():
        copy.wait_send()


def gather_all(shards, layout, orders):
    units = []
    for tensor, shard in enumerate(shards):
        columns = shard.shape[1]
        pieces = max(1, columns // 1024)
        step = columns // pieces // 128 * 128
        starts = [step * piece for piece in range(pieces)] + [columns]
        for piece in range(pieces):
            order = orders[len(units) % len(orders)]
            units.append((tensor, starts[piece], starts[piece + 1] - starts[piece], order))
    count = len(shards)
    semaphores = pltpu.SemaphoreType.DMA((len(units), len(layout)))
    return pl.pallas_call(
        partial(gather_kernel, layout, tuple(units), LANES, count),
        out_shape=[
            jax.ShapeDtypeStruct((2,) * len(layout) + shard.shape, shard.dtype) for shard in shards
        ],
        in_specs=[pl.BlockSpec(memory_space=pl.ANY)] * count,
        out_specs=[pl.BlockSpec(memory_space=pl.ANY)] * count,
        scratch_shapes=[pltpu.SemaphoreType.DMA((count,)), semaphores, semaphores],
        compiler_params=pltpu.CompilerParams(collective_id=0, has_side_effects=True),
        name="gather_weights",
    )(*shards)


def grad_kernel(layout, orders, bounds, chunks, *refs):
    x_ref, y_ref, out_ref = refs[:3]
    depth = len(layout)
    lanes = len(orders)
    scratch = refs[3:]
    sends, recvs, helds = (
        [scratch[kind * lanes * depth + lane * depth :][:depth] for lane in range(lanes)]
        for kind in range(3)
    )
    send_sem, recv_sem = scratch[3 * lanes * depth :]
    bits = {axis: lax.axis_index(axis) for axis in layout}
    groups = out_ref.shape[0] // lanes
    greet(layout)

    def exchange(lane, step, group):
        axis = orders[lane][step]
        slot = lax.rem(group, 2)
        return pltpu.make_async_remote_copy(
            src_ref=sends[lane][step],
            dst_ref=recvs[lane][step].at[slot],
            send_sem=send_sem.at[lane, step],
            recv_sem=recv_sem.at[lane, step, slot],
            device_id={axis: 1 - bits[axis]},
            device_id_type=MESH,
        )

    def first(lane, group):
        chunk = jnp.minimum(group * lanes + lane, chunks - 1)
        which = sum((chunk >= bound).astype(jnp.int32) for bound in bounds) if bounds else 0
        columns = y_ref[:, pl.ds(pl.multiple_of(chunk * CHUNK, CHUNK), CHUNK)]
        bit = bits[orders[lane][0]]
        given = jnp.dot(x_ref[which, 1 - bit], columns, preferred_element_type=F32)
        sends[lane][0][...] = given.astype(BF).reshape(sends[lane][0].shape)
        exchange(lane, 0, group).start()
        kept = jnp.dot(x_ref[which, bit], columns, preferred_element_type=F32)
        helds[lane][0][...] = kept.reshape(helds[lane][0].shape)

    def later(lane, step, group):
        order = orders[lane]
        slot = lax.rem(group, 2)
        exchange(lane, step - 1, group).wait()
        held, received = helds[lane][step - 1], recvs[lane][step - 1]
        if step == depth:
            out_ref[group * lanes + lane] = held[...] + received[slot].astype(F32)
            return
        position = [axis for axis in layout if axis not in order[:step]].index(order[step])
        bit = bits[order[step]]

        def total(choice):
            index = (slice(None),) * position + (choice,)
            return held[index] + received[(slot,) + index].astype(F32)

        sends[lane][step][...] = total(1 - bit).astype(BF)
        exchange(lane, step, group).start()
        helds[lane][step][...] = total(bit)

    @pl.loop(0, groups + depth)
    def _(turn):
        for step in reversed(range(depth + 1)):
            group = turn - step

            @pl.when((group >= 0) & (group < groups))
            def _():
                for lane in range(lanes):
                    if step:
                        later(lane, step, group)
                    else:
                        first(lane, group)


def grad_sums(lefts, rights, layout, orders, spans, collective):
    depth, lanes = len(layout), len(orders)
    tokens, width = lefts[0].shape
    rows = width // 2**depth
    padded = -(-rows // 16) * 16
    blocks = jnp.stack(lefts).transpose(0, 2, 1).reshape(len(lefts), -1, 2, rows, tokens)
    blocks = jnp.pad(blocks, ((0, 0),) * 3 + ((0, padded - rows), (0, 0)))
    x = blocks.swapaxes(1, 2).reshape(len(lefts), 2, -1, tokens)
    y = jnp.concatenate(rights, axis=1)
    chunks = y.shape[1] // CHUNK
    groups = -(-chunks // lanes)
    bounds, passed = [], 0
    for span in spans[:-1]:
        passed += span // CHUNK
        bounds.append(passed)
    send_shapes, recv_shapes, held_shapes = [], [], []
    for _ in range(lanes):
        for step in range(depth):
            shape = (2,) * (depth - 1 - step) + (padded, CHUNK)
            send_shapes.append(pltpu.VMEM(shape, BF))
            recv_shapes.append(pltpu.VMEM((2,) + shape, BF))
            held_shapes.append(pltpu.VMEM(shape, F32))
    out = pl.pallas_call(
        partial(grad_kernel, layout, orders, tuple(bounds), chunks),
        out_shape=jax.ShapeDtypeStruct((groups * lanes, padded, CHUNK), F32),
        in_specs=[pl.BlockSpec(memory_space=pltpu.VMEM)] * 2,
        out_specs=pl.BlockSpec(memory_space=pltpu.VMEM),
        scratch_shapes=send_shapes
        + recv_shapes
        + held_shapes
        + [
            pltpu.SemaphoreType.DMA((lanes, depth)),
            pltpu.SemaphoreType.DMA((lanes, depth, 2)),
        ],
        compiler_params=pltpu.CompilerParams(
            collective_id=collective, has_side_effects=True, vmem_limit_bytes=56 * 1024 * 1024
        ),
        name="sum_gradients",
    )(x, y)
    return out[:chunks, :rows].transpose(1, 0, 2).reshape(rows, -1)


def mm(left, right):
    return jnp.dot(left, right, preferred_element_type=F32)


def mm_nt(left, right):
    return lax.dot_general(left, right, (((1,), (1,)), ((), ())), preferred_element_type=F32)


def mm_tn(left, right):
    return lax.dot_general(left, right, (((0,), (0,)), ((), ())), preferred_element_type=F32)


def norm_forward(stream, gain_row):
    inverse = lax.rsqrt(jnp.mean(stream * stream, axis=-1, keepdims=True) + EPS)
    return stream * inverse * gain_row


def norm_backward(stream, gain_row, grad_out):
    inverse = lax.rsqrt(jnp.mean(stream * stream, axis=-1, keepdims=True) + EPS)
    scaled = grad_out * gain_row
    d_input = inverse * scaled - stream * inverse**3 * jnp.mean(
        stream * scaled, axis=-1, keepdims=True
    )
    return (d_input, jnp.sum(grad_out * stream * inverse, axis=0))


def head_split(queries, keyvals):
    rows, length = queries.shape[0], keyvals.shape[0]
    query_heads = queries.reshape(rows, HK, HQ // HK, HD)
    key_heads = keyvals[:, :KW].reshape(length, HK, HD)
    value_heads = keyvals[:, KW:].reshape(length, HK, HD)
    return (query_heads, key_heads, value_heads)


def scores_of(query_heads, key_heads, first_row):
    scores = jnp.einsum(
        "rhgd,khd->hgrk", query_heads, key_heads, preferred_element_type=F32
    ) * HD ** (-0.5)
    if first_row is not None:
        rows, length = query_heads.shape[0], key_heads.shape[0]
        allowed = (first_row + jnp.arange(rows))[:, None] >= jnp.arange(length)[None, :]
        scores = jnp.where(allowed, scores, -1000000000.0)
    return scores


def attend_forward(queries, keyvals, first_row):
    query_heads, key_heads, value_heads = head_split(queries, keyvals)
    scores = scores_of(query_heads, key_heads, first_row)
    row_max = jnp.max(scores, axis=-1, keepdims=True)
    expo_terms = jnp.exp(scores - row_max)
    row_total = jnp.sum(expo_terms, axis=-1, keepdims=True)
    attn_probs = (expo_terms / row_total).astype(BF)
    mixed = jnp.einsum("hgrk,khd->rhgd", attn_probs, value_heads, preferred_element_type=F32)
    return (mixed.reshape(queries.shape[0], QW).astype(BF), row_max + jnp.log(row_total))


def attend_backward(queries, keyvals, first_row, log_total, d_mixed):
    rows, length = queries.shape[0], keyvals.shape[0]
    query_heads, key_heads, value_heads = head_split(queries, keyvals)
    attn_probs = jnp.exp(scores_of(query_heads, key_heads, first_row) - log_total)
    d_heads = d_mixed.reshape(rows, HK, HQ // HK, HD)
    d_probs = jnp.einsum("rhgd,khd->hgrk", d_heads, value_heads, preferred_element_type=F32)
    d_scores = attn_probs * (d_probs - jnp.sum(attn_probs * d_probs, axis=-1, keepdims=True))
    d_scores = d_scores.astype(BF)
    d_queries = jnp.einsum(
        "hgrk,khd->rhgd", d_scores, key_heads, preferred_element_type=F32
    ) * HD ** (-0.5)
    d_keys = jnp.einsum(
        "hgrk,rhgd->khd", d_scores, query_heads, preferred_element_type=F32
    ) * HD ** (-0.5)
    d_values = jnp.einsum(
        "hgrk,rhgd->khd", attn_probs.astype(BF), d_heads, preferred_element_type=F32
    )
    d_keyvals = jnp.concatenate(
        [d_keys.reshape(length, KW).astype(BF), d_values.reshape(length, KW).astype(BF)], axis=-1
    )
    return (d_queries.reshape(rows, QW).astype(BF), d_keyvals)


def update(weight, gradient, moment, average, rate, factor):
    clipped = gradient * factor
    moment_new = MOMENTUM * moment + (1 - MOMENTUM) * clipped
    weight_new = weight - rate * ((1 - MOMENTUM) * clipped + MOMENTUM * moment_new)
    average_new = AVERAGE * average + (1 - AVERAGE) * weight_new
    return (weight_new, moment_new, average_new)


def on_device(
    dp_axes,
    mp_axes,
    source_ids,
    target_ids,
    prefix,
    attn_in,
    attn_out,
    ff_in,
    ff_out,
    table,
    gains,
    attn_in_mom,
    attn_out_mom,
    ff_in_mom,
    ff_out_mom,
    table_mom,
    gains_mom,
    attn_in_avg,
    attn_out_avg,
    ff_in_avg,
    ff_out_avg,
    table_avg,
    gains_avg,
):
    every = dp_axes + mp_axes
    core = mp_axes[-1]
    row_axes = mp_axes[1:]
    line = mp_axes[:-1]
    gather_orders = (
        line + dp_axes + (core,),
        line + dp_axes[::-1] + (core,),
        dp_axes + line + (core,),
    )
    sum_orders = tuple(order[::-1] for order in gather_orders)
    last = (line[-1], core)
    three = (gather_orders[0], gather_orders[1], line[:-1] + dp_axes[::-1] + last)
    six_orders = three + three[:2] + (line[:-1] + dp_axes + last,)
    two_dp, two_mp, two_rows = (2,) * len(dp_axes), (2,) * len(mp_axes), (2,) * len(row_axes)

    seq_count, length = source_ids.shape
    rows = length // 2 ** len(row_axes)
    first_row = lax.axis_index(row_axes) * rows

    shards = [attn_in[0], attn_out[0], ff_in[0], ff_out[0]]
    shards += [attn_in[1], attn_out[1], attn_in[2], attn_out[2], ff_in[1], ff_out[1]]
    shards = [shard.astype(BF) for shard in shards]
    in_kernels = attn_in.shape[1] % 16 == 0
    if in_kernels:
        full = gather_all(shards, every, six_orders)
    else:
        full = [
            gather_blocks(shard, every, gather_orders[k % 3]) for k, shard in enumerate(shards)
        ]
    full = [got.reshape((-1,) + shard.shape[1:]) for got, shard in zip(full, shards)]
    a_in, a_out = (full[0], full[4], full[6]), (full[1], full[5], full[7])
    f_in, f_out = (full[2], full[8]), (full[3], full[9])
    gain_all = gather_blocks(gains.astype(BF).T, every, gather_orders[0])
    gain_all = gain_all.reshape(-1, gains.shape[0]).T.astype(F32)

    vocab_part = table.shape[0]
    offset = lax.axis_index(mp_axes) * vocab_part
    table_bf = table.astype(BF)
    decoder_ids = jnp.concatenate(
        [jnp.zeros((seq_count, 1), jnp.int32), target_ids[:, :-1]], axis=1
    )
    ids_all = gather_blocks(jnp.stack([source_ids, decoder_ids]), dp_axes, dp_axes)
    ids_all = jnp.moveaxis(ids_all, len(dp_axes), 0).reshape(2, -1)
    local_ids = ids_all - offset
    inside = (local_ids >= 0) & (local_ids < vocab_part)

    def embed(which):
        found = jnp.where(
            inside[which][:, None],
            table_bf[jnp.clip(local_ids[which], 0, vocab_part - 1)],
            jnp.zeros((), BF),
        )
        width = found.shape[-1]
        found = found.reshape(two_dp + two_mp + (rows, width))
        found = sum_blocks(found, dp_axes + mp_axes, mp_axes[::-1], BF)
        for position, axis in enumerate(dp_axes):
            bit = lax.axis_index(axis)
            received = swap(take_bit(found, 1 - bit, position), axis)
            kept = take_bit(found, bit, position)
            found = jnp.stack(
                [jnp.where(bit == 0, kept, received), jnp.where(bit == 0, received, kept)],
                axis=position,
            )
        found = found.reshape(-1, rows, width)
        return jnp.moveaxis(found, 0, 1).reshape(rows, -1).astype(F32)

    stream_e = embed(0)
    stream_d = embed(1)

    table_rows = gather_blocks(table_bf, dp_axes, dp_axes[::-1]).reshape(-1, *table.shape)
    table_rows = jnp.moveaxis(table_rows, 0, 1).reshape(vocab_part, -1)

    def spread_keys(own):
        return gather_blocks(own, row_axes, row_axes).reshape(length, -1)

    def attention_forward(stream, source, block, gain_row, start):
        normed = norm_forward(stream, gain_row).astype(BF)
        anchor = normed if source is None else source
        keyvals = spread_keys(mm(anchor, a_in[block][:, QW:]).astype(BF))
        queries = mm(normed, a_in[block][:, :QW]).astype(BF)
        mixed, log_total = attend_forward(queries, keyvals, start)
        out = stream + mm(mixed, a_out[block])
        return (out, (stream, normed, anchor, queries, keyvals, mixed, log_total))

    def ffn_forward(stream, which, gain_row):
        normed = norm_forward(stream, gain_row).astype(BF)
        both = mm(normed, f_in[which])
        hidden_act = (jax.nn.gelu(both[:, :FF], approximate=True) * both[:, FF:]).astype(BF)
        return (stream + mm(hidden_act, f_out[which]), (stream, normed, both, hidden_act))

    stream_e, enc_attn = attention_forward(stream_e, None, 0, gain_all[0], None)
    stream_d, dec_self = attention_forward(stream_d, None, 1, gain_all[3], first_row)
    stream_e, enc_ffn = ffn_forward(stream_e, 0, gain_all[1])
    encoded = norm_forward(stream_e, gain_all[2]).astype(BF)
    stream_d, dec_cross = attention_forward(stream_d, encoded, 2, gain_all[4], None)
    stream_d, dec_ffn = ffn_forward(stream_d, 1, gain_all[5])
    hidden = norm_forward(stream_d, gain_all[6]).astype(BF)

    hidden_all = gather_blocks(hidden, mp_axes, mp_axes).reshape(-1, hidden.shape[-1])
    targets = target_ids.reshape(-1)
    vocab_ids = offset + jnp.arange(vocab_part)
    hits = vocab_ids[None, :] == targets[:, None]
    logits = mm_nt(hidden_all, table_rows) * D ** (-0.5)
    own_max = jnp.max(logits, axis=-1)
    expo = jnp.exp(logits - own_max[:, None])
    stats = jnp.stack(
        [own_max, jnp.sum(expo, axis=-1), jnp.sum(jnp.where(hits, logits, 0.0), axis=-1)]
    )
    expo = expo.astype(BF)
    for axis in mp_axes[::-1]:
        other = swap(stats, axis)
        joint = jnp.maximum(stats[0], other[0])
        stats = jnp.stack(
            [
                joint,
                stats[1] * jnp.exp(stats[0] - joint) + other[1] * jnp.exp(other[0] - joint),
                stats[2] + other[2],
            ]
        )
    log_norm = stats[0] + jnp.log(stats[1])
    prefix_group = lax.dynamic_slice_in_dim(prefix, lax.axis_index(dp_axes) * seq_count, seq_count)
    scored = (jnp.arange(length)[None, :] >= prefix_group[:, None]).astype(F32).reshape(-1)
    scored_count = jnp.sum((length - prefix).astype(F32))
    scale = jnp.exp(own_max - log_norm)
    d_logits = (
        (expo.astype(F32) * scale[:, None] - hits.astype(F32)) * (scored / scored_count)[:, None]
    ).astype(BF)
    d_final = (mm(d_logits, table_rows) * D ** (-0.5)).astype(BF)
    d_final = sum_blocks(d_final.reshape(two_mp + (rows, -1)), mp_axes, mp_axes[::-1])

    head_table = (mm_tn(d_logits, hidden_all) * D ** (-0.5)).astype(BF)
    half = vocab_part // 2
    width = table.shape[1]

    def table_sum(part, order):
        stacked = jnp.stack(jnp.split(part, 2 ** len(dp_axes), axis=1))
        return sum_blocks(stacked.reshape(two_dp + part.shape[:1] + (width,)), dp_axes, order)

    grad_table = jnp.concatenate(
        [table_sum(head_table[:half], dp_axes), table_sum(head_table[half:], dp_axes[::-1])], axis=0
    )

    def ffn_backward(saved, which, gain_row, d_stream):
        stream, normed, both, hidden_act = saved
        up_part = both[:, FF:]
        activated, gelu_pull = jax.vjp(partial(jax.nn.gelu, approximate=True), both[:, :FF])
        d_branch = d_stream.astype(BF)
        d_hidden = mm_nt(d_branch, f_out[which])
        d_both = jnp.concatenate(
            [gelu_pull(d_hidden * up_part)[0].astype(BF), (d_hidden * activated).astype(BF)], axis=1
        )
        d_normed = mm_nt(d_both, f_in[which])
        d_input, grad_gain = norm_backward(stream, gain_row, d_normed)
        return (d_stream + d_input, (normed, d_both, hidden_act, d_branch), grad_gain)

    def attention_backward(saved, cross, block, gain_row, start, d_stream):
        stream, normed, anchor, queries, keyvals, mixed, log_total = saved
        d_branch = d_stream.astype(BF)
        d_mixed = mm_nt(d_branch, a_out[block]).astype(BF)
        d_queries, d_keyvals = attend_backward(queries, keyvals, start, log_total, d_mixed)
        d_keyvals = sum_blocks(
            d_keyvals.reshape(two_rows + (rows, -1)), row_axes, row_axes[::-1], BF
        )
        d_normed = mm_nt(d_queries, a_in[block][:, :QW])
        d_anchor = mm_nt(d_keyvals, a_in[block][:, QW:])
        if not cross:
            d_normed = d_normed + d_anchor
        factors = (normed, anchor, d_queries, d_keyvals, mixed, d_branch)
        d_input, grad_gain = norm_backward(stream, gain_row, d_normed)
        return (d_stream + d_input, d_anchor, factors, grad_gain)

    d_y, gain6 = norm_backward(stream_d, gain_all[6], d_final)
    d_y, ffn_factors1, gain5 = ffn_backward(dec_ffn, 1, gain_all[5], d_y)
    d_y, d_encoded, attn_factors2, gain4 = attention_backward(
        dec_cross, True, 2, gain_all[4], None, d_y
    )
    d_y, _, attn_factors1, gain3 = attention_backward(
        dec_self, False, 1, gain_all[3], first_row, d_y
    )
    d_x, gain2 = norm_backward(stream_e, gain_all[2], d_encoded)
    d_x, ffn_factors0, gain1 = ffn_backward(enc_ffn, 0, gain_all[1], d_x)
    d_x, _, attn_factors0, gain0 = attention_backward(
        enc_attn, False, 0, gain_all[0], None, d_x
    )

    def spread_rows(d_rows):
        width = table.shape[1]
        piece = jnp.moveaxis(d_rows.astype(BF).reshape(rows, -1, width), 1, 0)
        piece = piece.reshape(two_dp + (rows, width))
        for position, axis in enumerate(dp_axes):
            bit = lax.axis_index(axis)
            received = swap(take_bit(piece, 1 - bit, position), axis)
            kept = take_bit(piece, bit, position)
            piece = jnp.stack(
                [jnp.where(bit == 0, kept, received), jnp.where(bit == 0, received, kept)],
                axis=position,
            )
        piece = piece.reshape((-1, rows, width))
        everyone = gather_blocks(piece, mp_axes, mp_axes)
        everyone = everyone.reshape((2 ** len(mp_axes), -1, rows, width))
        return jnp.moveaxis(everyone, 0, 1).reshape(-1, width)

    def look_back(which, d_rows):
        segment_ids = jnp.where(inside[which], local_ids[which], vocab_part)
        return jax.ops.segment_sum(
            spread_rows(d_rows).astype(F32), segment_ids, num_segments=vocab_part + 1
        )[:vocab_part]

    grad_table = grad_table + look_back(1, d_y) + look_back(0, d_x)

    gain_grads = jnp.stack([gain0, gain1, gain2, gain3, gain4, gain5, gain6])
    gain_blocks = jnp.moveaxis(gain_grads.reshape(gains.shape[0], -1, gains.shape[1]), 1, 0)
    grad_gains = sum_blocks(
        gain_blocks.reshape((2,) * len(every) + gains.shape), every, sum_orders[0]
    )

    lefts, rights = [], []
    for normed, anchor, d_queries, d_keyvals, mixed, d_branch in (
        attn_factors0,
        attn_factors1,
        attn_factors2,
    ):
        if anchor is normed:
            lefts += [normed, mixed]
            rights += [jnp.concatenate([d_queries, d_keyvals], axis=1), d_branch]
        else:
            lefts += [normed, anchor, mixed]
            rights += [d_queries, d_keyvals, d_branch]
    wide_lefts, wide_rights = [], []
    for normed, d_both, hidden_act, d_branch in (ffn_factors0, ffn_factors1):
        lefts.append(normed)
        rights.append(d_both)
        wide_lefts.append(hidden_act)
        wide_rights.append(d_branch)
    spans = [right.shape[1] for right in rights]
    wide_spans = [right.shape[1] for right in wide_rights]
    if in_kernels:
        back_orders = tuple(order[::-1] for order in three)
        own = grad_sums(lefts, rights, every, back_orders, spans, 1)
        wide = grad_sums(wide_lefts, wide_rights, every, back_orders, wide_spans, 2)
    else:

        def own_sum(left, right, kind):
            product = mm_tn(left, right).astype(BF)
            blocks = product.reshape((2,) * len(every) + (-1,) + product.shape[1:])
            return sum_blocks(blocks, every, sum_orders[kind % 3])

        pairs = list(enumerate(zip(lefts, rights)))
        own = jnp.concatenate([own_sum(*pair, k) for k, pair in pairs], axis=1)
        pairs = list(enumerate(zip(wide_lefts, wide_rights)))
        wide = jnp.concatenate([own_sum(*pair, k) for k, pair in pairs], axis=1)
    ends = (attn_in.shape[2], attn_in.shape[2] + attn_out.shape[2])
    ffn_from = 3 * ends[1]
    gradients = (
        jnp.stack([own[:, ends[1] * k : ends[1] * k + ends[0]] for k in range(3)]),
        jnp.stack([own[:, ends[1] * k + ends[0] : ends[1] * (k + 1)] for k in range(3)]),
        jnp.stack([own[:, ffn_from + 2 * FF * k : ffn_from + 2 * FF * (k + 1)] for k in range(2)]),
        jnp.stack(jnp.split(wide, 2, axis=1)),
        grad_table,
        grad_gains,
    )

    own_losses = ((log_norm - stats[2]) * scored).reshape(2 ** len(mp_axes), rows)
    loss_part = jnp.sum(take_bit(own_losses, lax.axis_index(mp_axes), 0))
    squares = sum((jnp.sum(gradient * gradient) for gradient in gradients))
    totals = jnp.stack([loss_part, squares])
    for axis in every[::-1]:
        totals = totals + swap(totals, axis)
    loss_sum = totals[0]
    grad_norm = jnp.sqrt(totals[1])
    factor = jnp.minimum(1.0, CLIP / grad_norm)
    weights = (attn_in, attn_out, ff_in, ff_out, table, gains)
    moments = (attn_in_mom, attn_out_mom, ff_in_mom, ff_out_mom, table_mom, gains_mom)
    averages = (attn_in_avg, attn_out_avg, ff_in_avg, ff_out_avg, table_avg, gains_avg)
    results = [
        update(weight, gradient, moment, average, rate, factor)
        for weight, gradient, moment, average, rate in zip(
            weights, gradients, moments, averages, step_rates()
        )
    ]
    return (loss_sum, scored_count, grad_norm) + tuple(
        results[array][kind] for kind in range(3) for array in range(6)
    )


def solution(mesh):
    dp_count, mp_count = mesh.shape["dp"], mesh.shape["mp"]
    dp_axes = tuple(f"d{k}" for k in range(dp_count.bit_length() - 1))
    mp_axes = tuple(f"m{k}" for k in range(mp_count.bit_length() - 1))
    every = dp_axes + mp_axes
    fine = Mesh(mesh.devices.reshape((2,) * len(every)), every)
    rows_split = P(None, every, None)
    params = (rows_split,) * 4 + (P(mp_axes, dp_axes), P(None, every))
    in_specs = (P(dp_axes, None), P(dp_axes, None), P()) + params * 3
    out_specs = (P(), P(), P()) + params * 3
    return jax.shard_map(
        partial(on_device, dp_axes, mp_axes),
        mesh=fine,
        in_specs=in_specs,
        out_specs=out_specs,
        check_vma=False,
    )
```

```python
from functools import partial

import jax
import jax.numpy as jnp
from jax import lax
from jax.experimental import pallas as pl
from jax.experimental.pallas import tpu as pltpu
from jax.sharding import Mesh
from jax.sharding import PartitionSpec as P

D = 1024
HQ = 16
HK = 8
HD = 64
FF = 2816
LEN = 1024
QW = 1024
KW = 512
PARAMS = 59644928

MOMENTUM = 0.9
AVERAGE = 0.9
CLIP = 0.0002
EPS = 1e-06

BF = jnp.bfloat16
F32 = jnp.float32
MESH = pl.DeviceIdType.MESH
CHUNK = 256
LANES = 3


def step_rates():
    base_rate = 3.5 * PARAMS**0.5 / CLIP
    return (
        base_rate * D ** (-0.5),
        base_rate * max(QW // LEN, 1) ** (-0.5),
        base_rate * D ** (-0.5),
        base_rate * FF ** (-0.5),
        base_rate * 2.0,
        base_rate * 0.3,
    )


def swap(value, axis):
    return lax.ppermute(value, axis, [(0, 1), (1, 0)])


def take_bit(value, bit, position):
    return lax.dynamic_index_in_dim(value, bit, position, keepdims=False)


def gather_blocks(block, layout, order):
    have = []
    held = block
    for axis in order:
        received = swap(held, axis)
        position = sum(layout.index(other) < layout.index(axis) for other in have)
        bit = lax.axis_index(axis)
        shape = held.shape
        joined = jnp.zeros(shape[:position] + (2,) + shape[position:], held.dtype)
        joined = lax.dynamic_update_index_in_dim(joined, held, bit, position)
        held = lax.dynamic_update_index_in_dim(joined, received, 1 - bit, position)
        have.append(axis)
    return held


def sum_blocks(terms, layout, order, last=F32):
    left = list(layout)
    held = terms
    for axis in order:
        position = left.index(axis)
        bit = lax.axis_index(axis)
        received = swap(take_bit(held, 1 - bit, position), axis)
        held = take_bit(held, bit, position).astype(F32) + received.astype(F32)
        left.remove(axis)
        if left:
            held = held.astype(terms.dtype)
    return held.astype(last)


def greet(axes):
    barrier = pltpu.get_barrier_semaphore()
    for axis in axes:
        pl.semaphore_signal(
            barrier, inc=1, device_id={axis: 1 - lax.axis_index(axis)}, device_id_type=MESH
        )
    pl.semaphore_wait(barrier, len(axes))


def gather_kernel(layout, units, lanes, count, *refs):
    ins, outs = refs[:count], refs[count : 2 * count]
    own_sem, send_sem, recv_sem = refs[2 * count :]
    bits = {axis: lax.axis_index(axis) for axis in layout}
    depth = len(layout)

    def region(unit, have):
        tensor, start, size, _ = units[unit]
        blocks = tuple(pl.ds(0, 2) if axis in have else bits[axis] for axis in layout)
        return outs[tensor].at[blocks + (slice(None), pl.ds(start, size))]

    own = [
        pltpu.make_async_copy(
            ins[k], outs[k].at[tuple(bits[axis] for axis in layout)], own_sem.at[k]
        )
        for k in range(count)
    ]
    for copy in own:
        copy.start()
    greet(layout)
    for copy in own:
        copy.wait()
    copies = {}
    groups = -(-len(units) // lanes)
    for turn in range(groups + depth - 1):
        for step in reversed(range(depth)):
            first = (turn - step) * lanes
            for unit in range(max(first, 0), min(first + lanes, len(units))):
                order = units[unit][3]
                if step:
                    copies[unit, step - 1].wait_recv()
                source = region(unit, order[:step])
                copy = pltpu.make_async_remote_copy(
                    src_ref=source,
                    dst_ref=source,
                    send_sem=send_sem.at[unit, step],
                    recv_sem=recv_sem.at[unit, step],
                    device_id={order[step]: 1 - bits[order[step]]},
                    device_id_type=MESH,
                )
                copy.start()
                copies[unit, step] = copy
    for unit in range(len(units)):
        copies[unit, depth - 1].wait_recv()
    for copy in copies.values():
        copy.wait_send()


def gather_all(shards, layout, orders):
    units = []
    for tensor, shard in enumerate(shards):
        columns = shard.shape[1]
        step = -(-512 * 32 // shard.shape[0] // 128) * 128
        pieces = -(-columns // step)
        starts = [step * piece for piece in range(pieces)] + [columns]
        for piece in range(pieces):
            order = orders[len(units) % len(orders)]
            units.append((tensor, starts[piece], starts[piece + 1] - starts[piece], order))
    count = len(shards)
    semaphores = pltpu.SemaphoreType.DMA((len(units), len(layout)))
    return pl.pallas_call(
        partial(gather_kernel, layout, tuple(units), LANES, count),
        out_shape=[
            jax.ShapeDtypeStruct((2,) * len(layout) + shard.shape, shard.dtype) for shard in shards
        ],
        in_specs=[pl.BlockSpec(memory_space=pl.ANY)] * count,
        out_specs=[pl.BlockSpec(memory_space=pl.ANY)] * count,
        scratch_shapes=[pltpu.SemaphoreType.DMA((count,)), semaphores, semaphores],
        compiler_params=pltpu.CompilerParams(collective_id=0, has_side_effects=True),
        name="gather_weights",
    )(*shards)


def grad_kernel(layout, orders, bounds, chunks, *refs):
    x_ref, y_ref, out_ref = refs[:3]
    depth = len(layout)
    lanes = len(orders)
    scratch = refs[3:]
    sends, recvs, helds = (
        [scratch[kind * lanes * depth + lane * depth :][:depth] for lane in range(lanes)]
        for kind in range(3)
    )
    send_sem, recv_sem = scratch[3 * lanes * depth :]
    bits = {axis: lax.axis_index(axis) for axis in layout}
    groups = out_ref.shape[0] // lanes
    greet(layout)

    def exchange(lane, step, group):
        axis = orders[lane][step]
        slot = lax.rem(group, 2)
        return pltpu.make_async_remote_copy(
            src_ref=sends[lane][step],
            dst_ref=recvs[lane][step].at[slot],
            send_sem=send_sem.at[lane, step],
            recv_sem=recv_sem.at[lane, step, slot],
            device_id={axis: 1 - bits[axis]},
            device_id_type=MESH,
        )

    def first(lane, group):
        chunk = jnp.minimum(group * lanes + lane, chunks - 1)
        which = sum((chunk >= bound).astype(jnp.int32) for bound in bounds) if bounds else 0
        columns = y_ref[:, pl.ds(pl.multiple_of(chunk * CHUNK, CHUNK), CHUNK)]
        bit = bits[orders[lane][0]]
        given = jnp.dot(x_ref[which, 1 - bit], columns, preferred_element_type=F32)
        sends[lane][0][...] = given.astype(BF).reshape(sends[lane][0].shape)
        exchange(lane, 0, group).start()
        kept = jnp.dot(x_ref[which, bit], columns, preferred_element_type=F32)
        helds[lane][0][...] = kept.reshape(helds[lane][0].shape)

    def later(lane, step, group):
        order = orders[lane]
        slot = lax.rem(group, 2)
        exchange(lane, step - 1, group).wait()
        held, received = helds[lane][step - 1], recvs[lane][step - 1]
        if step == depth:
            out_ref[group * lanes + lane] = held[...] + received[slot].astype(F32)
            return
        position = [axis for axis in layout if axis not in order[:step]].index(order[step])
        bit = bits[order[step]]

        def total(choice):
            index = (slice(None),) * position + (choice,)
            return held[index] + received[(slot,) + index].astype(F32)

        sends[lane][step][...] = total(1 - bit).astype(BF)
        exchange(lane, step, group).start()
        helds[lane][step][...] = total(bit)

    @pl.loop(0, groups + depth)
    def _(turn):
        for step in reversed(range(depth + 1)):
            group = turn - step

            @pl.when((group >= 0) & (group < groups))
            def _():
                for lane in range(lanes):
                    if step:
                        later(lane, step, group)
                    else:
                        first(lane, group)


def grad_sums(lefts, rights, layout, orders, spans, collective):
    depth, lanes = len(layout), len(orders)
    tokens, width = lefts[0].shape
    rows = width // 2**depth
    padded = -(-rows // 16) * 16
    blocks = jnp.stack(lefts).transpose(0, 2, 1).reshape(len(lefts), -1, 2, rows, tokens)
    blocks = jnp.pad(blocks, ((0, 0),) * 3 + ((0, padded - rows), (0, 0)))
    x = blocks.swapaxes(1, 2).reshape(len(lefts), 2, -1, tokens)
    y = jnp.concatenate(rights, axis=1)
    chunks = y.shape[1] // CHUNK
    groups = -(-chunks // lanes)
    bounds, passed = [], 0
    for span in spans[:-1]:
        passed += span // CHUNK
        bounds.append(passed)
    send_shapes, recv_shapes, held_shapes = [], [], []
    for _ in range(lanes):
        for step in range(depth):
            shape = (2,) * (depth - 1 - step) + (padded, CHUNK)
            send_shapes.append(pltpu.VMEM(shape, BF))
            recv_shapes.append(pltpu.VMEM((2,) + shape, BF))
            held_shapes.append(pltpu.VMEM(shape, F32))
    out = pl.pallas_call(
        partial(grad_kernel, layout, orders, tuple(bounds), chunks),
        out_shape=jax.ShapeDtypeStruct((groups * lanes, padded, CHUNK), F32),
        in_specs=[pl.BlockSpec(memory_space=pltpu.VMEM)] * 2,
        out_specs=pl.BlockSpec(memory_space=pltpu.VMEM),
        scratch_shapes=send_shapes
        + recv_shapes
        + held_shapes
        + [
            pltpu.SemaphoreType.DMA((lanes, depth)),
            pltpu.SemaphoreType.DMA((lanes, depth, 2)),
        ],
        compiler_params=pltpu.CompilerParams(
            collective_id=collective, has_side_effects=True, vmem_limit_bytes=56 * 1024 * 1024
        ),
        name="sum_gradients",
    )(x, y)
    return out[:chunks, :rows].transpose(1, 0, 2).reshape(rows, -1)


def mm(left, right):
    return jnp.dot(left, right, preferred_element_type=F32)


def mm_nt(left, right):
    return lax.dot_general(left, right, (((1,), (1,)), ((), ())), preferred_element_type=F32)


def mm_tn(left, right):
    return lax.dot_general(left, right, (((0,), (0,)), ((), ())), preferred_element_type=F32)


def norm_forward(stream, gain_row):
    inverse = lax.rsqrt(jnp.mean(stream * stream, axis=-1, keepdims=True) + EPS)
    return stream * inverse * gain_row


def norm_backward(stream, gain_row, grad_out):
    inverse = lax.rsqrt(jnp.mean(stream * stream, axis=-1, keepdims=True) + EPS)
    scaled = grad_out * gain_row
    d_input = inverse * scaled - stream * inverse**3 * jnp.mean(
        stream * scaled, axis=-1, keepdims=True
    )
    return (d_input, jnp.sum(grad_out * stream * inverse, axis=0))


def nt(left, right):
    return lax.dot_general(left, right, (((1,), (1,)), ((), ())), preferred_element_type=F32)


def attend_kernel(causal, row_ref, q_ref, k_ref, v_ref, o_ref):
    rows, length = q_ref.shape[0], k_ref.shape[0]
    shape = (rows, length)
    if causal:
        allowed = row_ref[0] + lax.broadcasted_iota(
            jnp.int32, shape, 0
        ) >= lax.broadcasted_iota(jnp.int32, shape, 1)
    for head in range(q_ref.shape[1] // HD):
        own = pl.ds(head * HD, HD)
        shared = pl.ds(head // (HQ // HK) * HD, HD)
        scores = nt(q_ref[:, own], k_ref[:, shared]) * HD ** (-0.5)
        if causal:
            scores = jnp.where(allowed, scores, -1000000000.0)
        expo = jnp.exp(scores - jnp.max(scores, axis=-1, keepdims=True))
        probs = expo * (1.0 / jnp.sum(expo, axis=-1, keepdims=True))
        mixed = jnp.dot(probs.astype(BF), v_ref[:, shared], preferred_element_type=F32)
        o_ref[:, own] = mixed.astype(BF)


def attend_back_kernel(causal, row_ref, q_ref, k_ref, v_ref, d_ref, dq_ref, dk_ref, dv_ref):
    rows, length = q_ref.shape[0], k_ref.shape[0]
    shape = (length, rows)
    share = HQ // HK
    if causal:
        allowed = row_ref[0] + lax.broadcasted_iota(
            jnp.int32, shape, 1
        ) >= lax.broadcasted_iota(jnp.int32, shape, 0)
    for pair in range(k_ref.shape[1] // HD):
        shared = pl.ds(pair * HD, HD)
        keys, values = k_ref[:, shared], v_ref[:, shared]
        d_keys = d_values = None
        for head in range(pair * share, (pair + 1) * share):
            own = pl.ds(head * HD, HD)
            queries, d_mixed = q_ref[:, own], d_ref[:, own]
            scores = nt(keys, queries) * HD ** (-0.5)
            if causal:
                scores = jnp.where(allowed, scores, -1000000000.0)
            expo = jnp.exp(scores - jnp.max(scores, axis=0, keepdims=True))
            probs = expo * (1.0 / jnp.sum(expo, axis=0, keepdims=True))
            d_probs = nt(values, d_mixed)
            mean = jnp.sum(probs * d_probs, axis=0, keepdims=True)
            d_scores = (probs * (d_probs - mean)).astype(BF)
            key_term = jnp.dot(d_scores, queries, preferred_element_type=F32)
            value_term = jnp.dot(probs.astype(BF), d_mixed, preferred_element_type=F32)
            d_keys = key_term if d_keys is None else d_keys + key_term
            d_values = value_term if d_values is None else d_values + value_term
            d_queries = lax.dot_general(
                keys, d_scores, (((0,), (0,)), ((), ())), preferred_element_type=F32
            )
            dq_ref[:, own] = (d_queries.T * HD ** (-0.5)).astype(BF)
        dk_ref[:, shared] = (d_keys * HD ** (-0.5)).astype(BF)
        dv_ref[:, shared] = d_values.astype(BF)


def attend_specs(rows, length):
    wide = 128 * (HQ // HK)
    queries = pl.BlockSpec((rows, wide), lambda i: (0, i))
    keys = pl.BlockSpec((length, 128), lambda i: (0, i))
    values = pl.BlockSpec((length, 128), lambda i: (0, i + KW // 128))
    return queries, keys, values


def attend_forward(queries, keyvals, first_row):
    rows, length = queries.shape[0], keyvals.shape[0]
    by_query, by_key, by_value = attend_specs(rows, length)
    return pl.pallas_call(
        partial(attend_kernel, first_row is not None),
        grid=(KW // 128,),
        out_shape=jax.ShapeDtypeStruct(queries.shape, BF),
        in_specs=[pl.BlockSpec(memory_space=pltpu.SMEM), by_query, by_key, by_value],
        out_specs=by_query,
        compiler_params=pltpu.CompilerParams(vmem_limit_bytes=56 * 1024 * 1024),
        cost_estimate=pl.CostEstimate(
            flops=4 * rows * length * QW,
            bytes_accessed=4 * rows * QW + 4 * length * KW,
            transcendentals=HQ * rows * length,
        ),
        name="attend",
    )(jnp.reshape(0 if first_row is None else first_row, (1,)), queries, keyvals, keyvals)


def attend_backward(queries, keyvals, first_row, d_mixed):
    rows, length = queries.shape[0], keyvals.shape[0]
    by_query, by_key, by_value = attend_specs(rows, length)
    d_queries, d_keys, d_values = pl.pallas_call(
        partial(attend_back_kernel, first_row is not None),
        grid=(KW // 128,),
        out_shape=[
            jax.ShapeDtypeStruct(queries.shape, BF),
            jax.ShapeDtypeStruct((length, KW), BF),
            jax.ShapeDtypeStruct((length, KW), BF),
        ],
        in_specs=[pl.BlockSpec(memory_space=pltpu.SMEM), by_query, by_key, by_value, by_query],
        out_specs=[by_query, by_key, by_key],
        compiler_params=pltpu.CompilerParams(vmem_limit_bytes=56 * 1024 * 1024),
        cost_estimate=pl.CostEstimate(
            flops=10 * rows * length * QW,
            bytes_accessed=6 * rows * QW + 8 * length * KW,
            transcendentals=HQ * rows * length,
        ),
        name="attend_back",
    )(jnp.reshape(0 if first_row is None else first_row, (1,)), queries, keyvals, keyvals, d_mixed)
    return (d_queries, jnp.concatenate([d_keys, d_values], axis=1))


def update(weight, gradient, moment, average, rate, factor):
    clipped = gradient * factor
    moment_new = MOMENTUM * moment + (1 - MOMENTUM) * clipped
    weight_new = weight - rate * ((1 - MOMENTUM) * clipped + MOMENTUM * moment_new)
    average_new = AVERAGE * average + (1 - AVERAGE) * weight_new
    return (weight_new, moment_new, average_new)


def on_device(
    dp_axes,
    mp_axes,
    source_ids,
    target_ids,
    prefix,
    attn_in,
    attn_out,
    ff_in,
    ff_out,
    table,
    gains,
    attn_in_mom,
    attn_out_mom,
    ff_in_mom,
    ff_out_mom,
    table_mom,
    gains_mom,
    attn_in_avg,
    attn_out_avg,
    ff_in_avg,
    ff_out_avg,
    table_avg,
    gains_avg,
):
    every = dp_axes + mp_axes
    core = mp_axes[-1]
    row_axes = mp_axes[1:]
    line = mp_axes[:-1]
    gather_orders = (
        line + dp_axes + (core,),
        line + dp_axes[::-1] + (core,),
        dp_axes + line + (core,),
    )
    sum_orders = tuple(order[::-1] for order in gather_orders)
    last = (line[-1], core)
    three = (gather_orders[0], gather_orders[1], line[:-1] + dp_axes[::-1] + last)
    six_orders = three + three[:2] + (line[:-1] + dp_axes + last,)
    two_dp, two_mp, two_rows = (2,) * len(dp_axes), (2,) * len(mp_axes), (2,) * len(row_axes)

    seq_count, length = source_ids.shape
    rows = length // 2 ** len(row_axes)
    first_row = lax.axis_index(row_axes) * rows

    vocab_part = table.shape[0]
    offset = lax.axis_index(mp_axes) * vocab_part
    table_bf = table.astype(BF)
    decoder_ids = jnp.concatenate(
        [jnp.zeros((seq_count, 1), jnp.int32), target_ids[:, :-1]], axis=1
    )
    ids_all = gather_blocks(jnp.stack([source_ids, decoder_ids]), dp_axes, dp_axes)
    ids_all = jnp.moveaxis(ids_all, len(dp_axes), 0).reshape(2, -1)
    local_ids = ids_all - offset
    inside = (local_ids >= 0) & (local_ids < vocab_part)

    def embed(which):
        found = jnp.where(
            inside[which][:, None],
            table_bf[jnp.clip(local_ids[which], 0, vocab_part - 1)],
            jnp.zeros((), BF),
        )
        width = found.shape[-1]
        found = found.reshape(two_dp + two_mp + (rows, width))
        found = sum_blocks(found, dp_axes + mp_axes, mp_axes[::-1], BF)
        for position, axis in enumerate(dp_axes):
            bit = lax.axis_index(axis)
            received = swap(take_bit(found, 1 - bit, position), axis)
            kept = take_bit(found, bit, position)
            found = jnp.stack(
                [jnp.where(bit == 0, kept, received), jnp.where(bit == 0, received, kept)],
                axis=position,
            )
        found = found.reshape(-1, rows, width)
        return jnp.moveaxis(found, 0, 1).reshape(rows, -1).astype(F32)

    stream_e = embed(0)
    stream_d = embed(1)

    shards = [attn_in[0], attn_out[0], ff_in[0], ff_out[0]]
    shards += [attn_in[1], attn_out[1], attn_in[2], attn_out[2], ff_in[1], ff_out[1]]
    shards = [shard.astype(BF) for shard in shards]
    in_kernels = attn_in.shape[1] % 16 == 0
    if in_kernels:
        early = (0, 1)
        full = [None] * len(shards)
        for k in early:
            full[k] = lax.all_gather(shards[k], every, axis=0, tiled=True)
        late = [k for k in range(len(shards)) if k not in early]
        held = lax.optimization_barrier([shards[k] for k in late] + [stream_e, stream_d])
        stream_e, stream_d = held[-2:]
        for k, got in zip(late, gather_all(held[:-2], every, six_orders)):
            full[k] = got
        full[4], table_bf = lax.optimization_barrier((full[4], table_bf))
    else:
        full = [
            gather_blocks(shard, every, gather_orders[k % 3]) for k, shard in enumerate(shards)
        ]
    full = [got.reshape((-1,) + shard.shape[1:]) for got, shard in zip(full, shards)]
    a_in, a_out = (full[0], full[4], full[6]), (full[1], full[5], full[7])
    f_in, f_out = (full[2], full[8]), (full[3], full[9])
    gain_all = gather_blocks(gains.astype(BF).T, every, gather_orders[0])
    gain_all = gain_all.reshape(-1, gains.shape[0]).T.astype(F32)

    table_rows = gather_blocks(table_bf, dp_axes, dp_axes[::-1]).reshape(-1, *table.shape)
    table_rows = jnp.moveaxis(table_rows, 0, 1).reshape(vocab_part, -1)

    def spread_keys(own):
        return gather_blocks(own, row_axes, row_axes).reshape(length, -1)

    def attention_forward(stream, source, block, gain_row, start):
        normed = norm_forward(stream, gain_row).astype(BF)
        anchor = normed if source is None else source
        keyvals = spread_keys(mm(anchor, a_in[block][:, QW:]).astype(BF))
        queries = mm(normed, a_in[block][:, :QW]).astype(BF)
        mixed = attend_forward(queries, keyvals, start)
        out = stream + mm(mixed, a_out[block])
        return (out, (stream, normed, anchor, queries, keyvals, mixed))

    def ffn_forward(stream, which, gain_row):
        normed = norm_forward(stream, gain_row).astype(BF)
        both = mm(normed, f_in[which])
        hidden_act = (jax.nn.gelu(both[:, :FF], approximate=True) * both[:, FF:]).astype(BF)
        return (stream + mm(hidden_act, f_out[which]), (stream, normed, both, hidden_act))

    stream_e, enc_attn = attention_forward(stream_e, None, 0, gain_all[0], None)
    stream_d, dec_self = attention_forward(stream_d, None, 1, gain_all[3], first_row)
    stream_e, enc_ffn = ffn_forward(stream_e, 0, gain_all[1])
    encoded = norm_forward(stream_e, gain_all[2]).astype(BF)
    stream_d, dec_cross = attention_forward(stream_d, encoded, 2, gain_all[4], None)
    stream_d, dec_ffn = ffn_forward(stream_d, 1, gain_all[5])
    hidden = norm_forward(stream_d, gain_all[6]).astype(BF)

    hidden_all = gather_blocks(hidden, mp_axes, mp_axes).reshape(-1, hidden.shape[-1])
    targets = target_ids.reshape(-1)
    vocab_ids = offset + jnp.arange(vocab_part)
    hits = vocab_ids[None, :] == targets[:, None]
    logits = mm_nt(hidden_all, table_rows) * D ** (-0.5)
    own_max = jnp.max(logits, axis=-1)
    expo = jnp.exp(logits - own_max[:, None])
    stats = jnp.stack(
        [own_max, jnp.sum(expo, axis=-1), jnp.sum(jnp.where(hits, logits, 0.0), axis=-1)]
    )
    expo = expo.astype(BF)
    for axis in mp_axes[::-1]:
        other = swap(stats, axis)
        joint = jnp.maximum(stats[0], other[0])
        stats = jnp.stack(
            [
                joint,
                stats[1] * jnp.exp(stats[0] - joint) + other[1] * jnp.exp(other[0] - joint),
                stats[2] + other[2],
            ]
        )
    log_norm = stats[0] + jnp.log(stats[1])
    prefix_group = lax.dynamic_slice_in_dim(prefix, lax.axis_index(dp_axes) * seq_count, seq_count)
    scored = (jnp.arange(length)[None, :] >= prefix_group[:, None]).astype(F32).reshape(-1)
    scored_count = jnp.sum((length - prefix).astype(F32))
    scale = jnp.exp(own_max - log_norm)
    d_logits = (
        (expo.astype(F32) * scale[:, None] - hits.astype(F32)) * (scored / scored_count)[:, None]
    ).astype(BF)
    d_final = (mm(d_logits, table_rows) * D ** (-0.5)).astype(BF)
    d_final = sum_blocks(d_final.reshape(two_mp + (rows, -1)), mp_axes, mp_axes[::-1])

    head_table = (mm_tn(d_logits, hidden_all) * D ** (-0.5)).astype(BF)
    half = vocab_part // 2
    width = table.shape[1]

    def table_sum(part, order):
        stacked = jnp.stack(jnp.split(part, 2 ** len(dp_axes), axis=1))
        return sum_blocks(stacked.reshape(two_dp + part.shape[:1] + (width,)), dp_axes, order)

    grad_table = jnp.concatenate(
        [table_sum(head_table[:half], dp_axes), table_sum(head_table[half:], dp_axes[::-1])], axis=0
    )

    def ffn_backward(saved, which, gain_row, d_stream):
        stream, normed, both, hidden_act = saved
        up_part = both[:, FF:]
        activated, gelu_pull = jax.vjp(partial(jax.nn.gelu, approximate=True), both[:, :FF])
        d_branch = d_stream.astype(BF)
        d_hidden = mm_nt(d_branch, f_out[which])
        d_both = jnp.concatenate(
            [gelu_pull(d_hidden * up_part)[0].astype(BF), (d_hidden * activated).astype(BF)], axis=1
        )
        d_normed = mm_nt(d_both, f_in[which])
        d_input, grad_gain = norm_backward(stream, gain_row, d_normed)
        return (d_stream + d_input, (normed, d_both, hidden_act, d_branch), grad_gain)

    def attention_backward(saved, cross, block, gain_row, start, d_stream):
        stream, normed, anchor, queries, keyvals, mixed = saved
        d_branch = d_stream.astype(BF)
        d_mixed = mm_nt(d_branch, a_out[block]).astype(BF)
        d_queries, d_keyvals = attend_backward(queries, keyvals, start, d_mixed)
        d_keyvals = sum_blocks(
            d_keyvals.reshape(two_rows + (rows, -1)), row_axes, row_axes[::-1], BF
        )
        d_normed = mm_nt(d_queries, a_in[block][:, :QW])
        d_anchor = mm_nt(d_keyvals, a_in[block][:, QW:])
        if not cross:
            d_normed = d_normed + d_anchor
        factors = (normed, anchor, d_queries, d_keyvals, mixed, d_branch)
        d_input, grad_gain = norm_backward(stream, gain_row, d_normed)
        return (d_stream + d_input, d_anchor, factors, grad_gain)

    d_y, gain6 = norm_backward(stream_d, gain_all[6], d_final)
    d_y, ffn_factors1, gain5 = ffn_backward(dec_ffn, 1, gain_all[5], d_y)
    if in_kernels:
        first_sum = lax.psum_scatter(
            mm_tn(ffn_factors1[0], ffn_factors1[1]).astype(BF), every, scatter_dimension=0, tiled=True
        ).astype(F32)
    d_y, d_encoded, attn_factors2, gain4 = attention_backward(
        dec_cross, True, 2, gain_all[4], None, d_y
    )
    d_y, _, attn_factors1, gain3 = attention_backward(
        dec_self, False, 1, gain_all[3], first_row, d_y
    )
    d_x, gain2 = norm_backward(stream_e, gain_all[2], d_encoded)
    d_x, ffn_factors0, gain1 = ffn_backward(enc_ffn, 0, gain_all[1], d_x)
    d_x, _, attn_factors0, gain0 = attention_backward(
        enc_attn, False, 0, gain_all[0], None, d_x
    )

    def spread_rows(d_rows):
        width = table.shape[1]
        piece = jnp.moveaxis(d_rows.astype(BF).reshape(rows, -1, width), 1, 0)
        piece = piece.reshape(two_dp + (rows, width))
        for position, axis in enumerate(dp_axes):
            bit = lax.axis_index(axis)
            received = swap(take_bit(piece, 1 - bit, position), axis)
            kept = take_bit(piece, bit, position)
            piece = jnp.stack(
                [jnp.where(bit == 0, kept, received), jnp.where(bit == 0, received, kept)],
                axis=position,
            )
        piece = piece.reshape((-1, rows, width))
        everyone = gather_blocks(piece, mp_axes, mp_axes)
        everyone = everyone.reshape((2 ** len(mp_axes), -1, rows, width))
        return jnp.moveaxis(everyone, 0, 1).reshape(-1, width)

    def look_back(which, d_rows):
        places = (local_ids[which][None, :] == jnp.arange(vocab_part)[:, None]).astype(BF)
        return mm(places, spread_rows(d_rows))

    grad_table = grad_table + look_back(1, d_y) + look_back(0, d_x)

    gain_grads = jnp.stack([gain0, gain1, gain2, gain3, gain4, gain5, gain6])
    gain_blocks = jnp.moveaxis(gain_grads.reshape(gains.shape[0], -1, gains.shape[1]), 1, 0)
    grad_gains = sum_blocks(
        gain_blocks.reshape((2,) * len(every) + gains.shape), every, sum_orders[0]
    )

    lefts, rights = [], []
    for normed, anchor, d_queries, d_keyvals, mixed, d_branch in (
        attn_factors0,
        attn_factors1,
        attn_factors2,
    ):
        if anchor is normed:
            lefts += [normed, mixed]
            rights += [jnp.concatenate([d_queries, d_keyvals], axis=1), d_branch]
        else:
            lefts += [normed, anchor, mixed]
            rights += [d_queries, d_keyvals, d_branch]
    wide_lefts, wide_rights = [], []
    for normed, d_both, hidden_act, d_branch in (ffn_factors0, ffn_factors1):
        if hidden_act is ffn_factors0[2] or not in_kernels:
            lefts.append(normed)
            rights.append(d_both)
        wide_lefts.append(hidden_act)
        wide_rights.append(d_branch)
    spans = [right.shape[1] for right in rights]
    wide_spans = [right.shape[1] for right in wide_rights]
    if in_kernels:
        back_orders = tuple(order[::-1] for order in three)
        own = grad_sums(lefts, rights, every, back_orders, spans, 1)
        own = jnp.concatenate([own, first_sum], axis=1)
        wide = grad_sums(wide_lefts, wide_rights, every, back_orders, wide_spans, 2)
    else:

        def own_sum(left, right, kind):
            product = mm_tn(left, right).astype(BF)
            blocks = product.reshape((2,) * len(every) + (-1,) + product.shape[1:])
            return sum_blocks(blocks, every, sum_orders[kind % 3])

        pairs = list(enumerate(zip(lefts, rights)))
        own = jnp.concatenate([own_sum(*pair, k) for k, pair in pairs], axis=1)
        pairs = list(enumerate(zip(wide_lefts, wide_rights)))
        wide = jnp.concatenate([own_sum(*pair, k) for k, pair in pairs], axis=1)
    ends = (attn_in.shape[2], attn_in.shape[2] + attn_out.shape[2])
    ffn_from = 3 * ends[1]
    gradients = (
        jnp.stack([own[:, ends[1] * k : ends[1] * k + ends[0]] for k in range(3)]),
        jnp.stack([own[:, ends[1] * k + ends[0] : ends[1] * (k + 1)] for k in range(3)]),
        jnp.stack([own[:, ffn_from + 2 * FF * k : ffn_from + 2 * FF * (k + 1)] for k in range(2)]),
        jnp.stack(jnp.split(wide, 2, axis=1)),
        grad_table,
        grad_gains,
    )

    own_losses = ((log_norm - stats[2]) * scored).reshape(2 ** len(mp_axes), rows)
    loss_part = jnp.sum(take_bit(own_losses, lax.axis_index(mp_axes), 0))
    squares = sum((jnp.sum(gradient * gradient) for gradient in gradients))
    totals = jnp.stack([loss_part, squares])
    for axis in every[::-1]:
        totals = totals + swap(totals, axis)
    loss_sum = totals[0]
    grad_norm = jnp.sqrt(totals[1])
    factor = jnp.minimum(1.0, CLIP / grad_norm)
    weights = (attn_in, attn_out, ff_in, ff_out, table, gains)
    moments = (attn_in_mom, attn_out_mom, ff_in_mom, ff_out_mom, table_mom, gains_mom)
    averages = (attn_in_avg, attn_out_avg, ff_in_avg, ff_out_avg, table_avg, gains_avg)
    results = [
        update(weight, gradient, moment, average, rate, factor)
        for weight, gradient, moment, average, rate in zip(
            weights, gradients, moments, averages, step_rates()
        )
    ]
    return (loss_sum, scored_count, grad_norm) + tuple(
        results[array][kind] for kind in range(3) for array in range(6)
    )


def solution(mesh):
    dp_count, mp_count = mesh.shape["dp"], mesh.shape["mp"]
    dp_axes = tuple(f"d{k}" for k in range(dp_count.bit_length() - 1))
    mp_axes = tuple(f"m{k}" for k in range(mp_count.bit_length() - 1))
    every = dp_axes + mp_axes
    fine = Mesh(mesh.devices.reshape((2,) * len(every)), every)
    rows_split = P(None, every, None)
    params = (rows_split,) * 4 + (P(mp_axes, dp_axes), P(None, every))
    in_specs = (P(dp_axes, None), P(dp_axes, None), P()) + params * 3
    out_specs = (P(), P(), P()) + params * 3
    return jax.shard_map(
        partial(on_device, dp_axes, mp_axes),
        mesh=fine,
        in_specs=in_specs,
        out_specs=out_specs,
        check_vma=False,
    )
```

```python
from functools import partial

import jax
import jax.numpy as jnp
from jax import lax
from jax.experimental import pallas as pl
from jax.experimental.pallas import tpu as pltpu
from jax.sharding import Mesh
from jax.sharding import PartitionSpec as P

D = 1024
HQ = 16
HK = 8
HD = 64
FF = 2816
LEN = 1024
QW = 1024
KW = 512
PARAMS = 59644928

MOMENTUM = 0.9
AVERAGE = 0.9
CLIP = 0.0002
EPS = 1e-06

BF = jnp.bfloat16
F32 = jnp.float32
MESH = pl.DeviceIdType.MESH
CHUNK = 256
LANES = 3
PREFIX_LOW = 192


def step_rates():
    base_rate = 3.5 * PARAMS**0.5 / CLIP
    return (
        base_rate * D ** (-0.5),
        base_rate * max(QW // LEN, 1) ** (-0.5),
        base_rate * D ** (-0.5),
        base_rate * FF ** (-0.5),
        base_rate * 2.0,
        base_rate * 0.3,
    )


def swap(value, axis):
    return lax.ppermute(value, axis, [(0, 1), (1, 0)])


def take_bit(value, bit, position):
    return lax.dynamic_index_in_dim(value, bit, position, keepdims=False)


def gather_blocks(block, layout, order):
    have = []
    held = block
    for axis in order:
        received = swap(held, axis)
        position = sum(layout.index(other) < layout.index(axis) for other in have)
        bit = lax.axis_index(axis)
        shape = held.shape
        joined = jnp.zeros(shape[:position] + (2,) + shape[position:], held.dtype)
        joined = lax.dynamic_update_index_in_dim(joined, held, bit, position)
        held = lax.dynamic_update_index_in_dim(joined, received, 1 - bit, position)
        have.append(axis)
    return held


def sum_blocks(terms, layout, order, last=F32, beside=None):
    left = list(layout)
    held = terms
    for axis in order:
        position = left.index(axis)
        bit = lax.axis_index(axis)
        received = swap(take_bit(held, 1 - bit, position), axis)
        if beside is not None and axis == order[1]:
            received, result = lax.optimization_barrier((received, beside(held)))
        held = take_bit(held, bit, position).astype(F32) + received.astype(F32)
        left.remove(axis)
        if left:
            held = held.astype(terms.dtype)
    return held.astype(last) if beside is None else (held.astype(last), result)


def greet(axes):
    barrier = pltpu.get_barrier_semaphore()
    for axis in axes:
        pl.semaphore_signal(
            barrier, inc=1, device_id={axis: 1 - lax.axis_index(axis)}, device_id_type=MESH
        )
    pl.semaphore_wait(barrier, len(axes))


def gather_kernel(layout, units, lanes, count, *refs):
    ins, outs = refs[:count], refs[count : 2 * count]
    own_sem, send_sem, recv_sem = refs[2 * count :]
    bits = {axis: lax.axis_index(axis) for axis in layout}
    depth = len(layout)

    def region(unit, have):
        tensor, start, size, _ = units[unit]
        blocks = tuple(pl.ds(0, 2) if axis in have else bits[axis] for axis in layout)
        return outs[tensor].at[blocks + (slice(None), pl.ds(start, size))]

    own = [
        pltpu.make_async_copy(
            ins[k], outs[k].at[tuple(bits[axis] for axis in layout)], own_sem.at[k]
        )
        for k in range(count)
    ]
    for copy in own:
        copy.start()
    greet(layout)
    for copy in own:
        copy.wait()
    copies = {}
    groups = -(-len(units) // lanes)
    for turn in range(groups + depth - 1):
        for step in reversed(range(depth)):
            first = (turn - step) * lanes
            for unit in range(max(first, 0), min(first + lanes, len(units))):
                order = units[unit][3]
                if step:
                    copies[unit, step - 1].wait_recv()
                source = region(unit, order[:step])
                copy = pltpu.make_async_remote_copy(
                    src_ref=source,
                    dst_ref=source,
                    send_sem=send_sem.at[unit, step],
                    recv_sem=recv_sem.at[unit, step],
                    device_id={order[step]: 1 - bits[order[step]]},
                    device_id_type=MESH,
                )
                copy.start()
                copies[unit, step] = copy
    for unit in range(len(units)):
        copies[unit, depth - 1].wait_recv()
    for copy in copies.values():
        copy.wait_send()


def gather_all(shards, layout, orders):
    units = []
    for tensor, shard in enumerate(shards):
        columns = shard.shape[1]
        step = -(-512 * 32 // shard.shape[0] // 128) * 128
        pieces = -(-columns // step)
        starts = [step * piece for piece in range(pieces)] + [columns]
        for piece in range(pieces):
            order = orders[len(units) % len(orders)]
            units.append((tensor, starts[piece], starts[piece + 1] - starts[piece], order))
    count = len(shards)
    semaphores = pltpu.SemaphoreType.DMA((len(units), len(layout)))
    return pl.pallas_call(
        partial(gather_kernel, layout, tuple(units), LANES, count),
        out_shape=[
            jax.ShapeDtypeStruct((2,) * len(layout) + shard.shape, shard.dtype) for shard in shards
        ],
        in_specs=[pl.BlockSpec(memory_space=pl.ANY)] * count,
        out_specs=[pl.BlockSpec(memory_space=pl.ANY)] * count,
        scratch_shapes=[pltpu.SemaphoreType.DMA((count,)), semaphores, semaphores],
        compiler_params=pltpu.CompilerParams(collective_id=0, has_side_effects=True),
        name="gather_weights",
    )(*shards)


def grad_kernel(layout, orders, bounds, chunks, *refs):
    x_ref, y_ref, out_ref = refs[:3]
    depth = len(layout)
    lanes = len(orders)
    scratch = refs[3:]
    sends, recvs, helds = (
        [scratch[kind * lanes * depth + lane * depth :][:depth] for lane in range(lanes)]
        for kind in range(3)
    )
    send_sem, recv_sem = scratch[3 * lanes * depth :]
    bits = {axis: lax.axis_index(axis) for axis in layout}
    groups = out_ref.shape[0] // lanes
    greet(layout)

    def exchange(lane, step, group):
        axis = orders[lane][step]
        slot = lax.rem(group, 2)
        return pltpu.make_async_remote_copy(
            src_ref=sends[lane][step],
            dst_ref=recvs[lane][step].at[slot],
            send_sem=send_sem.at[lane, step],
            recv_sem=recv_sem.at[lane, step, slot],
            device_id={axis: 1 - bits[axis]},
            device_id_type=MESH,
        )

    def first(lane, group):
        chunk = jnp.minimum(group * lanes + lane, chunks - 1)
        which = sum((chunk >= bound).astype(jnp.int32) for bound in bounds) if bounds else 0
        columns = y_ref[:, pl.ds(pl.multiple_of(chunk * CHUNK, CHUNK), CHUNK)]
        bit = bits[orders[lane][0]]
        given = jnp.dot(x_ref[which, 1 - bit], columns, preferred_element_type=F32)
        sends[lane][0][...] = given.astype(BF).reshape(sends[lane][0].shape)
        exchange(lane, 0, group).start()
        kept = jnp.dot(x_ref[which, bit], columns, preferred_element_type=F32)
        helds[lane][0][...] = kept.reshape(helds[lane][0].shape)

    def later(lane, step, group):
        order = orders[lane]
        slot = lax.rem(group, 2)
        exchange(lane, step - 1, group).wait()
        held, received = helds[lane][step - 1], recvs[lane][step - 1]
        if step == depth:
            out_ref[group * lanes + lane] = held[...] + received[slot].astype(F32)
            return
        position = [axis for axis in layout if axis not in order[:step]].index(order[step])
        bit = bits[order[step]]

        def total(choice):
            index = (slice(None),) * position + (choice,)
            return held[index] + received[(slot,) + index].astype(F32)

        sends[lane][step][...] = total(1 - bit).astype(BF)
        exchange(lane, step, group).start()
        helds[lane][step][...] = total(bit)

    @pl.loop(0, groups + depth)
    def _(turn):
        for step in reversed(range(depth + 1)):
            group = turn - step

            @pl.when((group >= 0) & (group < groups))
            def _():
                for lane in range(lanes):
                    if step:
                        later(lane, step, group)
                    else:
                        first(lane, group)


def grad_sums(lefts, rights, layout, orders, spans, collective):
    depth, lanes = len(layout), len(orders)
    tokens, width = max(left.shape[0] for left in lefts), lefts[0].shape[1]
    lefts, rights = (
        [jnp.pad(term, ((tokens - term.shape[0], 0), (0, 0))) for term in terms]
        for terms in (lefts, rights)
    )
    rows = width // 2**depth
    padded = -(-rows // 16) * 16
    blocks = jnp.stack(lefts).transpose(0, 2, 1).reshape(len(lefts), -1, 2, rows, tokens)
    blocks = jnp.pad(blocks, ((0, 0),) * 3 + ((0, padded - rows), (0, 0)))
    x = blocks.swapaxes(1, 2).reshape(len(lefts), 2, -1, tokens)
    y = jnp.concatenate(rights, axis=1)
    chunks = y.shape[1] // CHUNK
    groups = -(-chunks // lanes)
    bounds, passed = [], 0
    for span in spans[:-1]:
        passed += span // CHUNK
        bounds.append(passed)
    send_shapes, recv_shapes, held_shapes = [], [], []
    for _ in range(lanes):
        for step in range(depth):
            shape = (2,) * (depth - 1 - step) + (padded, CHUNK)
            send_shapes.append(pltpu.VMEM(shape, BF))
            recv_shapes.append(pltpu.VMEM((2,) + shape, BF))
            held_shapes.append(pltpu.VMEM(shape, F32))
    out = pl.pallas_call(
        partial(grad_kernel, layout, orders, tuple(bounds), chunks),
        out_shape=jax.ShapeDtypeStruct((groups * lanes, padded, CHUNK), F32),
        in_specs=[pl.BlockSpec(memory_space=pltpu.VMEM)] * 2,
        out_specs=pl.BlockSpec(memory_space=pltpu.VMEM),
        scratch_shapes=send_shapes
        + recv_shapes
        + held_shapes
        + [
            pltpu.SemaphoreType.DMA((lanes, depth)),
            pltpu.SemaphoreType.DMA((lanes, depth, 2)),
        ],
        compiler_params=pltpu.CompilerParams(
            collective_id=collective, has_side_effects=True, vmem_limit_bytes=56 * 1024 * 1024
        ),
        name="sum_gradients",
    )(x, y)
    return out[:chunks, :rows].transpose(1, 0, 2).reshape(rows, -1)


def total_kernel(layout, value_ref, out_ref, send_ref, recv_ref, send_sem, recv_sem):
    greet(layout)
    held = value_ref[...]
    for step, axis in enumerate(layout):
        send_ref[step] = held
        copy = pltpu.make_async_remote_copy(
            src_ref=send_ref.at[step],
            dst_ref=recv_ref.at[step],
            send_sem=send_sem.at[step],
            recv_sem=recv_sem.at[step],
            device_id={axis: 1 - lax.axis_index(axis)},
            device_id_type=MESH,
        )
        copy.start()
        copy.wait()
        held = held + recv_ref[step]
    out_ref[...] = held


def total_of(values, layout, collective):
    depth = len(layout)
    tile = jnp.broadcast_to(jnp.pad(values, (0, 8 - values.shape[0]))[:, None], (8, 128))
    sums = pl.pallas_call(
        partial(total_kernel, layout),
        out_shape=jax.ShapeDtypeStruct(tile.shape, F32),
        in_specs=[pl.BlockSpec(memory_space=pltpu.VMEM)],
        out_specs=pl.BlockSpec(memory_space=pltpu.VMEM),
        scratch_shapes=[pltpu.VMEM((depth, 8, 128), F32)] * 2
        + [pltpu.SemaphoreType.DMA((depth,))] * 2,
        compiler_params=pltpu.CompilerParams(collective_id=collective, has_side_effects=True),
        name="sum_numbers",
    )(tile)
    return sums[: values.shape[0], 0]


def rows_kernel(ids_ref, table_ref, out_ref, held_ref):
    groups = held_ref.shape[0]
    first = pl.program_id(0) * groups * 8

    def eight(group, carry):
        for k in range(8):
            place = ids_ref[first + group * 8 + k]
            held_ref[group, pl.ds(k, 1), :] = table_ref[pl.ds(place, 1), :]
        return carry

    lax.fori_loop(0, groups, eight, 0)
    out_ref[...] = held_ref[...].reshape(out_ref.shape).astype(BF)


def rows_of(table, places):
    count, width = places.shape[0], table.shape[1]
    step = 512
    return pl.pallas_call(
        rows_kernel,
        grid=(count // step,),
        out_shape=jax.ShapeDtypeStruct((count, width), BF),
        in_specs=[
            pl.BlockSpec(memory_space=pltpu.SMEM),
            pl.BlockSpec(table.shape, lambda i: (0, 0)),
        ],
        out_specs=pl.BlockSpec((step, width), lambda i: (i, 0)),
        scratch_shapes=[pltpu.VMEM((step // 8, 8, width), F32)],
        compiler_params=pltpu.CompilerParams(vmem_limit_bytes=48 * 1024 * 1024),
        cost_estimate=pl.CostEstimate(
            flops=0, bytes_accessed=80 * count * width, transcendentals=0
        ),
        name="look_up",
    )(places, table)


def mm(left, right):
    return jnp.dot(left, right, preferred_element_type=F32)


def mm_nt(left, right):
    return lax.dot_general(left, right, (((1,), (1,)), ((), ())), preferred_element_type=F32)


def mm_tn(left, right):
    return lax.dot_general(left, right, (((0,), (0,)), ((), ())), preferred_element_type=F32)


def norm_forward(stream, gain_row):
    inverse = lax.rsqrt(jnp.mean(stream * stream, axis=-1, keepdims=True) + EPS)
    return stream * inverse * gain_row


def norm_backward(stream, gain_row, grad_out):
    inverse = lax.rsqrt(jnp.mean(stream * stream, axis=-1, keepdims=True) + EPS)
    scaled = grad_out * gain_row
    d_input = inverse * scaled - stream * inverse**3 * jnp.mean(
        stream * scaled, axis=-1, keepdims=True
    )
    return (d_input, jnp.sum(grad_out * stream * inverse, axis=0))


def nt(left, right):
    return lax.dot_general(left, right, (((1,), (1,)), ((), ())), preferred_element_type=F32)


def allowed_keys(row_ref, shape, by_query, per_item):
    queries = lax.broadcasted_iota(jnp.int32, shape, by_query)
    keys = lax.broadcasted_iota(jnp.int32, shape, 1 - by_query)
    each = shape[1 - by_query] // per_item
    return row_ref[0] + queries * per_item >= lax.rem(keys, each) * per_item + keys // each


def attend_kernel(causal, row_ref, q_ref, k_ref, v_ref, o_ref):
    rows, length = q_ref.shape[0], k_ref.shape[0]
    shape = (rows, length)
    if causal:
        allowed = allowed_keys(row_ref, shape, 0, causal)
    for head in range(q_ref.shape[1] // HD):
        own = pl.ds(head * HD, HD)
        shared = pl.ds(head // (HQ // HK) * HD, HD)
        scores = nt(q_ref[:, own], k_ref[:, shared]) * HD ** (-0.5)
        if causal:
            scores = jnp.where(allowed, scores, -1000000000.0)
        expo = jnp.exp(scores - jnp.max(scores, axis=-1, keepdims=True))
        probs = expo * (1.0 / jnp.sum(expo, axis=-1, keepdims=True))
        mixed = jnp.dot(probs.astype(BF), v_ref[:, shared], preferred_element_type=F32)
        o_ref[:, own] = mixed.astype(BF)


def attend_back_kernel(causal, row_ref, q_ref, k_ref, v_ref, d_ref, dq_ref, dk_ref, dv_ref):
    rows, length = q_ref.shape[0], k_ref.shape[0]
    shape = (length, rows)
    share = HQ // HK
    if causal:
        allowed = allowed_keys(row_ref, shape, 1, causal)
    for pair in range(k_ref.shape[1] // HD):
        shared = pl.ds(pair * HD, HD)
        keys, values = k_ref[:, shared], v_ref[:, shared]
        d_keys = d_values = None
        for head in range(pair * share, (pair + 1) * share):
            own = pl.ds(head * HD, HD)
            queries, d_mixed = q_ref[:, own], d_ref[:, own]
            scores = nt(keys, queries) * HD ** (-0.5)
            if causal:
                scores = jnp.where(allowed, scores, -1000000000.0)
            expo = jnp.exp(scores - jnp.max(scores, axis=0, keepdims=True))
            probs = expo * (1.0 / jnp.sum(expo, axis=0, keepdims=True))
            d_probs = nt(values, d_mixed)
            mean = jnp.sum(probs * d_probs, axis=0, keepdims=True)
            d_scores = (probs * (d_probs - mean)).astype(BF)
            key_term = jnp.dot(d_scores, queries, preferred_element_type=F32)
            value_term = jnp.dot(probs.astype(BF), d_mixed, preferred_element_type=F32)
            d_keys = key_term if d_keys is None else d_keys + key_term
            d_values = value_term if d_values is None else d_values + value_term
            d_queries = lax.dot_general(
                keys, d_scores, (((0,), (0,)), ((), ())), preferred_element_type=F32
            )
            dq_ref[:, own] = (d_queries.T * HD ** (-0.5)).astype(BF)
        dk_ref[:, shared] = (d_keys * HD ** (-0.5)).astype(BF)
        dv_ref[:, shared] = d_values.astype(BF)


def attend_specs(rows, length):
    wide = 128 * (HQ // HK)
    queries = pl.BlockSpec((rows, wide), lambda i: (0, i))
    keys = pl.BlockSpec((length, 128), lambda i: (0, i))
    values = pl.BlockSpec((length, 128), lambda i: (0, i + KW // 128))
    return queries, keys, values


def attend_forward(queries, keyvals, first_row, per_item):
    rows, length = queries.shape[0], keyvals.shape[0]
    by_query, by_key, by_value = attend_specs(rows, length)
    return pl.pallas_call(
        partial(attend_kernel, 0 if first_row is None else per_item),
        grid=(KW // 128,),
        out_shape=jax.ShapeDtypeStruct(queries.shape, BF),
        in_specs=[pl.BlockSpec(memory_space=pltpu.SMEM), by_query, by_key, by_value],
        out_specs=by_query,
        compiler_params=pltpu.CompilerParams(vmem_limit_bytes=56 * 1024 * 1024),
        cost_estimate=pl.CostEstimate(
            flops=4 * rows * length * QW,
            bytes_accessed=4 * rows * QW + 4 * length * KW,
            transcendentals=HQ * rows * length,
        ),
        name="attend",
    )(jnp.reshape(0 if first_row is None else first_row, (1,)), queries, keyvals, keyvals)


def attend_backward(queries, keyvals, first_row, per_item, d_mixed):
    rows, length = queries.shape[0], keyvals.shape[0]
    by_query, by_key, by_value = attend_specs(rows, length)
    d_queries, d_keys, d_values = pl.pallas_call(
        partial(attend_back_kernel, 0 if first_row is None else per_item),
        grid=(KW // 128,),
        out_shape=[
            jax.ShapeDtypeStruct(queries.shape, BF),
            jax.ShapeDtypeStruct((length, KW), BF),
            jax.ShapeDtypeStruct((length, KW), BF),
        ],
        in_specs=[pl.BlockSpec(memory_space=pltpu.SMEM), by_query, by_key, by_value, by_query],
        out_specs=[by_query, by_key, by_key],
        compiler_params=pltpu.CompilerParams(vmem_limit_bytes=56 * 1024 * 1024),
        cost_estimate=pl.CostEstimate(
            flops=10 * rows * length * QW,
            bytes_accessed=6 * rows * QW + 8 * length * KW,
            transcendentals=HQ * rows * length,
        ),
        name="attend_back",
    )(jnp.reshape(0 if first_row is None else first_row, (1,)), queries, keyvals, keyvals, d_mixed)
    return (d_queries, jnp.concatenate([d_keys, d_values], axis=1))


def update(weight, gradient, moment, average, rate, factor):
    clipped = gradient * factor
    moment_new = MOMENTUM * moment + (1 - MOMENTUM) * clipped
    weight_new = weight - rate * ((1 - MOMENTUM) * clipped + MOMENTUM * moment_new)
    average_new = AVERAGE * average + (1 - AVERAGE) * weight_new
    return (weight_new, moment_new, average_new)


def on_device(
    dp_axes,
    mp_axes,
    source_ids,
    target_ids,
    prefix,
    attn_in,
    attn_out,
    ff_in,
    ff_out,
    table,
    gains,
    attn_in_mom,
    attn_out_mom,
    ff_in_mom,
    ff_out_mom,
    table_mom,
    gains_mom,
    attn_in_avg,
    attn_out_avg,
    ff_in_avg,
    ff_out_avg,
    table_avg,
    gains_avg,
):
    every = dp_axes + mp_axes
    core = mp_axes[-1]
    row_axes = mp_axes[1:]
    line = mp_axes[:-1]
    gather_orders = (
        line + dp_axes + (core,),
        line + dp_axes[::-1] + (core,),
        dp_axes + line + (core,),
    )
    sum_orders = tuple(order[::-1] for order in gather_orders)
    last = (line[-1], core)
    three = (gather_orders[0], gather_orders[1], line[:-1] + dp_axes[::-1] + last)
    six_orders = three + three[:2] + (line[:-1] + dp_axes + last,)
    two_dp, two_mp, two_rows = (2,) * len(dp_axes), (2,) * len(mp_axes), (2,) * len(row_axes)

    seq_count, length = source_ids.shape
    rows = length // 2 ** len(row_axes)
    per_item = 2 ** len(row_axes)
    skip = PREFIX_LOW // per_item
    first_row = lax.axis_index(row_axes)

    def by_device(values):
        return values.reshape(values.shape[:-1] + (rows, per_item)).swapaxes(-1, -2)

    def with_skipped(values):
        return jnp.pad(values, ((rows - values.shape[0], 0), (0, 0)))


    vocab_part = table.shape[0]
    offset = lax.axis_index(mp_axes) * vocab_part
    table_bf = table.astype(BF)
    decoder_ids = jnp.concatenate(
        [jnp.zeros((seq_count, 1), jnp.int32), target_ids[:, :-1]], axis=1
    )
    ids_all = by_device(gather_blocks(jnp.stack([source_ids, decoder_ids]), dp_axes, dp_axes))
    ids_all = ids_all.reshape(-1, 2, 2 ** len(mp_axes), rows).transpose(1, 2, 0, 3).reshape(2, -1)
    ids_all, sent_table = lax.optimization_barrier((ids_all, table_bf))
    table_rows = lax.all_gather(sent_table, dp_axes, axis=1, tiled=True)
    local_ids = ids_all - offset
    inside = (local_ids >= 0) & (local_ids < vocab_part)

    def trade(parts):
        for position, axis in enumerate(dp_axes):
            bit = lax.axis_index(axis)
            received = swap(take_bit(parts, 1 - bit, position), axis)
            kept = take_bit(parts, bit, position)
            parts = jnp.stack(
                [jnp.where(bit == 0, kept, received), jnp.where(bit == 0, received, kept)],
                axis=position,
            )
        return parts

    table_zero = jnp.pad(table, ((0, 8), (0, 0)))
    places = jnp.where(inside, local_ids, vocab_part)

    def look_up(which):
        found = rows_of(table_zero, places[which])
        return found.reshape(2 ** len(mp_axes), -1, found.shape[-1])

    def collect(found):
        return lax.psum_scatter(found, mp_axes, scatter_dimension=0)

    def embed(mine):
        width = mine.shape[-1]
        parts = trade(mine.reshape(two_dp + (rows, width))).reshape(-1, rows, width)
        return jnp.moveaxis(parts, 0, 1).reshape(rows, -1).astype(F32)

    found_e = look_up(0)
    mine_e = collect(found_e)
    found_d = look_up(1)
    mine_d = collect(found_d)

    shards = [attn_in[0], attn_out[0], ff_in[0], ff_out[0]]
    shards += [attn_in[1], attn_out[1], attn_in[2], attn_out[2], ff_in[1], ff_out[1]]
    shards = [shard.astype(BF) for shard in shards]
    in_kernels = attn_in.shape[1] % 16 == 0
    if in_kernels:
        *shards, found_e, found_d = lax.optimization_barrier(shards + [found_e, found_d])
        full = list(gather_all(shards, every, six_orders))
        full[0], mine_e, mine_d = lax.optimization_barrier((full[0], mine_e, mine_d))
    else:
        full = [
            gather_blocks(shard, every, gather_orders[k % 3]) for k, shard in enumerate(shards)
        ]
    full = [got.reshape((-1,) + shard.shape[1:]) for got, shard in zip(full, shards)]
    a_in, a_out = (full[0], full[4], full[6]), (full[1], full[5], full[7])
    f_in, f_out = (full[2], full[8]), (full[3], full[9])
    gain_all = gather_blocks(gains.astype(BF).T, every, gather_orders[0])
    gain_all = gain_all.reshape(-1, gains.shape[0]).T.astype(F32)

    def spread_keys(own):
        return gather_blocks(own, row_axes, row_axes).reshape(length, -1)

    def attention_forward(stream, source, block, gain_row, start):
        normed = norm_forward(stream, gain_row).astype(BF)
        anchor = normed if source is None else source
        keyvals = spread_keys(mm(anchor, a_in[block][:, QW:]).astype(BF))
        first = 0 if start is None else skip
        queries = mm(normed[first:], a_in[block][:, :QW]).astype(BF)
        position = None if start is None else start + first * per_item
        mixed = attend_forward(queries, keyvals, position, per_item)
        out = stream[first:] + mm(mixed, a_out[block])
        return (out, (stream, normed, anchor, queries, keyvals, mixed))

    def ffn_forward(stream, which, gain_row):
        normed = norm_forward(stream, gain_row).astype(BF)
        both = mm(normed, f_in[which])
        hidden_act = (jax.nn.gelu(both[:, :FF], approximate=True) * both[:, FF:]).astype(BF)
        return (stream + mm(hidden_act, f_out[which]), (stream, normed, both, hidden_act))

    stream_e = embed(mine_e)
    stream_e, enc_attn = attention_forward(stream_e, None, 0, gain_all[0], None)
    stream_e, mine_d = lax.optimization_barrier((stream_e, mine_d))
    stream_d = embed(mine_d)
    stream_d, dec_self = attention_forward(stream_d, None, 1, gain_all[3], first_row)
    stream_e, enc_ffn = ffn_forward(stream_e, 0, gain_all[1])
    encoded = norm_forward(stream_e, gain_all[2]).astype(BF)
    stream_d, dec_cross = attention_forward(stream_d, encoded, 2, gain_all[4], None)
    stream_d, dec_ffn = ffn_forward(stream_d, 1, gain_all[5])
    hidden = norm_forward(stream_d, gain_all[6]).astype(BF)

    hidden_all = gather_blocks(hidden, mp_axes, mp_axes).reshape(-1, hidden.shape[-1])
    targets = by_device(target_ids)[..., skip:].reshape(-1)
    vocab_ids = offset + jnp.arange(vocab_part)
    hits = vocab_ids[None, :] == targets[:, None]
    logits = mm_nt(hidden_all, table_rows) * D ** (-0.5)
    own_max = jnp.max(logits, axis=-1)
    expo = jnp.exp(logits - own_max[:, None])
    stats = jnp.stack(
        [own_max, jnp.sum(expo, axis=-1), jnp.sum(jnp.where(hits, logits, 0.0), axis=-1)]
    )
    expo = expo.astype(BF)
    for axis in mp_axes[::-1]:
        other = swap(stats, axis)
        joint = jnp.maximum(stats[0], other[0])
        stats = jnp.stack(
            [
                joint,
                stats[1] * jnp.exp(stats[0] - joint) + other[1] * jnp.exp(other[0] - joint),
                stats[2] + other[2],
            ]
        )
    log_norm = stats[0] + jnp.log(stats[1])
    prefix_group = lax.dynamic_slice_in_dim(prefix, lax.axis_index(dp_axes) * seq_count, seq_count)
    positions = by_device(jnp.arange(length))[..., skip:].reshape(1, -1)
    scored = (positions >= prefix_group[:, None]).astype(F32).reshape(-1)
    scored_count = jnp.sum((length - prefix).astype(F32))
    scale = jnp.exp(own_max - log_norm)
    d_logits = (
        (expo.astype(F32) * scale[:, None] - hits.astype(F32)) * (scored / scored_count)[:, None]
    ).astype(BF)
    d_final = (mm(d_logits, table_rows) * D ** (-0.5)).astype(BF)

    def table_term(held):
        _, rows_all = lax.optimization_barrier((held, hidden_all))
        return (mm_tn(d_logits, rows_all) * D ** (-0.5)).astype(BF)

    d_final, head_table = sum_blocks(
        d_final.reshape(two_mp + hidden.shape), mp_axes, mp_axes[::-1], F32, table_term
    )

    grad_table = lax.psum_scatter(head_table, dp_axes, scatter_dimension=1, tiled=True)

    def ffn_backward(saved, which, gain_row, d_stream):
        stream, normed, both, hidden_act = saved
        up_part = both[:, FF:]
        activated, gelu_pull = jax.vjp(partial(jax.nn.gelu, approximate=True), both[:, :FF])
        d_branch = d_stream.astype(BF)
        d_hidden = mm_nt(d_branch, f_out[which])
        d_both = jnp.concatenate(
            [gelu_pull(d_hidden * up_part)[0].astype(BF), (d_hidden * activated).astype(BF)], axis=1
        )
        d_normed = mm_nt(d_both, f_in[which])
        d_input, grad_gain = norm_backward(stream, gain_row, d_normed)
        return (d_stream + d_input, (normed, d_both, hidden_act, d_branch), grad_gain)

    def attention_backward(saved, cross, block, gain_row, start, d_stream):
        stream, normed, anchor, queries, keyvals, mixed = saved
        d_branch = d_stream.astype(BF)
        d_mixed = mm_nt(d_branch, a_out[block]).astype(BF)
        queries = with_skipped(queries)
        d_queries, d_keyvals = attend_backward(
            queries, keyvals, start, per_item, with_skipped(d_mixed)
        )
        d_keyvals = sum_blocks(
            d_keyvals.reshape(two_rows + (rows, -1)), row_axes, row_axes[::-1], BF
        )
        d_queries = d_queries[rows - stream.shape[0] :]
        d_normed = mm_nt(d_queries, a_in[block][:, :QW])
        d_anchor = mm_nt(d_keyvals, a_in[block][:, QW:])
        if not cross:
            d_normed = d_normed + d_anchor
        factors = (normed, anchor, with_skipped(d_queries), d_keyvals, mixed, d_branch)
        d_input, grad_gain = norm_backward(stream, gain_row, d_normed)
        if start is not None:
            d_stream = with_skipped(d_stream)
        return (d_stream + d_input, d_anchor, factors, grad_gain)

    d_y, gain6 = norm_backward(stream_d, gain_all[6], d_final)
    d_y, ffn_factors1, gain5 = ffn_backward(dec_ffn, 1, gain_all[5], d_y)
    d_y, d_encoded, attn_factors2, gain4 = attention_backward(
        dec_cross, True, 2, gain_all[4], None, d_y
    )
    d_y, _, attn_factors1, gain3 = attention_backward(
        dec_self, False, 1, gain_all[3], first_row, d_y
    )
    d_x, gain2 = norm_backward(stream_e, gain_all[2], d_encoded)
    d_x, ffn_factors0, gain1 = ffn_backward(enc_ffn, 0, gain_all[1], d_x)
    d_x, _, attn_factors0, gain0 = attention_backward(
        enc_attn, False, 0, gain_all[0], None, d_x
    )

    def trade_rows(d_rows):
        width = table.shape[1]
        parts = jnp.moveaxis(d_rows.astype(BF).reshape(rows, -1, width), 1, 0)
        return trade(parts.reshape(two_dp + (rows, width))).reshape(-1, width)

    def look_back(which, spread):
        places = (local_ids[which][None, :] == jnp.arange(vocab_part)[:, None]).astype(BF)
        return mm(places, spread.reshape(-1, spread.shape[-1]))

    traded_y, traded_x = trade_rows(d_y), trade_rows(d_x)
    spread_y, spread_x = (lax.all_gather(traded, mp_axes) for traded in (traded_y, traded_x))

    gain_grads = jnp.stack([gain0, gain1, gain2, gain3, gain4, gain5, gain6])
    gain_blocks = jnp.moveaxis(gain_grads.reshape(gains.shape[0], -1, gains.shape[1]), 1, 0)
    grad_gains = sum_blocks(
        gain_blocks.reshape((2,) * len(every) + gains.shape), every, sum_orders[0]
    )

    lefts, rights = [], []
    if in_kernels:
        traded_x, ffn_left, attn_left = lax.optimization_barrier(
            (traded_x, ffn_factors0[2], attn_factors0[0])
        )
        attn_factors0 = (attn_left, attn_left) + attn_factors0[2:]
        ffn_factors0 = ffn_factors0[:2] + (ffn_left,) + ffn_factors0[3:]
    for normed, anchor, d_queries, d_keyvals, mixed, d_branch in (
        attn_factors0,
        attn_factors1,
        attn_factors2,
    ):
        if anchor is normed:
            lefts += [normed, mixed]
            rights += [jnp.concatenate([d_queries, d_keyvals], axis=1), d_branch]
        else:
            lefts += [with_skipped(normed), anchor, mixed]
            rights += [d_queries, d_keyvals, d_branch]
    wide_lefts, wide_rights = [], []
    for normed, d_both, hidden_act, d_branch in (ffn_factors0, ffn_factors1):
        lefts.append(normed)
        rights.append(d_both)
        wide_lefts.append(hidden_act)
        wide_rights.append(d_branch)
    spans = [right.shape[1] for right in rights]
    wide_spans = [right.shape[1] for right in wide_rights]
    if in_kernels:
        back_orders = tuple(order[::-1] for order in three)
        own = grad_sums(lefts, rights, every, back_orders, spans, 1)
        wide = grad_sums(wide_lefts, wide_rights, every, back_orders, wide_spans, 2)
        own, wide, spread_x, spread_y = lax.optimization_barrier((own, wide, spread_x, spread_y))
    else:

        def own_sum(left, right, kind):
            product = mm_tn(left, right).astype(BF)
            blocks = product.reshape((2,) * len(every) + (-1,) + product.shape[1:])
            return sum_blocks(blocks, every, sum_orders[kind % 3])

        pairs = list(enumerate(zip(lefts, rights)))
        own = jnp.concatenate([own_sum(*pair, k) for k, pair in pairs], axis=1)
        pairs = list(enumerate(zip(wide_lefts, wide_rights)))
        wide = jnp.concatenate([own_sum(*pair, k) for k, pair in pairs], axis=1)
    grad_table = grad_table.astype(F32) + look_back(1, spread_y) + look_back(0, spread_x)
    ends = (attn_in.shape[2], attn_in.shape[2] + attn_out.shape[2])
    ffn_from = 3 * ends[1]
    gradients = (
        jnp.stack([own[:, ends[1] * k : ends[1] * k + ends[0]] for k in range(3)]),
        jnp.stack([own[:, ends[1] * k + ends[0] : ends[1] * (k + 1)] for k in range(3)]),
        jnp.stack([own[:, ffn_from + 2 * FF * k : ffn_from + 2 * FF * (k + 1)] for k in range(2)]),
        jnp.stack(jnp.split(wide, 2, axis=1)),
        grad_table,
        grad_gains,
    )

    own_losses = ((log_norm - stats[2]) * scored).reshape(2 ** len(mp_axes), -1)
    loss_part = jnp.sum(take_bit(own_losses, lax.axis_index(mp_axes), 0))
    squares = sum((jnp.sum(gradient * gradient) for gradient in gradients))
    totals = jnp.stack([loss_part, squares])
    totals = total_of(totals, every[::-1], 3)
    loss_sum = totals[0]
    grad_norm = jnp.sqrt(totals[1])
    factor = jnp.minimum(1.0, CLIP / grad_norm)
    weights = (attn_in, attn_out, ff_in, ff_out, table, gains)
    moments = (attn_in_mom, attn_out_mom, ff_in_mom, ff_out_mom, table_mom, gains_mom)
    averages = (attn_in_avg, attn_out_avg, ff_in_avg, ff_out_avg, table_avg, gains_avg)
    results = [
        update(weight, gradient, moment, average, rate, factor)
        for weight, gradient, moment, average, rate in zip(
            weights, gradients, moments, averages, step_rates()
        )
    ]
    return (loss_sum, scored_count, grad_norm) + tuple(
        results[array][kind] for kind in range(3) for array in range(6)
    )


def solution(mesh):
    dp_count, mp_count = mesh.shape["dp"], mesh.shape["mp"]
    dp_axes = tuple(f"d{k}" for k in range(dp_count.bit_length() - 1))
    mp_axes = tuple(f"m{k}" for k in range(mp_count.bit_length() - 1))
    every = dp_axes + mp_axes
    fine = Mesh(mesh.devices.reshape((2,) * len(every)), every)
    rows_split = P(None, every, None)
    params = (rows_split,) * 4 + (P(mp_axes, dp_axes), P(None, every))
    in_specs = (P(dp_axes, None), P(dp_axes, None), P()) + params * 3
    out_specs = (P(), P(), P()) + params * 3
    return jax.shard_map(
        partial(on_device, dp_axes, mp_axes),
        mesh=fine,
        in_specs=in_specs,
        out_specs=out_specs,
        check_vma=False,
    )
```

```python
from functools import partial

import jax
import jax.numpy as jnp
from jax import lax
from jax.experimental import pallas as pl
from jax.experimental.pallas import tpu as pltpu
from jax.sharding import Mesh
from jax.sharding import PartitionSpec as P

D = 1024
HQ = 16
HK = 8
HD = 64
FF = 2816
LEN = 1024
QW = 1024
KW = 512
PARAMS = 59644928

MOMENTUM = 0.9
AVERAGE = 0.9
CLIP = 0.0002
EPS = 1e-06

BF = jnp.bfloat16
F32 = jnp.float32
MESH = pl.DeviceIdType.MESH
CHUNK = 256
LANES = 3
PREFIX_LOW = 192


def step_rates():
    base_rate = 3.5 * PARAMS**0.5 / CLIP
    return (
        base_rate * D ** (-0.5),
        base_rate * max(QW // LEN, 1) ** (-0.5),
        base_rate * D ** (-0.5),
        base_rate * FF ** (-0.5),
        base_rate * 2.0,
        base_rate * 0.3,
    )


def swap(value, axis):
    return lax.ppermute(value, axis, [(0, 1), (1, 0)])


def take_bit(value, bit, position):
    return lax.dynamic_index_in_dim(value, bit, position, keepdims=False)


def gather_blocks(block, layout, order):
    have = []
    held = block
    for axis in order:
        received = swap(held, axis)
        position = sum(layout.index(other) < layout.index(axis) for other in have)
        bit = lax.axis_index(axis)
        shape = held.shape
        joined = jnp.zeros(shape[:position] + (2,) + shape[position:], held.dtype)
        joined = lax.dynamic_update_index_in_dim(joined, held, bit, position)
        held = lax.dynamic_update_index_in_dim(joined, received, 1 - bit, position)
        have.append(axis)
    return held


def sum_blocks(terms, layout, order, last=F32, beside=None):
    left = list(layout)
    held = terms
    for axis in order:
        position = left.index(axis)
        bit = lax.axis_index(axis)
        received = swap(take_bit(held, 1 - bit, position), axis)
        if beside is not None and axis == order[1]:
            received, result = lax.optimization_barrier((received, beside(held)))
        held = take_bit(held, bit, position).astype(F32) + received.astype(F32)
        left.remove(axis)
        if left:
            held = held.astype(terms.dtype)
    return held.astype(last) if beside is None else (held.astype(last), result)


def greet(axes):
    barrier = pltpu.get_barrier_semaphore()
    for axis in axes:
        pl.semaphore_signal(
            barrier, inc=1, device_id={axis: 1 - lax.axis_index(axis)}, device_id_type=MESH
        )
    pl.semaphore_wait(barrier, len(axes))


def gather_kernel(layout, units, lanes, count, *refs):
    ins, outs = refs[:count], refs[count : 2 * count]
    own_sem, send_sem, recv_sem = refs[2 * count :]
    bits = {axis: lax.axis_index(axis) for axis in layout}
    depth = len(layout)

    def region(unit, have):
        tensor, start, size, _ = units[unit]
        blocks = tuple(pl.ds(0, 2) if axis in have else bits[axis] for axis in layout)
        return outs[tensor].at[blocks + (slice(None), pl.ds(start, size))]

    own = [
        pltpu.make_async_copy(
            ins[k], outs[k].at[tuple(bits[axis] for axis in layout)], own_sem.at[k]
        )
        for k in range(count)
    ]
    for copy in own:
        copy.start()
    greet(layout)
    for copy in own:
        copy.wait()
    copies = {}
    groups = -(-len(units) // lanes)
    for turn in range(groups + depth - 1):
        for step in reversed(range(depth)):
            first = (turn - step) * lanes
            for unit in range(max(first, 0), min(first + lanes, len(units))):
                order = units[unit][3]
                if step:
                    copies[unit, step - 1].wait_recv()
                source = region(unit, order[:step])
                copy = pltpu.make_async_remote_copy(
                    src_ref=source,
                    dst_ref=source,
                    send_sem=send_sem.at[unit, step],
                    recv_sem=recv_sem.at[unit, step],
                    device_id={order[step]: 1 - bits[order[step]]},
                    device_id_type=MESH,
                )
                copy.start()
                copies[unit, step] = copy
    for unit in range(len(units)):
        copies[unit, depth - 1].wait_recv()
    for copy in copies.values():
        copy.wait_send()


def gather_all(shards, layout, orders):
    units = []
    for tensor, shard in enumerate(shards):
        columns = shard.shape[1]
        step = -(-512 * 32 // shard.shape[0] // 128) * 128
        pieces = -(-columns // step)
        starts = [step * piece for piece in range(pieces)] + [columns]
        for piece in range(pieces):
            order = orders[len(units) % len(orders)]
            units.append((tensor, starts[piece], starts[piece + 1] - starts[piece], order))
    count = len(shards)
    semaphores = pltpu.SemaphoreType.DMA((len(units), len(layout)))
    return pl.pallas_call(
        partial(gather_kernel, layout, tuple(units), LANES, count),
        out_shape=[
            jax.ShapeDtypeStruct((2,) * len(layout) + shard.shape, shard.dtype) for shard in shards
        ],
        in_specs=[pl.BlockSpec(memory_space=pl.ANY)] * count,
        out_specs=[pl.BlockSpec(memory_space=pl.ANY)] * count,
        scratch_shapes=[pltpu.SemaphoreType.DMA((count,)), semaphores, semaphores],
        compiler_params=pltpu.CompilerParams(collective_id=0, has_side_effects=True),
        name="gather_weights",
    )(*shards)


def grad_kernel(layout, orders, bounds, chunks, counts, *refs):
    lefts, rights = refs[: counts[0]], refs[counts[0] : sum(counts)]
    out_ref = refs[sum(counts)]
    scratch = refs[sum(counts) + 1 :]
    depth = len(layout)
    lanes = len(orders)
    sends, recvs, helds = (
        [scratch[kind * lanes * depth + lane * depth :][:depth] for lane in range(lanes)]
        for kind in range(3)
    )
    given_ref, x_ref, y_ref, in_sem, send_sem, recv_sem = scratch[3 * lanes * depth :]
    bits = {axis: lax.axis_index(axis) for axis in layout}
    groups = out_ref.shape[1] // CHUNK // lanes
    tokens = y_ref.shape[0]

    copies, passed = [], 0
    for k, term in enumerate(lefts + rights):
        absent = tokens - term.shape[0]
        if k < len(lefts):
            place = given_ref.at[k]
        else:
            place = y_ref.at[:, pl.ds(passed, term.shape[1])]
            passed += term.shape[1]
        if absent:
            place[pl.ds(0, absent), :] = jnp.zeros((absent, term.shape[1]), BF)
        copy = pltpu.make_async_copy(term, place.at[pl.ds(absent, term.shape[0])], in_sem.at[k])
        copy.start()
        copies.append(copy)
    greet(layout)
    padded = x_ref.shape[2] * 2 // 2**depth

    def turned(k):
        copies[k].wait()
        rows = lefts[k].shape[1] // 2**depth
        across = given_ref[k].astype(F32).T.reshape(-1, 2, rows, tokens)
        for bit in range(2):
            blocks = across[:, bit]
            if padded > rows:
                filler = jnp.zeros((blocks.shape[0], padded - rows, tokens), F32)
                blocks = jnp.concatenate([blocks, filler], axis=1)
            x_ref[k, bit] = blocks.reshape(-1, tokens).astype(BF)
    for copy in copies[len(lefts) :]:
        copy.wait()
    turned(0)
    early = [k for k in range(1, len(lefts)) if bounds[k - 1] // lanes < k - 1]
    for k in early:
        turned(k)

    def exchange(lane, step, group):
        axis = orders[lane][step]
        slot = lax.rem(group, 2)
        return pltpu.make_async_remote_copy(
            src_ref=sends[lane][step],
            dst_ref=recvs[lane][step].at[slot],
            send_sem=send_sem.at[lane, step],
            recv_sem=recv_sem.at[lane, step, slot],
            device_id={axis: 1 - bits[axis]},
            device_id_type=MESH,
        )

    def first(lane, group):
        chunk = jnp.minimum(group * lanes + lane, chunks - 1)
        which = sum((chunk >= bound).astype(jnp.int32) for bound in bounds) if bounds else 0
        columns = y_ref[:, pl.ds(pl.multiple_of(chunk * CHUNK, CHUNK), CHUNK)]
        bit = bits[orders[lane][0]]
        given = jnp.dot(x_ref[which, 1 - bit], columns, preferred_element_type=F32)
        sends[lane][0][...] = given.astype(BF).reshape(sends[lane][0].shape)
        exchange(lane, 0, group).start()
        kept = jnp.dot(x_ref[which, bit], columns, preferred_element_type=F32)
        helds[lane][0][...] = kept.reshape(helds[lane][0].shape)

    def later(lane, step, group):
        order = orders[lane]
        slot = lax.rem(group, 2)
        exchange(lane, step - 1, group).wait()
        held, received = helds[lane][step - 1], recvs[lane][step - 1]
        if step == depth:
            chunk = group * lanes + lane
            out_ref[:, pl.ds(pl.multiple_of(chunk * CHUNK, CHUNK), CHUNK)] = held[
                ...
            ] + received[slot].astype(F32)
            return
        position = [axis for axis in layout if axis not in order[:step]].index(order[step])
        bit = bits[order[step]]

        def total(choice):
            index = (slice(None),) * position + (choice,)
            return held[index] + received[(slot,) + index].astype(F32)

        sends[lane][step][...] = total(1 - bit).astype(BF)
        exchange(lane, step, group).start()
        helds[lane][step][...] = total(bit)

    @pl.loop(0, groups + depth)
    def _(turn):
        for k in range(1, len(lefts)):
            if k not in early:
                pl.when(turn == k - 1)(partial(turned, k))
        for step in reversed(range(depth + 1)):
            group = turn - step

            @pl.when((group >= 0) & (group < groups))
            def _():
                for lane in range(lanes):
                    if step:
                        later(lane, step, group)
                    else:
                        first(lane, group)


def grad_sums(lefts, rights, layout, orders, spans, collective):
    depth, lanes = len(layout), len(orders)
    tokens, width = max(left.shape[0] for left in lefts), lefts[0].shape[1]
    rows = width // 2**depth
    padded = -(-rows // 16) * 16
    total = sum(right.shape[1] for right in rights)
    chunks = total // CHUNK
    groups = -(-chunks // lanes)
    bounds, passed = [], 0
    for span in spans[:-1]:
        passed += span // CHUNK
        bounds.append(passed)
    send_shapes, recv_shapes, held_shapes = [], [], []
    for _ in range(lanes):
        for step in range(depth):
            shape = (2,) * (depth - 1 - step) + (padded, CHUNK)
            send_shapes.append(pltpu.VMEM(shape, BF))
            recv_shapes.append(pltpu.VMEM((2,) + shape, BF))
            held_shapes.append(pltpu.VMEM(shape, F32))
    counts = (len(lefts), len(rights))
    out = pl.pallas_call(
        partial(grad_kernel, layout, orders, tuple(bounds), chunks, counts),
        out_shape=jax.ShapeDtypeStruct((padded, groups * lanes * CHUNK), F32),
        in_specs=[pl.BlockSpec(memory_space=pl.ANY)] * sum(counts),
        out_specs=pl.BlockSpec(memory_space=pltpu.VMEM),
        scratch_shapes=send_shapes
        + recv_shapes
        + held_shapes
        + [
            pltpu.VMEM((len(lefts), tokens, width), BF),
            pltpu.VMEM((len(lefts), 2, 2 ** (depth - 1) * padded, tokens), BF),
            pltpu.VMEM((tokens, total), BF),
            pltpu.SemaphoreType.DMA((sum(counts),)),
            pltpu.SemaphoreType.DMA((lanes, depth)),
            pltpu.SemaphoreType.DMA((lanes, depth, 2)),
        ],
        compiler_params=pltpu.CompilerParams(
            collective_id=collective, has_side_effects=True, vmem_limit_bytes=56 * 1024 * 1024
        ),
        name="sum_gradients",
    )(*lefts, *rights)
    return out[:rows, :total]


def total_kernel(layout, value_ref, out_ref, send_ref, recv_ref, send_sem, recv_sem):
    greet(layout)
    held = value_ref[...]
    for step, axis in enumerate(layout):
        send_ref[step] = held
        copy = pltpu.make_async_remote_copy(
            src_ref=send_ref.at[step],
            dst_ref=recv_ref.at[step],
            send_sem=send_sem.at[step],
            recv_sem=recv_sem.at[step],
            device_id={axis: 1 - lax.axis_index(axis)},
            device_id_type=MESH,
        )
        copy.start()
        copy.wait()
        held = held + recv_ref[step]
    out_ref[...] = held


def total_of(values, layout, collective):
    depth = len(layout)
    tile = jnp.broadcast_to(jnp.pad(values, (0, 8 - values.shape[0]))[:, None], (8, 128))
    sums = pl.pallas_call(
        partial(total_kernel, layout),
        out_shape=jax.ShapeDtypeStruct(tile.shape, F32),
        in_specs=[pl.BlockSpec(memory_space=pltpu.VMEM)],
        out_specs=pl.BlockSpec(memory_space=pltpu.VMEM),
        scratch_shapes=[pltpu.VMEM((depth, 8, 128), F32)] * 2
        + [pltpu.SemaphoreType.DMA((depth,))] * 2,
        compiler_params=pltpu.CompilerParams(collective_id=collective, has_side_effects=True),
        name="sum_numbers",
    )(tile)
    return sums[: values.shape[0], 0]


def rows_kernel(ids_ref, table_ref, out_ref, held_ref):
    groups = held_ref.shape[0]
    first = pl.program_id(0) * groups * 8

    def eight(group, carry):
        for k in range(8):
            place = ids_ref[first + group * 8 + k]
            held_ref[group, pl.ds(k, 1), :] = table_ref[pl.ds(place, 1), :]
        return carry

    lax.fori_loop(0, groups, eight, 0)
    out_ref[...] = held_ref[...].reshape(out_ref.shape).astype(BF)


def rows_of(table, places):
    count, width = places.shape[0], table.shape[1]
    step = 512
    return pl.pallas_call(
        rows_kernel,
        grid=(count // step,),
        out_shape=jax.ShapeDtypeStruct((count, width), BF),
        in_specs=[
            pl.BlockSpec(memory_space=pltpu.SMEM),
            pl.BlockSpec(table.shape, lambda i: (0, 0)),
        ],
        out_specs=pl.BlockSpec((step, width), lambda i: (i, 0)),
        scratch_shapes=[pltpu.VMEM((step // 8, 8, width), F32)],
        compiler_params=pltpu.CompilerParams(vmem_limit_bytes=48 * 1024 * 1024),
        cost_estimate=pl.CostEstimate(
            flops=0, bytes_accessed=80 * count * width, transcendentals=0
        ),
        name="look_up",
    )(places, table)


def mm(left, right):
    return jnp.dot(left, right, preferred_element_type=F32)


def mm_nt(left, right):
    return lax.dot_general(left, right, (((1,), (1,)), ((), ())), preferred_element_type=F32)


def mm_tn(left, right):
    return lax.dot_general(left, right, (((0,), (0,)), ((), ())), preferred_element_type=F32)


def norm_forward(stream, gain_row):
    inverse = lax.rsqrt(jnp.mean(stream * stream, axis=-1, keepdims=True) + EPS)
    return stream * inverse * gain_row


def norm_backward(stream, gain_row, grad_out):
    inverse = lax.rsqrt(jnp.mean(stream * stream, axis=-1, keepdims=True) + EPS)
    scaled = grad_out * gain_row
    d_input = inverse * scaled - stream * inverse**3 * jnp.mean(
        stream * scaled, axis=-1, keepdims=True
    )
    return (d_input, jnp.sum(grad_out * stream * inverse, axis=0))


def nt(left, right):
    return lax.dot_general(left, right, (((1,), (1,)), ((), ())), preferred_element_type=F32)


def allowed_keys(row_ref, shape, by_query, per_item):
    queries = lax.broadcasted_iota(jnp.int32, shape, by_query)
    keys = lax.broadcasted_iota(jnp.int32, shape, 1 - by_query)
    each = shape[1 - by_query] // per_item
    return row_ref[0] + queries * per_item >= lax.rem(keys, each) * per_item + keys // each


def attend_kernel(causal, row_ref, q_ref, k_ref, v_ref, o_ref):
    rows, length = q_ref.shape[0], k_ref.shape[0]
    shape = (rows, length)
    if causal:
        allowed = allowed_keys(row_ref, shape, 0, causal)
    for head in range(q_ref.shape[1] // HD):
        own = pl.ds(head * HD, HD)
        shared = pl.ds(head // (HQ // HK) * HD, HD)
        scores = nt(q_ref[:, own], k_ref[:, shared]) * HD ** (-0.5)
        if causal:
            scores = jnp.where(allowed, scores, -1000000000.0)
        expo = jnp.exp(scores - jnp.max(scores, axis=-1, keepdims=True))
        probs = expo * (1.0 / jnp.sum(expo, axis=-1, keepdims=True))
        mixed = jnp.dot(probs.astype(BF), v_ref[:, shared], preferred_element_type=F32)
        o_ref[:, own] = mixed.astype(BF)


def attend_back_kernel(causal, row_ref, q_ref, k_ref, v_ref, d_ref, dq_ref, dk_ref, dv_ref):
    rows, length = q_ref.shape[0], k_ref.shape[0]
    shape = (length, rows)
    share = HQ // HK
    if causal:
        allowed = allowed_keys(row_ref, shape, 1, causal)
    for pair in range(k_ref.shape[1] // HD):
        shared = pl.ds(pair * HD, HD)
        keys, values = k_ref[:, shared], v_ref[:, shared]
        d_keys = d_values = None
        for head in range(pair * share, (pair + 1) * share):
            own = pl.ds(head * HD, HD)
            queries, d_mixed = q_ref[:, own], d_ref[:, own]
            scores = nt(keys, queries) * HD ** (-0.5)
            if causal:
                scores = jnp.where(allowed, scores, -1000000000.0)
            expo = jnp.exp(scores - jnp.max(scores, axis=0, keepdims=True))
            probs = expo * (1.0 / jnp.sum(expo, axis=0, keepdims=True))
            d_probs = nt(values, d_mixed)
            mean = jnp.sum(probs * d_probs, axis=0, keepdims=True)
            d_scores = (probs * (d_probs - mean)).astype(BF)
            key_term = jnp.dot(d_scores, queries, preferred_element_type=F32)
            value_term = jnp.dot(probs.astype(BF), d_mixed, preferred_element_type=F32)
            d_keys = key_term if d_keys is None else d_keys + key_term
            d_values = value_term if d_values is None else d_values + value_term
            d_queries = lax.dot_general(
                keys, d_scores, (((0,), (0,)), ((), ())), preferred_element_type=F32
            )
            dq_ref[:, own] = (d_queries.T * HD ** (-0.5)).astype(BF)
        dk_ref[:, shared] = (d_keys * HD ** (-0.5)).astype(BF)
        dv_ref[:, shared] = d_values.astype(BF)


def attend_specs(rows, length):
    wide = 128 * (HQ // HK)
    queries = pl.BlockSpec((rows, wide), lambda i: (0, i))
    keys = pl.BlockSpec((length, 128), lambda i: (0, i))
    values = pl.BlockSpec((length, 128), lambda i: (0, i + KW // 128))
    return queries, keys, values


def attend_forward(queries, keyvals, first_row, per_item):
    rows, length = queries.shape[0], keyvals.shape[0]
    by_query, by_key, by_value = attend_specs(rows, length)
    return pl.pallas_call(
        partial(attend_kernel, 0 if first_row is None else per_item),
        grid=(KW // 128,),
        out_shape=jax.ShapeDtypeStruct(queries.shape, BF),
        in_specs=[pl.BlockSpec(memory_space=pltpu.SMEM), by_query, by_key, by_value],
        out_specs=by_query,
        compiler_params=pltpu.CompilerParams(vmem_limit_bytes=56 * 1024 * 1024),
        cost_estimate=pl.CostEstimate(
            flops=4 * rows * length * QW,
            bytes_accessed=4 * rows * QW + 4 * length * KW,
            transcendentals=HQ * rows * length,
        ),
        name="attend",
    )(jnp.reshape(0 if first_row is None else first_row, (1,)), queries, keyvals, keyvals)


def attend_backward(queries, keyvals, first_row, per_item, d_mixed):
    rows, length = queries.shape[0], keyvals.shape[0]
    by_query, by_key, by_value = attend_specs(rows, length)
    d_queries, d_keys, d_values = pl.pallas_call(
        partial(attend_back_kernel, 0 if first_row is None else per_item),
        grid=(KW // 128,),
        out_shape=[
            jax.ShapeDtypeStruct(queries.shape, BF),
            jax.ShapeDtypeStruct((length, KW), BF),
            jax.ShapeDtypeStruct((length, KW), BF),
        ],
        in_specs=[pl.BlockSpec(memory_space=pltpu.SMEM), by_query, by_key, by_value, by_query],
        out_specs=[by_query, by_key, by_key],
        compiler_params=pltpu.CompilerParams(vmem_limit_bytes=56 * 1024 * 1024),
        cost_estimate=pl.CostEstimate(
            flops=10 * rows * length * QW,
            bytes_accessed=6 * rows * QW + 8 * length * KW,
            transcendentals=HQ * rows * length,
        ),
        name="attend_back",
    )(jnp.reshape(0 if first_row is None else first_row, (1,)), queries, keyvals, keyvals, d_mixed)
    return (d_queries, jnp.concatenate([d_keys, d_values], axis=1))


def update(weight, gradient, moment, average, rate, factor):
    clipped = gradient * factor
    moment_new = MOMENTUM * moment + (1 - MOMENTUM) * clipped
    weight_new = weight - rate * ((1 - MOMENTUM) * clipped + MOMENTUM * moment_new)
    average_new = AVERAGE * average + (1 - AVERAGE) * weight_new
    return (weight_new, moment_new, average_new)


def on_device(
    dp_axes,
    mp_axes,
    source_ids,
    target_ids,
    prefix,
    attn_in,
    attn_out,
    ff_in,
    ff_out,
    table,
    gains,
    attn_in_mom,
    attn_out_mom,
    ff_in_mom,
    ff_out_mom,
    table_mom,
    gains_mom,
    attn_in_avg,
    attn_out_avg,
    ff_in_avg,
    ff_out_avg,
    table_avg,
    gains_avg,
):
    every = dp_axes + mp_axes
    core = mp_axes[-1]
    row_axes = mp_axes[1:]
    line = mp_axes[:-1]
    gather_orders = (
        line + dp_axes + (core,),
        line + dp_axes[::-1] + (core,),
        dp_axes + line + (core,),
    )
    sum_orders = tuple(order[::-1] for order in gather_orders)
    last = (line[-1], core)
    three = (gather_orders[0], gather_orders[1], line[:-1] + dp_axes[::-1] + last)
    six_orders = three + three[:2] + (line[:-1] + dp_axes + last,)
    two_dp, two_mp, two_rows = (2,) * len(dp_axes), (2,) * len(mp_axes), (2,) * len(row_axes)

    seq_count, length = source_ids.shape
    rows = length // 2 ** len(row_axes)
    per_item = 2 ** len(row_axes)
    skip = PREFIX_LOW // per_item
    first_row = lax.axis_index(row_axes)

    def by_device(values):
        return values.reshape(values.shape[:-1] + (rows, per_item)).swapaxes(-1, -2)

    def with_skipped(values):
        return jnp.pad(values, ((rows - values.shape[0], 0), (0, 0)))


    vocab_part = table.shape[0]
    offset = lax.axis_index(mp_axes) * vocab_part
    table_bf = table.astype(BF)
    decoder_ids = jnp.concatenate(
        [jnp.zeros((seq_count, 1), jnp.int32), target_ids[:, :-1]], axis=1
    )
    ids_all = by_device(gather_blocks(jnp.stack([source_ids, decoder_ids]), dp_axes, dp_axes))
    ids_all = ids_all.reshape(-1, 2, 2 ** len(mp_axes), rows).transpose(1, 2, 0, 3).reshape(2, -1)
    table_rows = lax.all_gather(table_bf, dp_axes, axis=1, tiled=True)
    local_ids = ids_all - offset
    inside = (local_ids >= 0) & (local_ids < vocab_part)

    def trade(parts):
        for position, axis in enumerate(dp_axes):
            bit = lax.axis_index(axis)
            received = swap(take_bit(parts, 1 - bit, position), axis)
            kept = take_bit(parts, bit, position)
            parts = jnp.stack(
                [jnp.where(bit == 0, kept, received), jnp.where(bit == 0, received, kept)],
                axis=position,
            )
        return parts

    table_zero = jnp.pad(table, ((0, 8), (0, 0)))
    places = jnp.where(inside, local_ids, vocab_part)

    def look_up(which):
        found = rows_of(table_zero, places[which])
        return found.reshape(2 ** len(mp_axes), -1, found.shape[-1])

    def collect(found):
        return lax.psum_scatter(found, mp_axes, scatter_dimension=0)

    def embed(mine):
        width = mine.shape[-1]
        parts = trade(mine.reshape(two_dp + (rows, width))).reshape(-1, rows, width)
        return jnp.moveaxis(parts, 0, 1).reshape(rows, -1).astype(F32)

    found_e = look_up(0)
    mine_e = collect(found_e)
    found_d = look_up(1)
    mine_d = collect(found_d)

    shards = [attn_in[0], attn_out[0], ff_in[0], ff_out[0]]
    shards += [attn_in[1], attn_out[1], attn_in[2], attn_out[2], ff_in[1], ff_out[1]]
    shards = [shard.astype(BF) for shard in shards]
    in_kernels = attn_in.shape[1] % 16 == 0
    if in_kernels:
        *shards, found_e, found_d, table_rows = lax.optimization_barrier(
            shards + [found_e, found_d, table_rows]
        )
        behind = (8, 9,)
        full = [None] * len(shards)
        ahead = [k for k in range(len(shards)) if k not in behind]
        for k, got in zip(ahead, gather_all([shards[k] for k in ahead], every, six_orders)):
            full[k] = got
        full[0], mine_e, mine_d = lax.optimization_barrier((full[0], mine_e, mine_d))
        full[0], *sent = lax.optimization_barrier([full[0]] + [shards[k] for k in behind])
        for k, shard in zip(behind, sent):
            full[k] = lax.all_gather(shard, every, axis=0, tiled=True)
    else:
        full = [
            gather_blocks(shard, every, gather_orders[k % 3]) for k, shard in enumerate(shards)
        ]
    full = [got.reshape((-1,) + shard.shape[1:]) for got, shard in zip(full, shards)]
    a_in, a_out = (full[0], full[4], full[6]), (full[1], full[5], full[7])
    f_in, f_out = (full[2], full[8]), (full[3], full[9])
    gain_all = gather_blocks(gains.astype(BF).T, every, gather_orders[0])
    gain_all = gain_all.reshape(-1, gains.shape[0]).T.astype(F32)

    def spread_keys(own):
        return gather_blocks(own, row_axes, row_axes).reshape(length, -1)

    def attention_forward(stream, source, block, gain_row, start):
        normed = norm_forward(stream, gain_row).astype(BF)
        anchor = normed if source is None else source
        keyvals = spread_keys(mm(anchor, a_in[block][:, QW:]).astype(BF))
        first = 0 if start is None else skip
        queries = mm(normed[first:], a_in[block][:, :QW]).astype(BF)
        position = None if start is None else start + first * per_item
        mixed = attend_forward(queries, keyvals, position, per_item)
        out = stream[first:] + mm(mixed, a_out[block])
        return (out, (stream, normed, anchor, queries, keyvals, mixed))

    def ffn_forward(stream, which, gain_row):
        normed = norm_forward(stream, gain_row).astype(BF)
        both = mm(normed, f_in[which])
        hidden_act = (jax.nn.gelu(both[:, :FF], approximate=True) * both[:, FF:]).astype(BF)
        return (stream + mm(hidden_act, f_out[which]), (stream, normed, both, hidden_act))

    stream_e = embed(mine_e)
    stream_e, enc_attn = attention_forward(stream_e, None, 0, gain_all[0], None)
    stream_e, mine_d = lax.optimization_barrier((stream_e, mine_d))
    stream_d = embed(mine_d)
    stream_d, dec_self = attention_forward(stream_d, None, 1, gain_all[3], first_row)
    stream_e, enc_ffn = ffn_forward(stream_e, 0, gain_all[1])
    encoded = norm_forward(stream_e, gain_all[2]).astype(BF)
    stream_d, dec_cross = attention_forward(stream_d, encoded, 2, gain_all[4], None)
    stream_d, dec_ffn = ffn_forward(stream_d, 1, gain_all[5])
    hidden = norm_forward(stream_d, gain_all[6]).astype(BF)

    hidden_all = gather_blocks(hidden, mp_axes, mp_axes).reshape(-1, hidden.shape[-1])
    targets = by_device(target_ids)[..., skip:].reshape(-1)
    vocab_ids = offset + jnp.arange(vocab_part)
    hits = vocab_ids[None, :] == targets[:, None]
    logits = mm_nt(hidden_all, table_rows) * D ** (-0.5)
    own_max = jnp.max(logits, axis=-1)
    expo = jnp.exp(logits - own_max[:, None])
    stats = jnp.stack(
        [own_max, jnp.sum(expo, axis=-1), jnp.sum(jnp.where(hits, logits, 0.0), axis=-1)]
    )
    expo = expo.astype(BF)
    for axis in mp_axes[::-1]:
        other = swap(stats, axis)
        joint = jnp.maximum(stats[0], other[0])
        stats = jnp.stack(
            [
                joint,
                stats[1] * jnp.exp(stats[0] - joint) + other[1] * jnp.exp(other[0] - joint),
                stats[2] + other[2],
            ]
        )
    log_norm = stats[0] + jnp.log(stats[1])
    prefix_group = lax.dynamic_slice_in_dim(prefix, lax.axis_index(dp_axes) * seq_count, seq_count)
    positions = by_device(jnp.arange(length))[..., skip:].reshape(1, -1)
    scored = (positions >= prefix_group[:, None]).astype(F32).reshape(-1)
    scored_count = jnp.sum((length - prefix).astype(F32))
    scale = jnp.exp(own_max - log_norm)
    d_logits = (
        (expo.astype(F32) * scale[:, None] - hits.astype(F32)) * (scored / scored_count)[:, None]
    ).astype(BF)
    d_final = (mm(d_logits, table_rows) * D ** (-0.5)).astype(BF)

    def table_term(held):
        _, rows_all = lax.optimization_barrier((held, hidden_all))
        return (mm_tn(d_logits, rows_all) * D ** (-0.5)).astype(BF)

    d_final, head_table = sum_blocks(
        d_final.reshape(two_mp + hidden.shape), mp_axes, mp_axes[::-1], F32, table_term
    )

    grad_table = lax.psum_scatter(head_table, dp_axes, scatter_dimension=1, tiled=True)

    def ffn_backward(saved, which, gain_row, d_stream):
        stream, normed, both, hidden_act = saved
        up_part = both[:, FF:]
        activated, gelu_pull = jax.vjp(partial(jax.nn.gelu, approximate=True), both[:, :FF])
        d_branch = d_stream.astype(BF)
        d_hidden = mm_nt(d_branch, f_out[which])
        d_both = jnp.concatenate(
            [gelu_pull(d_hidden * up_part)[0].astype(BF), (d_hidden * activated).astype(BF)], axis=1
        )
        d_normed = mm_nt(d_both, f_in[which])
        d_input, grad_gain = norm_backward(stream, gain_row, d_normed)
        return (d_stream + d_input, (normed, d_both, hidden_act, d_branch), grad_gain)

    def attention_backward(saved, cross, block, gain_row, start, d_stream):
        stream, normed, anchor, queries, keyvals, mixed = saved
        d_branch = d_stream.astype(BF)
        d_mixed = mm_nt(d_branch, a_out[block]).astype(BF)
        queries = with_skipped(queries)
        d_queries, d_keyvals = attend_backward(
            queries, keyvals, start, per_item, with_skipped(d_mixed)
        )
        d_keyvals = sum_blocks(
            d_keyvals.reshape(two_rows + (rows, -1)), row_axes, row_axes[::-1], BF
        )
        d_queries = d_queries[rows - stream.shape[0] :]
        d_normed = mm_nt(d_queries, a_in[block][:, :QW])
        d_anchor = mm_nt(d_keyvals, a_in[block][:, QW:])
        if not cross:
            d_normed = d_normed + d_anchor
        factors = (normed, anchor, d_queries, d_keyvals, mixed, d_branch)
        d_input, grad_gain = norm_backward(stream, gain_row, d_normed)
        if start is not None:
            d_stream = with_skipped(d_stream)
        return (d_stream + d_input, d_anchor, factors, grad_gain)

    d_y, gain6 = norm_backward(stream_d, gain_all[6], d_final)
    d_y, ffn_factors1, gain5 = ffn_backward(dec_ffn, 1, gain_all[5], d_y)
    d_y, d_encoded, attn_factors2, gain4 = attention_backward(
        dec_cross, True, 2, gain_all[4], None, d_y
    )
    d_y, _, attn_factors1, gain3 = attention_backward(
        dec_self, False, 1, gain_all[3], first_row, d_y
    )
    d_encoded, grad_table = lax.optimization_barrier((d_encoded, grad_table))
    d_x, gain2 = norm_backward(stream_e, gain_all[2], d_encoded)
    d_x, ffn_factors0, gain1 = ffn_backward(enc_ffn, 0, gain_all[1], d_x)
    d_x, _, attn_factors0, gain0 = attention_backward(
        enc_attn, False, 0, gain_all[0], None, d_x
    )

    def trade_rows(d_rows):
        width = table.shape[1]
        parts = jnp.moveaxis(d_rows.astype(BF).reshape(rows, -1, width), 1, 0)
        return trade(parts.reshape(two_dp + (rows, width))).reshape(-1, width)

    def look_back(which, spread):
        places = (local_ids[which][None, :] == jnp.arange(vocab_part)[:, None]).astype(BF)
        return mm(places, spread.reshape(-1, spread.shape[-1]))

    traded_y, traded_x = trade_rows(d_y), trade_rows(d_x)
    spread_y, spread_x = (lax.all_gather(traded, mp_axes) for traded in (traded_y, traded_x))

    gain_grads = jnp.stack([gain0, gain1, gain2, gain3, gain4, gain5, gain6])
    gain_blocks = jnp.moveaxis(gain_grads.reshape(gains.shape[0], -1, gains.shape[1]), 1, 0)
    grad_gains = sum_blocks(
        gain_blocks.reshape((2,) * len(every) + gains.shape), every, sum_orders[0]
    )

    if in_kernels:
        traded_x, ffn_left, attn_left = lax.optimization_barrier(
            (traded_x, ffn_factors0[2], attn_factors0[0])
        )
        attn_factors0 = (attn_left, attn_left) + attn_factors0[2:]
        ffn_factors0 = ffn_factors0[:2] + (ffn_left,) + ffn_factors0[3:]
    lefts, rights, spans = [], [], []
    for normed, anchor, d_queries, d_keyvals, mixed, d_branch in (
        attn_factors0,
        attn_factors1,
        attn_factors2,
    ):
        lefts += [normed, mixed] if anchor is normed else [normed, anchor, mixed]
        rights += [d_queries, d_keyvals, d_branch]
        widths = [d_queries.shape[1], d_keyvals.shape[1]]
        spans += ([sum(widths)] if anchor is normed else widths) + [d_branch.shape[1]]
    wide_lefts, wide_rights = [], []
    for normed, d_both, hidden_act, d_branch in (ffn_factors0, ffn_factors1):
        lefts.append(normed)
        rights.append(d_both)
        spans.append(d_both.shape[1])
        wide_lefts.append(hidden_act)
        wide_rights.append(d_branch)
    wide_spans = [right.shape[1] for right in wide_rights]
    if in_kernels:
        back_orders = tuple(order[::-1] for order in three)
        own = grad_sums(lefts, rights, every, back_orders, spans, 1)
        wide = grad_sums(wide_lefts, wide_rights, every, back_orders[:2], wide_spans, 2)
        own, wide, spread_x, spread_y = lax.optimization_barrier((own, wide, spread_x, spread_y))
    else:

        def own_sum(left, right, kind):
            product = mm_tn(left, right).astype(BF)
            blocks = product.reshape((2,) * len(every) + (-1,) + product.shape[1:])
            return sum_blocks(blocks, every, sum_orders[kind % 3])

        everything = jnp.concatenate([with_skipped(right) for right in rights], axis=1)
        ends = [sum(spans[: k + 1]) for k in range(len(spans))]
        parts = jnp.split(everything, ends[:-1], axis=1)
        pairs = list(enumerate(zip([with_skipped(left) for left in lefts], parts)))
        own = jnp.concatenate([own_sum(*pair, k) for k, pair in pairs], axis=1)
        pairs = list(enumerate(zip(wide_lefts, wide_rights)))
        wide = jnp.concatenate([own_sum(*pair, k) for k, pair in pairs], axis=1)
    grad_table = grad_table.astype(F32) + look_back(1, spread_y) + look_back(0, spread_x)
    ends = (attn_in.shape[2], attn_in.shape[2] + attn_out.shape[2])
    ffn_from = 3 * ends[1]
    gradients = (
        jnp.stack([own[:, ends[1] * k : ends[1] * k + ends[0]] for k in range(3)]),
        jnp.stack([own[:, ends[1] * k + ends[0] : ends[1] * (k + 1)] for k in range(3)]),
        jnp.stack([own[:, ffn_from + 2 * FF * k : ffn_from + 2 * FF * (k + 1)] for k in range(2)]),
        jnp.stack(jnp.split(wide, 2, axis=1)),
        grad_table,
        grad_gains,
    )

    own_losses = ((log_norm - stats[2]) * scored).reshape(2 ** len(mp_axes), -1)
    loss_part = jnp.sum(take_bit(own_losses, lax.axis_index(mp_axes), 0))
    squares = sum((jnp.sum(gradient * gradient) for gradient in gradients))
    totals = jnp.stack([loss_part, squares])
    totals = total_of(totals, every[::-1], 3)
    loss_sum = totals[0]
    grad_norm = jnp.sqrt(totals[1])
    factor = jnp.minimum(1.0, CLIP / grad_norm)
    weights = (attn_in, attn_out, ff_in, ff_out, table, gains)
    moments = (attn_in_mom, attn_out_mom, ff_in_mom, ff_out_mom, table_mom, gains_mom)
    averages = (attn_in_avg, attn_out_avg, ff_in_avg, ff_out_avg, table_avg, gains_avg)
    results = [
        update(weight, gradient, moment, average, rate, factor)
        for weight, gradient, moment, average, rate in zip(
            weights, gradients, moments, averages, step_rates()
        )
    ]
    return (loss_sum, scored_count, grad_norm) + tuple(
        results[array][kind] for kind in range(3) for array in range(6)
    )


def solution(mesh):
    dp_count, mp_count = mesh.shape["dp"], mesh.shape["mp"]
    dp_axes = tuple(f"d{k}" for k in range(dp_count.bit_length() - 1))
    mp_axes = tuple(f"m{k}" for k in range(mp_count.bit_length() - 1))
    every = dp_axes + mp_axes
    fine = Mesh(mesh.devices.reshape((2,) * len(every)), every)
    rows_split = P(None, every, None)
    params = (rows_split,) * 4 + (P(mp_axes, dp_axes), P(None, every))
    in_specs = (P(dp_axes, None), P(dp_axes, None), P()) + params * 3
    out_specs = (P(), P(), P()) + params * 3
    return jax.shard_map(
        partial(on_device, dp_axes, mp_axes),
        mesh=fine,
        in_specs=in_specs,
        out_specs=out_specs,
        check_vma=False,
    )
```

```python
from functools import partial

import jax
import jax.numpy as jnp
from jax import lax
from jax.experimental import pallas as pl
from jax.experimental.pallas import tpu as pltpu
from jax.sharding import Mesh
from jax.sharding import PartitionSpec as P

D = 1024
HQ = 16
HK = 8
HD = 64
FF = 2816
LEN = 1024
QW = 1024
KW = 512
PARAMS = 59644928

MOMENTUM = 0.9
AVERAGE = 0.9
CLIP = 0.0002
EPS = 1e-06

BF = jnp.bfloat16
F32 = jnp.float32
MESH = pl.DeviceIdType.MESH
CHUNK = 256
LANES = 3
PREFIX_LOW = 192


def step_rates():
    base_rate = 3.5 * PARAMS**0.5 / CLIP
    return (
        base_rate * D ** (-0.5),
        base_rate * max(QW // LEN, 1) ** (-0.5),
        base_rate * D ** (-0.5),
        base_rate * FF ** (-0.5),
        base_rate * 2.0,
        base_rate * 0.3,
    )


def swap(value, axis):
    return lax.ppermute(value, axis, [(0, 1), (1, 0)])


def take_bit(value, bit, position):
    return lax.dynamic_index_in_dim(value, bit, position, keepdims=False)


def gather_blocks(block, layout, order):
    have = []
    held = block
    for axis in order:
        received = swap(held, axis)
        position = sum(layout.index(other) < layout.index(axis) for other in have)
        bit = lax.axis_index(axis)
        shape = held.shape
        joined = jnp.zeros(shape[:position] + (2,) + shape[position:], held.dtype)
        joined = lax.dynamic_update_index_in_dim(joined, held, bit, position)
        held = lax.dynamic_update_index_in_dim(joined, received, 1 - bit, position)
        have.append(axis)
    return held


def sum_blocks(terms, layout, order, last=F32, beside=None):
    left = list(layout)
    held = terms
    for axis in order:
        position = left.index(axis)
        bit = lax.axis_index(axis)
        received = swap(take_bit(held, 1 - bit, position), axis)
        if beside is not None and axis == order[1]:
            received, result = lax.optimization_barrier((received, beside(held)))
        held = take_bit(held, bit, position).astype(F32) + received.astype(F32)
        left.remove(axis)
        if left:
            held = held.astype(terms.dtype)
    return held.astype(last) if beside is None else (held.astype(last), result)


def greet(axes):
    barrier = pltpu.get_barrier_semaphore()
    for axis in axes:
        pl.semaphore_signal(
            barrier, inc=1, device_id={axis: 1 - lax.axis_index(axis)}, device_id_type=MESH
        )
    pl.semaphore_wait(barrier, len(axes))


def gather_kernel(layout, units, lanes, count, *refs):
    ins, outs = refs[:count], refs[count : 2 * count]
    own_sem, send_sem, recv_sem = refs[2 * count :]
    bits = {axis: lax.axis_index(axis) for axis in layout}
    depth = len(layout)

    def region(unit, have):
        tensor, start, size, _ = units[unit]
        blocks = tuple(pl.ds(0, 2) if axis in have else bits[axis] for axis in layout)
        return outs[tensor].at[blocks + (slice(None), pl.ds(start, size))]

    own = [
        pltpu.make_async_copy(
            ins[k], outs[k].at[tuple(bits[axis] for axis in layout)], own_sem.at[k]
        )
        for k in range(count)
    ]
    for copy in own:
        copy.start()
    greet(layout)
    for copy in own:
        copy.wait()
    copies = {}
    groups = -(-len(units) // lanes)
    for turn in range(groups + depth - 1):
        for step in reversed(range(depth)):
            first = (turn - step) * lanes
            for unit in range(max(first, 0), min(first + lanes, len(units))):
                order = units[unit][3]
                if step:
                    copies[unit, step - 1].wait_recv()
                source = region(unit, order[:step])
                copy = pltpu.make_async_remote_copy(
                    src_ref=source,
                    dst_ref=source,
                    send_sem=send_sem.at[unit, step],
                    recv_sem=recv_sem.at[unit, step],
                    device_id={order[step]: 1 - bits[order[step]]},
                    device_id_type=MESH,
                )
                copy.start()
                copies[unit, step] = copy
    for unit in range(len(units)):
        copies[unit, depth - 1].wait_recv()
    for copy in copies.values():
        copy.wait_send()


def gather_all(shards, layout, orders):
    units = []
    for tensor, shard in enumerate(shards):
        columns = shard.shape[1]
        step = -(-512 * 32 // shard.shape[0] // 128) * 128
        pieces = -(-columns // step)
        starts = [step * piece for piece in range(pieces)] + [columns]
        for piece in range(pieces):
            order = orders[len(units) % len(orders)]
            units.append((tensor, starts[piece], starts[piece + 1] - starts[piece], order))
    count = len(shards)
    semaphores = pltpu.SemaphoreType.DMA((len(units), len(layout)))
    return pl.pallas_call(
        partial(gather_kernel, layout, tuple(units), LANES, count),
        out_shape=[
            jax.ShapeDtypeStruct((2,) * len(layout) + shard.shape, shard.dtype) for shard in shards
        ],
        in_specs=[pl.BlockSpec(memory_space=pl.ANY)] * count,
        out_specs=[pl.BlockSpec(memory_space=pl.ANY)] * count,
        scratch_shapes=[pltpu.SemaphoreType.DMA((count,)), semaphores, semaphores],
        compiler_params=pltpu.CompilerParams(collective_id=0, has_side_effects=True),
        name="gather_weights",
    )(*shards)


def grad_kernel(layout, orders, bounds, chunks, counts, chunk_width, *refs):
    lefts, rights = refs[: counts[0]], refs[counts[0] : sum(counts)]
    out_ref = refs[sum(counts)]
    scratch = refs[sum(counts) + 1 :]
    depth = len(layout)
    lanes = len(orders)
    sends, recvs, helds = (
        [scratch[kind * lanes * depth + lane * depth :][:depth] for lane in range(lanes)]
        for kind in range(3)
    )
    given_ref, x_ref, y_ref, in_sem, send_sem, recv_sem = scratch[3 * lanes * depth :]
    bits = {axis: lax.axis_index(axis) for axis in layout}
    groups = out_ref.shape[1] // chunk_width // lanes
    tokens = y_ref.shape[0]

    copies, passed = [], 0
    for k, term in enumerate(lefts + rights):
        absent = tokens - term.shape[0]
        if k < len(lefts):
            place = given_ref.at[k]
        else:
            place = y_ref.at[:, pl.ds(passed, term.shape[1])]
            passed += term.shape[1]
        if absent:
            place[pl.ds(0, absent), :] = jnp.zeros((absent, term.shape[1]), BF)
        copy = pltpu.make_async_copy(term, place.at[pl.ds(absent, term.shape[0])], in_sem.at[k])
        copy.start()
        copies.append(copy)
    greet(layout)
    padded = x_ref.shape[2] * 2 // 2**depth

    def turned(k):
        copies[k].wait()
        rows = lefts[k].shape[1] // 2**depth
        across = given_ref[k].astype(F32).T.reshape(-1, 2, rows, tokens)
        for bit in range(2):
            blocks = across[:, bit]
            if padded > rows:
                filler = jnp.zeros((blocks.shape[0], padded - rows, tokens), F32)
                blocks = jnp.concatenate([blocks, filler], axis=1)
            x_ref[k, bit] = blocks.reshape(-1, tokens).astype(BF)
    for copy in copies[len(lefts) :]:
        copy.wait()
    turned(0)
    early = [k for k in range(1, len(lefts)) if bounds[k - 1] // lanes < k - 1]
    for k in early:
        turned(k)

    def exchange(lane, step, group):
        axis = orders[lane][step]
        slot = lax.rem(group, 2)
        return pltpu.make_async_remote_copy(
            src_ref=sends[lane][step],
            dst_ref=recvs[lane][step].at[slot],
            send_sem=send_sem.at[lane, step],
            recv_sem=recv_sem.at[lane, step, slot],
            device_id={axis: 1 - bits[axis]},
            device_id_type=MESH,
        )

    def first(lane, group):
        chunk = jnp.minimum(group * lanes + lane, chunks - 1)
        which = sum((chunk >= bound).astype(jnp.int32) for bound in bounds) if bounds else 0
        columns = y_ref[:, pl.ds(pl.multiple_of(chunk * chunk_width, chunk_width), chunk_width)]
        bit = bits[orders[lane][0]]
        given = jnp.dot(x_ref[which, 1 - bit], columns, preferred_element_type=F32)
        sends[lane][0][...] = given.astype(BF).reshape(sends[lane][0].shape)
        exchange(lane, 0, group).start()
        kept = jnp.dot(x_ref[which, bit], columns, preferred_element_type=F32)
        helds[lane][0][...] = kept.reshape(helds[lane][0].shape)

    def later(lane, step, group):
        order = orders[lane]
        slot = lax.rem(group, 2)
        exchange(lane, step - 1, group).wait()
        held, received = helds[lane][step - 1], recvs[lane][step - 1]
        if step == depth:
            chunk = group * lanes + lane
            out_ref[:, pl.ds(pl.multiple_of(chunk * chunk_width, chunk_width), chunk_width)] = held[
                ...
            ] + received[slot].astype(F32)
            return
        position = [axis for axis in layout if axis not in order[:step]].index(order[step])
        bit = bits[order[step]]

        def total(choice):
            index = (slice(None),) * position + (choice,)
            return held[index] + received[(slot,) + index].astype(F32)

        sends[lane][step][...] = total(1 - bit).astype(BF)
        exchange(lane, step, group).start()
        helds[lane][step][...] = total(bit)

    @pl.loop(0, groups + depth)
    def _(turn):
        for k in range(1, len(lefts)):
            if k not in early:
                pl.when(turn == k - 1)(partial(turned, k))
        for step in reversed(range(depth + 1)):
            group = turn - step

            @pl.when((group >= 0) & (group < groups))
            def _():
                for lane in range(lanes):
                    if step:
                        later(lane, step, group)
                    else:
                        first(lane, group)


def grad_sums(lefts, rights, layout, orders, spans, collective, chunk_width=CHUNK):
    depth, lanes = len(layout), len(orders)
    tokens, width = max(left.shape[0] for left in lefts), lefts[0].shape[1]
    rows = width // 2**depth
    padded = -(-rows // 16) * 16
    total = sum(right.shape[1] for right in rights)
    chunks = total // chunk_width
    groups = -(-chunks // lanes)
    bounds, passed = [], 0
    for span in spans[:-1]:
        passed += span // chunk_width
        bounds.append(passed)
    send_shapes, recv_shapes, held_shapes = [], [], []
    for _ in range(lanes):
        for step in range(depth):
            shape = (2,) * (depth - 1 - step) + (padded, chunk_width)
            send_shapes.append(pltpu.VMEM(shape, BF))
            recv_shapes.append(pltpu.VMEM((2,) + shape, BF))
            held_shapes.append(pltpu.VMEM(shape, F32))
    counts = (len(lefts), len(rights))
    out = pl.pallas_call(
        partial(grad_kernel, layout, orders, tuple(bounds), chunks, counts, chunk_width),
        out_shape=jax.ShapeDtypeStruct((padded, groups * lanes * chunk_width), F32),
        in_specs=[pl.BlockSpec(memory_space=pl.ANY)] * sum(counts),
        out_specs=pl.BlockSpec(memory_space=pltpu.VMEM),
        scratch_shapes=send_shapes
        + recv_shapes
        + held_shapes
        + [
            pltpu.VMEM((len(lefts), tokens, width), BF),
            pltpu.VMEM((len(lefts), 2, 2 ** (depth - 1) * padded, tokens), BF),
            pltpu.VMEM((tokens, total), BF),
            pltpu.SemaphoreType.DMA((sum(counts),)),
            pltpu.SemaphoreType.DMA((lanes, depth)),
            pltpu.SemaphoreType.DMA((lanes, depth, 2)),
        ],
        compiler_params=pltpu.CompilerParams(
            collective_id=collective, has_side_effects=True, vmem_limit_bytes=56 * 1024 * 1024
        ),
        name="sum_gradients",
    )(*lefts, *rights)
    return out[:rows, :total]


def greet_rounds(rounds):
    barrier = pltpu.get_barrier_semaphore()
    for partners in rounds:
        for axes in partners:
            other = {axis: 1 - lax.axis_index(axis) for axis in axes}
            pl.semaphore_signal(barrier, inc=1, device_id=other, device_id_type=MESH)
    pl.semaphore_wait(barrier, sum(len(partners) for partners in rounds))


def total_kernel(rounds, value_ref, out_ref, send_ref, recv_ref, send_sem, recv_sem):
    greet_rounds(rounds)
    held = value_ref[...]
    for step, partners in enumerate(rounds):
        send_ref[step] = held
        copies = []
        for k, axes in enumerate(partners):
            copy = pltpu.make_async_remote_copy(
                src_ref=send_ref.at[step],
                dst_ref=recv_ref.at[step, k],
                send_sem=send_sem.at[step, k],
                recv_sem=recv_sem.at[step, k],
                device_id={axis: 1 - lax.axis_index(axis) for axis in axes},
                device_id_type=MESH,
            )
            copy.start()
            copies.append(copy)
        for copy in copies:
            copy.wait()
        held = held + recv_ref[step, 0]
        if len(partners) > 1:
            held = held + (recv_ref[step, 1] + recv_ref[step, 2])
    out_ref[...] = held


def total_of(values, layout, collective):
    pairs = [layout[k : k + 2] for k in range(0, len(layout), 2)]
    rounds = tuple(
        ((pair[0],),) if len(pair) == 1 else ((pair[0],), (pair[1],), pair) for pair in pairs
    )
    depth = len(rounds)
    tile = jnp.broadcast_to(jnp.pad(values, (0, 8 - values.shape[0]))[:, None], (8, 128))
    sums = pl.pallas_call(
        partial(total_kernel, rounds),
        out_shape=jax.ShapeDtypeStruct(tile.shape, F32),
        in_specs=[pl.BlockSpec(memory_space=pltpu.VMEM)],
        out_specs=pl.BlockSpec(memory_space=pltpu.VMEM),
        scratch_shapes=[
            pltpu.VMEM((depth, 8, 128), F32),
            pltpu.VMEM((depth, 3, 8, 128), F32),
            pltpu.SemaphoreType.DMA((depth, 3)),
            pltpu.SemaphoreType.DMA((depth, 3)),
        ],
        compiler_params=pltpu.CompilerParams(collective_id=collective, has_side_effects=True),
        name="sum_numbers",
    )(tile)
    return sums[: values.shape[0], 0]


def rows_kernel(ids_ref, table_ref, out_ref, held_ref):
    groups = held_ref.shape[0]
    first = pl.program_id(0) * groups * 8

    def eight(group, carry):
        for k in range(8):
            place = ids_ref[first + group * 8 + k]
            held_ref[group, pl.ds(k, 1), :] = table_ref[pl.ds(place, 1), :]
        return carry

    lax.fori_loop(0, groups, eight, 0)
    out_ref[...] = held_ref[...].reshape(out_ref.shape).astype(BF)


def rows_of(table, places):
    count, width = places.shape[0], table.shape[1]
    step = 512
    return pl.pallas_call(
        rows_kernel,
        grid=(count // step,),
        out_shape=jax.ShapeDtypeStruct((count, width), BF),
        in_specs=[
            pl.BlockSpec(memory_space=pltpu.SMEM),
            pl.BlockSpec(table.shape, lambda i: (0, 0)),
        ],
        out_specs=pl.BlockSpec((step, width), lambda i: (i, 0)),
        scratch_shapes=[pltpu.VMEM((step // 8, 8, width), F32)],
        compiler_params=pltpu.CompilerParams(vmem_limit_bytes=48 * 1024 * 1024),
        cost_estimate=pl.CostEstimate(
            flops=0, bytes_accessed=80 * count * width, transcendentals=0
        ),
        name="look_up",
    )(places, table)


def mm(left, right):
    return jnp.dot(left, right, preferred_element_type=F32)


def mm_nt(left, right):
    return lax.dot_general(left, right, (((1,), (1,)), ((), ())), preferred_element_type=F32)


def mm_tn(left, right):
    return lax.dot_general(left, right, (((0,), (0,)), ((), ())), preferred_element_type=F32)


def norm_forward(stream, gain_row):
    inverse = lax.rsqrt(jnp.mean(stream * stream, axis=-1, keepdims=True) + EPS)
    return stream * inverse * gain_row


def norm_backward(stream, gain_row, grad_out):
    inverse = lax.rsqrt(jnp.mean(stream * stream, axis=-1, keepdims=True) + EPS)
    scaled = grad_out * gain_row
    d_input = inverse * scaled - stream * inverse**3 * jnp.mean(
        stream * scaled, axis=-1, keepdims=True
    )
    return (d_input, jnp.sum(grad_out * stream * inverse, axis=0))


def nt(left, right):
    return lax.dot_general(left, right, (((1,), (1,)), ((), ())), preferred_element_type=F32)


def allowed_keys(row_ref, shape, by_query, per_item):
    queries = lax.broadcasted_iota(jnp.int32, shape, by_query)
    keys = lax.broadcasted_iota(jnp.int32, shape, 1 - by_query)
    each = shape[1 - by_query] // per_item
    return row_ref[0] + queries * per_item >= lax.rem(keys, each) * per_item + keys // each


def attend_kernel(causal, row_ref, q_ref, k_ref, v_ref, o_ref):
    rows, length = q_ref.shape[0], k_ref.shape[0]
    shape = (rows, length)
    if causal:
        allowed = allowed_keys(row_ref, shape, 0, causal)
    for head in range(q_ref.shape[1] // HD):
        own = pl.ds(head * HD, HD)
        shared = pl.ds(head // (HQ // HK) * HD, HD)
        scores = nt(q_ref[:, own], k_ref[:, shared]) * HD ** (-0.5)
        if causal:
            scores = jnp.where(allowed, scores, -1000000000.0)
        expo = jnp.exp(scores - jnp.max(scores, axis=-1, keepdims=True))
        probs = expo * (1.0 / jnp.sum(expo, axis=-1, keepdims=True))
        mixed = jnp.dot(probs.astype(BF), v_ref[:, shared], preferred_element_type=F32)
        o_ref[:, own] = mixed.astype(BF)


def attend_back_kernel(causal, row_ref, q_ref, k_ref, v_ref, d_ref, dq_ref, dk_ref, dv_ref):
    rows, length = q_ref.shape[0], k_ref.shape[0]
    shape = (length, rows)
    share = HQ // HK
    if causal:
        allowed = allowed_keys(row_ref, shape, 1, causal)
    for pair in range(k_ref.shape[1] // HD):
        shared = pl.ds(pair * HD, HD)
        keys, values = k_ref[:, shared], v_ref[:, shared]
        d_keys = d_values = None
        for head in range(pair * share, (pair + 1) * share):
            own = pl.ds(head * HD, HD)
            queries, d_mixed = q_ref[:, own], d_ref[:, own]
            scores = nt(keys, queries) * HD ** (-0.5)
            if causal:
                scores = jnp.where(allowed, scores, -1000000000.0)
            expo = jnp.exp(scores - jnp.max(scores, axis=0, keepdims=True))
            probs = expo * (1.0 / jnp.sum(expo, axis=0, keepdims=True))
            d_probs = nt(values, d_mixed)
            mean = jnp.sum(probs * d_probs, axis=0, keepdims=True)
            d_scores = (probs * (d_probs - mean)).astype(BF)
            key_term = jnp.dot(d_scores, queries, preferred_element_type=F32)
            value_term = jnp.dot(probs.astype(BF), d_mixed, preferred_element_type=F32)
            d_keys = key_term if d_keys is None else d_keys + key_term
            d_values = value_term if d_values is None else d_values + value_term
            d_queries = lax.dot_general(
                keys, d_scores, (((0,), (0,)), ((), ())), preferred_element_type=F32
            )
            dq_ref[:, own] = (d_queries.T * HD ** (-0.5)).astype(BF)
        dk_ref[:, shared] = (d_keys * HD ** (-0.5)).astype(BF)
        dv_ref[:, shared] = d_values.astype(BF)


def attend_specs(rows, length):
    wide = 128 * (HQ // HK)
    queries = pl.BlockSpec((rows, wide), lambda i: (0, i))
    keys = pl.BlockSpec((length, 128), lambda i: (0, i))
    values = pl.BlockSpec((length, 128), lambda i: (0, i + KW // 128))
    return queries, keys, values


def attend_forward(queries, keyvals, first_row, per_item):
    rows, length = queries.shape[0], keyvals.shape[0]
    by_query, by_key, by_value = attend_specs(rows, length)
    return pl.pallas_call(
        partial(attend_kernel, 0 if first_row is None else per_item),
        grid=(KW // 128,),
        out_shape=jax.ShapeDtypeStruct(queries.shape, BF),
        in_specs=[pl.BlockSpec(memory_space=pltpu.SMEM), by_query, by_key, by_value],
        out_specs=by_query,
        compiler_params=pltpu.CompilerParams(vmem_limit_bytes=56 * 1024 * 1024),
        cost_estimate=pl.CostEstimate(
            flops=4 * rows * length * QW,
            bytes_accessed=4 * rows * QW + 4 * length * KW,
            transcendentals=HQ * rows * length,
        ),
        name="attend",
    )(jnp.reshape(0 if first_row is None else first_row, (1,)), queries, keyvals, keyvals)


def attend_backward(queries, keyvals, first_row, per_item, d_mixed):
    rows, length = queries.shape[0], keyvals.shape[0]
    by_query, by_key, by_value = attend_specs(rows, length)
    d_queries, d_keys, d_values = pl.pallas_call(
        partial(attend_back_kernel, 0 if first_row is None else per_item),
        grid=(KW // 128,),
        out_shape=[
            jax.ShapeDtypeStruct(queries.shape, BF),
            jax.ShapeDtypeStruct((length, KW), BF),
            jax.ShapeDtypeStruct((length, KW), BF),
        ],
        in_specs=[pl.BlockSpec(memory_space=pltpu.SMEM), by_query, by_key, by_value, by_query],
        out_specs=[by_query, by_key, by_key],
        compiler_params=pltpu.CompilerParams(vmem_limit_bytes=56 * 1024 * 1024),
        cost_estimate=pl.CostEstimate(
            flops=10 * rows * length * QW,
            bytes_accessed=6 * rows * QW + 8 * length * KW,
            transcendentals=HQ * rows * length,
        ),
        name="attend_back",
    )(jnp.reshape(0 if first_row is None else first_row, (1,)), queries, keyvals, keyvals, d_mixed)
    return (d_queries, jnp.concatenate([d_keys, d_values], axis=1))


def update(weight, gradient, moment, average, rate, factor):
    clipped = gradient * factor
    moment_new = MOMENTUM * moment + (1 - MOMENTUM) * clipped
    weight_new = weight - rate * ((1 - MOMENTUM) * clipped + MOMENTUM * moment_new)
    average_new = AVERAGE * average + (1 - AVERAGE) * weight_new
    return (weight_new, moment_new, average_new)


def on_device(
    dp_axes,
    mp_axes,
    source_ids,
    target_ids,
    prefix,
    attn_in,
    attn_out,
    ff_in,
    ff_out,
    table,
    gains,
    attn_in_mom,
    attn_out_mom,
    ff_in_mom,
    ff_out_mom,
    table_mom,
    gains_mom,
    attn_in_avg,
    attn_out_avg,
    ff_in_avg,
    ff_out_avg,
    table_avg,
    gains_avg,
):
    every = dp_axes + mp_axes
    core = mp_axes[-1]
    row_axes = mp_axes[1:]
    line = mp_axes[:-1]
    gather_orders = (
        line + dp_axes + (core,),
        line + dp_axes[::-1] + (core,),
        dp_axes + line + (core,),
    )
    sum_orders = tuple(order[::-1] for order in gather_orders)
    last = (line[-1], core)
    three = (gather_orders[0], gather_orders[1], line[:-1] + dp_axes[::-1] + last)
    six_orders = three + three[:2] + (line[:-1] + dp_axes + last,)
    two_dp, two_mp, two_rows = (2,) * len(dp_axes), (2,) * len(mp_axes), (2,) * len(row_axes)

    seq_count, length = source_ids.shape
    rows = length // 2 ** len(row_axes)
    per_item = 2 ** len(row_axes)
    skip = PREFIX_LOW // per_item
    first_row = lax.axis_index(row_axes)

    def by_device(values):
        return values.reshape(values.shape[:-1] + (rows, per_item)).swapaxes(-1, -2)

    def with_skipped(values):
        return jnp.pad(values, ((rows - values.shape[0], 0), (0, 0)))


    vocab_part = table.shape[0]
    offset = lax.axis_index(mp_axes) * vocab_part
    table_bf = table.astype(BF)
    decoder_ids = jnp.concatenate(
        [jnp.zeros((seq_count, 1), jnp.int32), target_ids[:, :-1]], axis=1
    )
    ids_all = by_device(gather_blocks(jnp.stack([source_ids, decoder_ids]), dp_axes, dp_axes))
    ids_all = ids_all.reshape(-1, 2, 2 ** len(mp_axes), rows).transpose(1, 2, 0, 3).reshape(2, -1)
    table_rows = lax.all_gather(table_bf, dp_axes, axis=1, tiled=True)
    local_ids = ids_all - offset
    inside = (local_ids >= 0) & (local_ids < vocab_part)

    def trade(parts):
        for position, axis in enumerate(dp_axes):
            bit = lax.axis_index(axis)
            received = swap(take_bit(parts, 1 - bit, position), axis)
            kept = take_bit(parts, bit, position)
            parts = jnp.stack(
                [jnp.where(bit == 0, kept, received), jnp.where(bit == 0, received, kept)],
                axis=position,
            )
        return parts

    table_zero = jnp.pad(table, ((0, 8), (0, 0)))
    places = jnp.where(inside, local_ids, vocab_part)

    def look_up(which):
        found = rows_of(table_zero, places[which])
        return found.reshape(2 ** len(mp_axes), -1, found.shape[-1])

    def collect(found):
        return lax.psum_scatter(found, mp_axes, scatter_dimension=0)

    def embed(mine):
        width = mine.shape[-1]
        parts = trade(mine.reshape(two_dp + (rows, width))).reshape(-1, rows, width)
        return jnp.moveaxis(parts, 0, 1).reshape(rows, -1).astype(F32)

    found_e = look_up(0)
    mine_e = collect(found_e)
    found_d = look_up(1)
    mine_d = collect(found_d)

    gain_all = gather_blocks(gains.astype(BF).T, every, gather_orders[0])
    gain_all = gain_all.reshape(-1, gains.shape[0]).T.astype(F32)
    shards = [attn_in[0], attn_out[0], ff_in[0], ff_out[0]]
    shards += [attn_in[1], attn_out[1], attn_in[2], attn_out[2], ff_in[1], ff_out[1]]
    shards = [shard.astype(BF) for shard in shards]
    in_kernels = attn_in.shape[1] % 16 == 0
    if in_kernels:
        *shards, found_e, found_d, table_rows, gain_all = lax.optimization_barrier(
            shards + [found_e, found_d, table_rows, gain_all]
        )
        behind = (8, 9,)
        full = [None] * len(shards)
        ahead = [k for k in range(len(shards)) if k not in behind]
        for k, got in zip(ahead, gather_all([shards[k] for k in ahead], every, six_orders)):
            full[k] = got
        full[0], mine_e, mine_d = lax.optimization_barrier((full[0], mine_e, mine_d))
        full[0], *sent = lax.optimization_barrier([full[0]] + [shards[k] for k in behind])
        for k, shard in zip(behind, sent):
            full[k] = lax.all_gather(shard, every, axis=0, tiled=True)
    else:
        full = [
            gather_blocks(shard, every, gather_orders[k % 3]) for k, shard in enumerate(shards)
        ]
    full = [got.reshape((-1,) + shard.shape[1:]) for got, shard in zip(full, shards)]
    a_in, a_out = (full[0], full[4], full[6]), (full[1], full[5], full[7])
    f_in, f_out = (full[2], full[8]), (full[3], full[9])
    def spread_keys(own):
        return gather_blocks(own, row_axes, row_axes).reshape(length, -1)

    def attention_forward(stream, source, block, gain_row, start):
        normed = norm_forward(stream, gain_row).astype(BF)
        anchor = normed if source is None else source
        keyvals = spread_keys(mm(anchor, a_in[block][:, QW:]).astype(BF))
        first = 0 if start is None else skip
        queries = mm(normed[first:], a_in[block][:, :QW]).astype(BF)
        position = None if start is None else start + first * per_item
        mixed = attend_forward(queries, keyvals, position, per_item)
        out = stream[first:] + mm(mixed, a_out[block])
        return (out, (stream, normed, anchor, queries, keyvals, mixed))

    def ffn_forward(stream, which, gain_row):
        normed = norm_forward(stream, gain_row).astype(BF)
        both = mm(normed, f_in[which])
        hidden_act = (jax.nn.gelu(both[:, :FF], approximate=True) * both[:, FF:]).astype(BF)
        return (stream + mm(hidden_act, f_out[which]), (stream, normed, both, hidden_act))

    stream_e = embed(mine_e)
    stream_e, enc_attn = attention_forward(stream_e, None, 0, gain_all[0], None)
    stream_e, mine_d = lax.optimization_barrier((stream_e, mine_d))
    stream_d = embed(mine_d)
    stream_d, dec_self = attention_forward(stream_d, None, 1, gain_all[3], first_row)
    stream_e, enc_ffn = ffn_forward(stream_e, 0, gain_all[1])
    encoded = norm_forward(stream_e, gain_all[2]).astype(BF)
    stream_d, dec_cross = attention_forward(stream_d, encoded, 2, gain_all[4], None)
    stream_d, dec_ffn = ffn_forward(stream_d, 1, gain_all[5])
    hidden = norm_forward(stream_d, gain_all[6]).astype(BF)

    hidden_all = gather_blocks(hidden, mp_axes, mp_axes).reshape(-1, hidden.shape[-1])
    targets = by_device(target_ids)[..., skip:].reshape(-1)
    vocab_ids = offset + jnp.arange(vocab_part)
    hits = vocab_ids[None, :] == targets[:, None]
    logits = mm_nt(hidden_all, table_rows) * D ** (-0.5)
    own_max = jnp.max(logits, axis=-1)
    expo = jnp.exp(logits - own_max[:, None])
    stats = jnp.stack(
        [own_max, jnp.sum(expo, axis=-1), jnp.sum(jnp.where(hits, logits, 0.0), axis=-1)]
    )
    expo = expo.astype(BF)
    for axis in mp_axes[::-1]:
        other = swap(stats, axis)
        joint = jnp.maximum(stats[0], other[0])
        stats = jnp.stack(
            [
                joint,
                stats[1] * jnp.exp(stats[0] - joint) + other[1] * jnp.exp(other[0] - joint),
                stats[2] + other[2],
            ]
        )
    log_norm = stats[0] + jnp.log(stats[1])
    prefix_group = lax.dynamic_slice_in_dim(prefix, lax.axis_index(dp_axes) * seq_count, seq_count)
    positions = by_device(jnp.arange(length))[..., skip:].reshape(1, -1)
    scored = (positions >= prefix_group[:, None]).astype(F32).reshape(-1)
    scored_count = jnp.sum((length - prefix).astype(F32))
    scale = jnp.exp(own_max - log_norm)
    d_logits = (
        (expo.astype(F32) * scale[:, None] - hits.astype(F32)) * (scored / scored_count)[:, None]
    ).astype(BF)
    d_final = (mm(d_logits, table_rows) * D ** (-0.5)).astype(BF)

    def table_term(held):
        _, rows_all = lax.optimization_barrier((held, hidden_all))
        return (mm_tn(d_logits, rows_all) * D ** (-0.5)).astype(BF)

    d_final, head_table = sum_blocks(
        d_final.reshape(two_mp + hidden.shape), mp_axes, mp_axes[::-1], F32, table_term
    )

    grad_table = lax.psum_scatter(head_table, dp_axes, scatter_dimension=1, tiled=True)

    def ffn_backward(saved, which, gain_row, d_stream):
        stream, normed, both, hidden_act = saved
        up_part = both[:, FF:]
        activated, gelu_pull = jax.vjp(partial(jax.nn.gelu, approximate=True), both[:, :FF])
        d_branch = d_stream.astype(BF)
        d_hidden = mm_nt(d_branch, f_out[which])
        d_both = jnp.concatenate(
            [gelu_pull(d_hidden * up_part)[0].astype(BF), (d_hidden * activated).astype(BF)], axis=1
        )
        d_normed = mm_nt(d_both, f_in[which])
        d_input, grad_gain = norm_backward(stream, gain_row, d_normed)
        return (d_stream + d_input, (normed, d_both, hidden_act, d_branch), grad_gain)

    def attention_backward(saved, cross, block, gain_row, start, d_stream):
        stream, normed, anchor, queries, keyvals, mixed = saved
        d_branch = d_stream.astype(BF)
        d_mixed = mm_nt(d_branch, a_out[block]).astype(BF)
        queries = with_skipped(queries)
        d_queries, d_keyvals = attend_backward(
            queries, keyvals, start, per_item, with_skipped(d_mixed)
        )
        d_keyvals = sum_blocks(
            d_keyvals.reshape(two_rows + (rows, -1)), row_axes, row_axes[::-1], BF
        )
        d_queries = d_queries[rows - stream.shape[0] :]
        d_normed = mm_nt(d_queries, a_in[block][:, :QW])
        d_anchor = mm_nt(d_keyvals, a_in[block][:, QW:])
        if not cross:
            d_normed = d_normed + d_anchor
        factors = (normed, anchor, d_queries, d_keyvals, mixed, d_branch)
        d_input, grad_gain = norm_backward(stream, gain_row, d_normed)
        if start is not None:
            d_stream = with_skipped(d_stream)
        return (d_stream + d_input, d_anchor, factors, grad_gain)

    d_y, gain6 = norm_backward(stream_d, gain_all[6], d_final)
    d_y, ffn_factors1, gain5 = ffn_backward(dec_ffn, 1, gain_all[5], d_y)
    d_y, d_encoded, attn_factors2, gain4 = attention_backward(
        dec_cross, True, 2, gain_all[4], None, d_y
    )
    d_y, _, attn_factors1, gain3 = attention_backward(
        dec_self, False, 1, gain_all[3], first_row, d_y
    )
    d_encoded, grad_table = lax.optimization_barrier((d_encoded, grad_table))
    d_x, gain2 = norm_backward(stream_e, gain_all[2], d_encoded)
    d_x, ffn_factors0, gain1 = ffn_backward(enc_ffn, 0, gain_all[1], d_x)
    d_x, _, attn_factors0, gain0 = attention_backward(
        enc_attn, False, 0, gain_all[0], None, d_x
    )

    def trade_rows(d_rows):
        width = table.shape[1]
        parts = jnp.moveaxis(d_rows.astype(BF).reshape(rows, -1, width), 1, 0)
        return trade(parts.reshape(two_dp + (rows, width))).reshape(-1, width)

    def look_back(which, spread):
        own_ids = local_ids[which].astype(jnp.int16)
        places = (own_ids[None, :] == jnp.arange(vocab_part, dtype=jnp.int16)[:, None]).astype(BF)
        return mm(places, spread.reshape(-1, spread.shape[-1]))

    traded_y, traded_x = trade_rows(d_y), trade_rows(d_x)
    spread_y, spread_x = (lax.all_gather(traded, mp_axes) for traded in (traded_y, traded_x))

    gain_grads = jnp.stack([gain0, gain1, gain2, gain3, gain4, gain5, gain6])
    gain_blocks = jnp.moveaxis(gain_grads.reshape(gains.shape[0], -1, gains.shape[1]), 1, 0)
    grad_gains = sum_blocks(
        gain_blocks.reshape((2,) * len(every) + gains.shape), every, sum_orders[0]
    )

    if in_kernels:
        traded_x, ffn_left, attn_left = lax.optimization_barrier(
            (traded_x, ffn_factors0[2], attn_factors0[0])
        )
        attn_factors0 = (attn_left, attn_left) + attn_factors0[2:]
        ffn_factors0 = ffn_factors0[:2] + (ffn_left,) + ffn_factors0[3:]
    lefts, rights, spans = [], [], []
    for normed, anchor, d_queries, d_keyvals, mixed, d_branch in (
        attn_factors0,
        attn_factors1,
        attn_factors2,
    ):
        lefts += [normed, mixed] if anchor is normed else [normed, anchor, mixed]
        rights += [d_queries, d_keyvals, d_branch]
        widths = [d_queries.shape[1], d_keyvals.shape[1]]
        spans += ([sum(widths)] if anchor is normed else widths) + [d_branch.shape[1]]
    wide_lefts, wide_rights = [], []
    for normed, d_both, hidden_act, d_branch in (ffn_factors0, ffn_factors1):
        lefts.append(normed)
        rights.append(d_both)
        spans.append(d_both.shape[1])
        wide_lefts.append(hidden_act)
        wide_rights.append(d_branch)
    wide_spans = [right.shape[1] for right in wide_rights]
    if in_kernels:
        back_orders = tuple(order[::-1] for order in three)
        six_back = tuple(order[::-1] for order in six_orders)
        own = grad_sums(lefts, rights, every, six_back, spans, 1, 128)
        wide = grad_sums(wide_lefts, wide_rights, every, back_orders[:2], wide_spans, 2)
        own, wide, spread_x, spread_y = lax.optimization_barrier((own, wide, spread_x, spread_y))
    else:

        def own_sum(left, right, kind):
            product = mm_tn(left, right).astype(BF)
            blocks = product.reshape((2,) * len(every) + (-1,) + product.shape[1:])
            return sum_blocks(blocks, every, sum_orders[kind % 3])

        everything = jnp.concatenate([with_skipped(right) for right in rights], axis=1)
        ends = [sum(spans[: k + 1]) for k in range(len(spans))]
        parts = jnp.split(everything, ends[:-1], axis=1)
        pairs = list(enumerate(zip([with_skipped(left) for left in lefts], parts)))
        own = jnp.concatenate([own_sum(*pair, k) for k, pair in pairs], axis=1)
        pairs = list(enumerate(zip(wide_lefts, wide_rights)))
        wide = jnp.concatenate([own_sum(*pair, k) for k, pair in pairs], axis=1)
    grad_table = grad_table.astype(F32) + look_back(1, spread_y) + look_back(0, spread_x)
    ends = (attn_in.shape[2], attn_in.shape[2] + attn_out.shape[2])
    ffn_from = 3 * ends[1]
    gradients = (
        jnp.stack([own[:, ends[1] * k : ends[1] * k + ends[0]] for k in range(3)]),
        jnp.stack([own[:, ends[1] * k + ends[0] : ends[1] * (k + 1)] for k in range(3)]),
        jnp.stack([own[:, ffn_from + 2 * FF * k : ffn_from + 2 * FF * (k + 1)] for k in range(2)]),
        jnp.stack(jnp.split(wide, 2, axis=1)),
        grad_table,
        grad_gains,
    )

    own_losses = ((log_norm - stats[2]) * scored).reshape(2 ** len(mp_axes), -1)
    loss_part = jnp.sum(take_bit(own_losses, lax.axis_index(mp_axes), 0))
    squares = sum((jnp.sum(gradient * gradient) for gradient in gradients))
    totals = jnp.stack([loss_part, squares])
    totals = total_of(totals, every[::-1], 3)
    loss_sum = totals[0]
    grad_norm = jnp.sqrt(totals[1])
    factor = jnp.minimum(1.0, CLIP / grad_norm)
    weights = (attn_in, attn_out, ff_in, ff_out, table, gains)
    moments = (attn_in_mom, attn_out_mom, ff_in_mom, ff_out_mom, table_mom, gains_mom)
    averages = (attn_in_avg, attn_out_avg, ff_in_avg, ff_out_avg, table_avg, gains_avg)
    results = [
        update(weight, gradient, moment, average, rate, factor)
        for weight, gradient, moment, average, rate in zip(
            weights, gradients, moments, averages, step_rates()
        )
    ]
    return (loss_sum, scored_count, grad_norm) + tuple(
        results[array][kind] for kind in range(3) for array in range(6)
    )


def solution(mesh):
    dp_count, mp_count = mesh.shape["dp"], mesh.shape["mp"]
    dp_axes = tuple(f"d{k}" for k in range(dp_count.bit_length() - 1))
    mp_axes = tuple(f"m{k}" for k in range(mp_count.bit_length() - 1))
    every = dp_axes + mp_axes
    fine = Mesh(mesh.devices.reshape((2,) * len(every)), every)
    rows_split = P(None, every, None)
    params = (rows_split,) * 4 + (P(mp_axes, dp_axes), P(None, every))
    in_specs = (P(dp_axes, None), P(dp_axes, None), P()) + params * 3
    out_specs = (P(), P(), P()) + params * 3
    return jax.shard_map(
        partial(on_device, dp_axes, mp_axes),
        mesh=fine,
        in_specs=in_specs,
        out_specs=out_specs,
        check_vma=False,
    )
```

```python
from functools import partial

import jax
import jax.numpy as jnp
from jax import lax
from jax.experimental import pallas as pl
from jax.experimental.pallas import tpu as pltpu
from jax.sharding import Mesh
from jax.sharding import PartitionSpec as P

D = 1024
HQ = 16
HK = 8
HD = 64
FF = 2816
LEN = 1024
QW = 1024
KW = 512
PARAMS = 59644928

MOMENTUM = 0.9
AVERAGE = 0.9
CLIP = 0.0002
EPS = 1e-06

BF = jnp.bfloat16
F32 = jnp.float32
MESH = pl.DeviceIdType.MESH
CHUNK = 256
LANES = 3
PREFIX_LOW = 192


def step_rates():
    base_rate = 3.5 * PARAMS**0.5 / CLIP
    return (
        base_rate * D ** (-0.5),
        base_rate * max(QW // LEN, 1) ** (-0.5),
        base_rate * D ** (-0.5),
        base_rate * FF ** (-0.5),
        base_rate * 2.0,
        base_rate * 0.3,
    )


def swap(value, axis):
    return lax.ppermute(value, axis, [(0, 1), (1, 0)])


def take_bit(value, bit, position):
    return lax.dynamic_index_in_dim(value, bit, position, keepdims=False)


def gather_blocks(block, layout, order):
    have = []
    held = block
    for axis in order:
        received = swap(held, axis)
        position = sum(layout.index(other) < layout.index(axis) for other in have)
        bit = lax.axis_index(axis)
        shape = held.shape
        joined = jnp.zeros(shape[:position] + (2,) + shape[position:], held.dtype)
        joined = lax.dynamic_update_index_in_dim(joined, held, bit, position)
        held = lax.dynamic_update_index_in_dim(joined, received, 1 - bit, position)
        have.append(axis)
    return held


def sum_blocks(terms, layout, order, last=F32, beside=None):
    left = list(layout)
    held = terms
    for axis in order:
        position = left.index(axis)
        bit = lax.axis_index(axis)
        received = swap(take_bit(held, 1 - bit, position), axis)
        if beside is not None and axis == order[1]:
            received, result = lax.optimization_barrier((received, beside(held)))
        held = take_bit(held, bit, position).astype(F32) + received.astype(F32)
        left.remove(axis)
        if left:
            held = held.astype(terms.dtype)
    return held.astype(last) if beside is None else (held.astype(last), result)


def greet(axes):
    barrier = pltpu.get_barrier_semaphore()
    for axis in axes:
        pl.semaphore_signal(
            barrier, inc=1, device_id={axis: 1 - lax.axis_index(axis)}, device_id_type=MESH
        )
    pl.semaphore_wait(barrier, len(axes))


def gather_kernel(layout, units, lanes, count, *refs):
    ins, outs = refs[:count], refs[count : 2 * count]
    own_sem, send_sem, recv_sem = refs[2 * count :]
    bits = {axis: lax.axis_index(axis) for axis in layout}
    depth = len(layout)

    def region(unit, have):
        tensor, start, size, _ = units[unit]
        blocks = tuple(pl.ds(0, 2) if axis in have else bits[axis] for axis in layout)
        return outs[tensor].at[blocks + (slice(None), pl.ds(start, size))]

    own = [
        pltpu.make_async_copy(
            ins[k], outs[k].at[tuple(bits[axis] for axis in layout)], own_sem.at[k]
        )
        for k in range(count)
    ]
    for copy in own:
        copy.start()
    greet(layout)
    for copy in own:
        copy.wait()
    copies = {}
    groups = -(-len(units) // lanes)
    for turn in range(groups + depth - 1):
        for step in reversed(range(depth)):
            first = (turn - step) * lanes
            for unit in range(max(first, 0), min(first + lanes, len(units))):
                order = units[unit][3]
                if step:
                    copies[unit, step - 1].wait_recv()
                source = region(unit, order[:step])
                copy = pltpu.make_async_remote_copy(
                    src_ref=source,
                    dst_ref=source,
                    send_sem=send_sem.at[unit, step],
                    recv_sem=recv_sem.at[unit, step],
                    device_id={order[step]: 1 - bits[order[step]]},
                    device_id_type=MESH,
                )
                copy.start()
                copies[unit, step] = copy
    for unit in range(len(units)):
        copies[unit, depth - 1].wait_recv()
    for copy in copies.values():
        copy.wait_send()


def gather_all(shards, layout, orders):
    units = []
    for tensor, shard in enumerate(shards):
        columns = shard.shape[1]
        step = -(-512 * 32 // shard.shape[0] // 128) * 128
        pieces = -(-columns // step)
        starts = [step * piece for piece in range(pieces)] + [columns]
        for piece in range(pieces):
            order = orders[len(units) % len(orders)]
            units.append((tensor, starts[piece], starts[piece + 1] - starts[piece], order))
    count = len(shards)
    semaphores = pltpu.SemaphoreType.DMA((len(units), len(layout)))
    return pl.pallas_call(
        partial(gather_kernel, layout, tuple(units), LANES, count),
        out_shape=[
            jax.ShapeDtypeStruct((2,) * len(layout) + shard.shape, shard.dtype) for shard in shards
        ],
        in_specs=[pl.BlockSpec(memory_space=pl.ANY)] * count,
        out_specs=[pl.BlockSpec(memory_space=pl.ANY)] * count,
        scratch_shapes=[pltpu.SemaphoreType.DMA((count,)), semaphores, semaphores],
        compiler_params=pltpu.CompilerParams(collective_id=0, has_side_effects=True),
        name="gather_weights",
    )(*shards)


def grad_kernel(layout, orders, bounds, chunks, counts, chunk_width, *refs):
    lefts, rights = refs[: counts[0]], refs[counts[0] : sum(counts)]
    out_ref = refs[sum(counts)]
    scratch = refs[sum(counts) + 1 :]
    depth = len(layout)
    lanes = len(orders)
    sends, recvs, helds = (
        [scratch[kind * lanes * depth + lane * depth :][:depth] for lane in range(lanes)]
        for kind in range(3)
    )
    given_ref, x_ref, y_ref, in_sem, send_sem, recv_sem = scratch[3 * lanes * depth :]
    bits = {axis: lax.axis_index(axis) for axis in layout}
    groups = out_ref.shape[1] // chunk_width // lanes
    tokens = y_ref.shape[0]

    copies, passed = [], 0
    for k, term in enumerate(lefts + rights):
        absent = tokens - term.shape[0]
        if k < len(lefts):
            place = given_ref.at[k]
        else:
            place = y_ref.at[:, pl.ds(passed, term.shape[1])]
            passed += term.shape[1]
        if absent:
            place[pl.ds(0, absent), :] = jnp.zeros((absent, term.shape[1]), BF)
        copy = pltpu.make_async_copy(term, place.at[pl.ds(absent, term.shape[0])], in_sem.at[k])
        copy.start()
        copies.append(copy)
    greet(layout)
    padded = x_ref.shape[2] * 2 // 2**depth

    def turned(k):
        copies[k].wait()
        rows = lefts[k].shape[1] // 2**depth
        across = given_ref[k].astype(F32).T.reshape(-1, 2, rows, tokens)
        for bit in range(2):
            blocks = across[:, bit]
            if padded > rows:
                filler = jnp.zeros((blocks.shape[0], padded - rows, tokens), F32)
                blocks = jnp.concatenate([blocks, filler], axis=1)
            x_ref[k, bit] = blocks.reshape(-1, tokens).astype(BF)
    for copy in copies[len(lefts) :]:
        copy.wait()
    turned(0)
    early = [k for k in range(1, len(lefts)) if bounds[k - 1] // lanes < k - 1]
    for k in early:
        turned(k)

    def exchange(lane, step, group):
        axis = orders[lane][step]
        slot = lax.rem(group, 2)
        return pltpu.make_async_remote_copy(
            src_ref=sends[lane][step],
            dst_ref=recvs[lane][step].at[slot],
            send_sem=send_sem.at[lane, step],
            recv_sem=recv_sem.at[lane, step, slot],
            device_id={axis: 1 - bits[axis]},
            device_id_type=MESH,
        )

    def first(lane, group):
        chunk = jnp.minimum(group * lanes + lane, chunks - 1)
        which = sum((chunk >= bound).astype(jnp.int32) for bound in bounds) if bounds else 0
        columns = y_ref[:, pl.ds(pl.multiple_of(chunk * chunk_width, chunk_width), chunk_width)]
        bit = bits[orders[lane][0]]
        given = jnp.dot(x_ref[which, 1 - bit], columns, preferred_element_type=F32)
        sends[lane][0][...] = given.astype(BF).reshape(sends[lane][0].shape)
        exchange(lane, 0, group).start()
        kept = jnp.dot(x_ref[which, bit], columns, preferred_element_type=F32)
        helds[lane][0][...] = kept.reshape(helds[lane][0].shape)

    def later(lane, step, group):
        order = orders[lane]
        slot = lax.rem(group, 2)
        exchange(lane, step - 1, group).wait()
        held, received = helds[lane][step - 1], recvs[lane][step - 1]
        if step == depth:
            chunk = group * lanes + lane
            out_ref[:, pl.ds(pl.multiple_of(chunk * chunk_width, chunk_width), chunk_width)] = held[
                ...
            ] + received[slot].astype(F32)
            return
        position = [axis for axis in layout if axis not in order[:step]].index(order[step])
        bit = bits[order[step]]

        def total(choice):
            index = (slice(None),) * position + (choice,)
            return held[index] + received[(slot,) + index].astype(F32)

        sends[lane][step][...] = total(1 - bit).astype(BF)
        exchange(lane, step, group).start()
        helds[lane][step][...] = total(bit)

    @pl.loop(0, groups + depth)
    def _(turn):
        for k in range(1, len(lefts)):
            if k not in early:
                pl.when(turn == k - 1)(partial(turned, k))
        for step in reversed(range(depth + 1)):
            group = turn - step

            @pl.when((group >= 0) & (group < groups))
            def _():
                for lane in range(lanes):
                    if step:
                        later(lane, step, group)
                    else:
                        first(lane, group)


def grad_sums(lefts, rights, layout, orders, spans, collective, chunk_width=CHUNK):
    depth, lanes = len(layout), len(orders)
    tokens, width = max(left.shape[0] for left in lefts), lefts[0].shape[1]
    rows = width // 2**depth
    padded = -(-rows // 16) * 16
    total = sum(right.shape[1] for right in rights)
    chunks = total // chunk_width
    groups = -(-chunks // lanes)
    bounds, passed = [], 0
    for span in spans[:-1]:
        passed += span // chunk_width
        bounds.append(passed)
    send_shapes, recv_shapes, held_shapes = [], [], []
    for _ in range(lanes):
        for step in range(depth):
            shape = (2,) * (depth - 1 - step) + (padded, chunk_width)
            send_shapes.append(pltpu.VMEM(shape, BF))
            recv_shapes.append(pltpu.VMEM((2,) + shape, BF))
            held_shapes.append(pltpu.VMEM(shape, F32))
    counts = (len(lefts), len(rights))
    out = pl.pallas_call(
        partial(grad_kernel, layout, orders, tuple(bounds), chunks, counts, chunk_width),
        out_shape=jax.ShapeDtypeStruct((padded, groups * lanes * chunk_width), F32),
        in_specs=[pl.BlockSpec(memory_space=pl.ANY)] * sum(counts),
        out_specs=pl.BlockSpec(memory_space=pltpu.VMEM),
        scratch_shapes=send_shapes
        + recv_shapes
        + held_shapes
        + [
            pltpu.VMEM((len(lefts), tokens, width), BF),
            pltpu.VMEM((len(lefts), 2, 2 ** (depth - 1) * padded, tokens), BF),
            pltpu.VMEM((tokens, total), BF),
            pltpu.SemaphoreType.DMA((sum(counts),)),
            pltpu.SemaphoreType.DMA((lanes, depth)),
            pltpu.SemaphoreType.DMA((lanes, depth, 2)),
        ],
        compiler_params=pltpu.CompilerParams(
            collective_id=collective, has_side_effects=True, vmem_limit_bytes=56 * 1024 * 1024
        ),
        name="sum_gradients",
    )(*lefts, *rights)
    return out[:rows, :total]


def greet_rounds(rounds):
    barrier = pltpu.get_barrier_semaphore()
    for partners in rounds:
        for axes in partners:
            other = {axis: 1 - lax.axis_index(axis) for axis in axes}
            pl.semaphore_signal(barrier, inc=1, device_id=other, device_id_type=MESH)
    pl.semaphore_wait(barrier, sum(len(partners) for partners in rounds))


def total_kernel(rounds, value_ref, out_ref, send_ref, recv_ref, send_sem, recv_sem):
    greet_rounds(rounds)
    held = value_ref[...]
    for step, partners in enumerate(rounds):
        send_ref[step] = held
        copies = []
        for k, axes in enumerate(partners):
            copy = pltpu.make_async_remote_copy(
                src_ref=send_ref.at[step],
                dst_ref=recv_ref.at[step, k],
                send_sem=send_sem.at[step, k],
                recv_sem=recv_sem.at[step, k],
                device_id={axis: 1 - lax.axis_index(axis) for axis in axes},
                device_id_type=MESH,
            )
            copy.start()
            copies.append(copy)
        for copy in copies:
            copy.wait()
        held = held + recv_ref[step, 0]
        if len(partners) > 1:
            held = held + (recv_ref[step, 1] + recv_ref[step, 2])
    out_ref[...] = held


def total_of(values, layout, collective):
    pairs = [layout[k : k + 2] for k in range(0, len(layout), 2)]
    rounds = tuple(
        ((pair[0],),) if len(pair) == 1 else ((pair[0],), (pair[1],), pair) for pair in pairs
    )
    depth = len(rounds)
    tile = jnp.broadcast_to(jnp.pad(values, (0, 8 - values.shape[0]))[:, None], (8, 128))
    sums = pl.pallas_call(
        partial(total_kernel, rounds),
        out_shape=jax.ShapeDtypeStruct(tile.shape, F32),
        in_specs=[pl.BlockSpec(memory_space=pltpu.VMEM)],
        out_specs=pl.BlockSpec(memory_space=pltpu.VMEM),
        scratch_shapes=[
            pltpu.VMEM((depth, 8, 128), F32),
            pltpu.VMEM((depth, 3, 8, 128), F32),
            pltpu.SemaphoreType.DMA((depth, 3)),
            pltpu.SemaphoreType.DMA((depth, 3)),
        ],
        compiler_params=pltpu.CompilerParams(collective_id=collective, has_side_effects=True),
        name="sum_numbers",
    )(tile)
    return sums[: values.shape[0], 0]


def rows_kernel(ids_ref, table_ref, out_ref, held_ref):
    groups = held_ref.shape[0]
    first = pl.program_id(0) * groups * 8

    def eight(group, carry):
        for k in range(8):
            place = ids_ref[first + group * 8 + k]
            held_ref[group, pl.ds(k, 1), :] = table_ref[pl.ds(place, 1), :]
        return carry

    lax.fori_loop(0, groups, eight, 0)
    out_ref[...] = held_ref[...].reshape(out_ref.shape).astype(BF)


def rows_of(table, places):
    count, width = places.shape[0], table.shape[1]
    step = 512
    return pl.pallas_call(
        rows_kernel,
        grid=(count // step,),
        out_shape=jax.ShapeDtypeStruct((count, width), BF),
        in_specs=[
            pl.BlockSpec(memory_space=pltpu.SMEM),
            pl.BlockSpec(table.shape, lambda i: (0, 0)),
        ],
        out_specs=pl.BlockSpec((step, width), lambda i: (i, 0)),
        scratch_shapes=[pltpu.VMEM((step // 8, 8, width), F32)],
        compiler_params=pltpu.CompilerParams(vmem_limit_bytes=48 * 1024 * 1024),
        cost_estimate=pl.CostEstimate(
            flops=0, bytes_accessed=80 * count * width, transcendentals=0
        ),
        name="look_up",
    )(places, table)


def mm(left, right):
    return jnp.dot(left, right, preferred_element_type=F32)


def mm_nt(left, right):
    return lax.dot_general(left, right, (((1,), (1,)), ((), ())), preferred_element_type=F32)


def mm_tn(left, right):
    return lax.dot_general(left, right, (((0,), (0,)), ((), ())), preferred_element_type=F32)


def norm_forward(stream, gain_row):
    inverse = lax.rsqrt(jnp.mean(stream * stream, axis=-1, keepdims=True) + EPS)
    return stream * inverse * gain_row


def norm_backward(stream, gain_row, grad_out):
    inverse = lax.rsqrt(jnp.mean(stream * stream, axis=-1, keepdims=True) + EPS)
    scaled = grad_out * gain_row
    d_input = inverse * scaled - stream * inverse**3 * jnp.mean(
        stream * scaled, axis=-1, keepdims=True
    )
    return (d_input, jnp.sum(grad_out * stream * inverse, axis=0))


def nt(left, right):
    return lax.dot_general(left, right, (((1,), (1,)), ((), ())), preferred_element_type=F32)


def allowed_keys(row_ref, shape, by_query, per_item):
    queries = lax.broadcasted_iota(jnp.int32, shape, by_query)
    keys = lax.broadcasted_iota(jnp.int32, shape, 1 - by_query)
    each = shape[1 - by_query] // per_item
    return row_ref[0] + queries * per_item >= lax.rem(keys, each) * per_item + keys // each


def attend_kernel(causal, row_ref, q_ref, k_ref, v_ref, o_ref):
    rows, length = q_ref.shape[0], k_ref.shape[0]
    shape = (rows, length)
    if causal:
        allowed = allowed_keys(row_ref, shape, 0, causal)
    for head in range(q_ref.shape[1] // HD):
        own = pl.ds(head * HD, HD)
        shared = pl.ds(head // (HQ // HK) * HD, HD)
        scores = nt(q_ref[:, own], k_ref[:, shared]) * HD ** (-0.5)
        if causal:
            scores = jnp.where(allowed, scores, -1000000000.0)
        expo = jnp.exp(scores - jnp.max(scores, axis=-1, keepdims=True))
        probs = expo * (1.0 / jnp.sum(expo, axis=-1, keepdims=True))
        mixed = jnp.dot(probs.astype(BF), v_ref[:, shared], preferred_element_type=F32)
        o_ref[:, own] = mixed.astype(BF)


def attend_back_kernel(causal, row_ref, q_ref, k_ref, v_ref, d_ref, dq_ref, dk_ref, dv_ref):
    rows, length = q_ref.shape[0], k_ref.shape[0]
    shape = (length, rows)
    share = HQ // HK
    if causal:
        allowed = allowed_keys(row_ref, shape, 1, causal)
    for pair in range(k_ref.shape[1] // HD):
        shared = pl.ds(pair * HD, HD)
        keys, values = k_ref[:, shared], v_ref[:, shared]
        d_keys = d_values = None
        for head in range(pair * share, (pair + 1) * share):
            own = pl.ds(head * HD, HD)
            queries, d_mixed = q_ref[:, own], d_ref[:, own]
            scores = nt(keys, queries) * HD ** (-0.5)
            if causal:
                scores = jnp.where(allowed, scores, -1000000000.0)
            expo = jnp.exp(scores - jnp.max(scores, axis=0, keepdims=True))
            probs = expo * (1.0 / jnp.sum(expo, axis=0, keepdims=True))
            d_probs = nt(values, d_mixed)
            mean = jnp.sum(probs * d_probs, axis=0, keepdims=True)
            d_scores = (probs * (d_probs - mean)).astype(BF)
            key_term = jnp.dot(d_scores, queries, preferred_element_type=F32)
            value_term = jnp.dot(probs.astype(BF), d_mixed, preferred_element_type=F32)
            d_keys = key_term if d_keys is None else d_keys + key_term
            d_values = value_term if d_values is None else d_values + value_term
            d_queries = lax.dot_general(
                keys, d_scores, (((0,), (0,)), ((), ())), preferred_element_type=F32
            )
            dq_ref[:, own] = (d_queries.T * HD ** (-0.5)).astype(BF)
        dk_ref[:, shared] = (d_keys * HD ** (-0.5)).astype(BF)
        dv_ref[:, shared] = d_values.astype(BF)


def attend_specs(rows, length):
    wide = 128 * (HQ // HK)
    queries = pl.BlockSpec((rows, wide), lambda i: (0, i))
    keys = pl.BlockSpec((length, 128), lambda i: (0, i))
    values = pl.BlockSpec((length, 128), lambda i: (0, i + KW // 128))
    return queries, keys, values


def attend_forward(queries, keyvals, first_row, per_item):
    rows, length = queries.shape[0], keyvals.shape[0]
    by_query, by_key, by_value = attend_specs(rows, length)
    return pl.pallas_call(
        partial(attend_kernel, 0 if first_row is None else per_item),
        grid=(KW // 128,),
        out_shape=jax.ShapeDtypeStruct(queries.shape, BF),
        in_specs=[pl.BlockSpec(memory_space=pltpu.SMEM), by_query, by_key, by_value],
        out_specs=by_query,
        compiler_params=pltpu.CompilerParams(vmem_limit_bytes=56 * 1024 * 1024),
        cost_estimate=pl.CostEstimate(
            flops=4 * rows * length * QW,
            bytes_accessed=4 * rows * QW + 4 * length * KW,
            transcendentals=HQ * rows * length,
        ),
        name="attend",
    )(jnp.reshape(0 if first_row is None else first_row, (1,)), queries, keyvals, keyvals)


def attend_backward(queries, keyvals, first_row, per_item, d_mixed):
    rows, length = queries.shape[0], keyvals.shape[0]
    by_query, by_key, by_value = attend_specs(rows, length)
    d_queries, d_keys, d_values = pl.pallas_call(
        partial(attend_back_kernel, 0 if first_row is None else per_item),
        grid=(KW // 128,),
        out_shape=[
            jax.ShapeDtypeStruct(queries.shape, BF),
            jax.ShapeDtypeStruct((length, KW), BF),
            jax.ShapeDtypeStruct((length, KW), BF),
        ],
        in_specs=[pl.BlockSpec(memory_space=pltpu.SMEM), by_query, by_key, by_value, by_query],
        out_specs=[by_query, by_key, by_key],
        compiler_params=pltpu.CompilerParams(vmem_limit_bytes=56 * 1024 * 1024),
        cost_estimate=pl.CostEstimate(
            flops=10 * rows * length * QW,
            bytes_accessed=6 * rows * QW + 8 * length * KW,
            transcendentals=HQ * rows * length,
        ),
        name="attend_back",
    )(jnp.reshape(0 if first_row is None else first_row, (1,)), queries, keyvals, keyvals, d_mixed)
    return (d_queries, jnp.concatenate([d_keys, d_values], axis=1))


def update(weight, gradient, moment, average, rate, factor):
    clipped = gradient * factor
    moment_new = MOMENTUM * moment + (1 - MOMENTUM) * clipped
    weight_new = weight - rate * ((1 - MOMENTUM) * clipped + MOMENTUM * moment_new)
    average_new = AVERAGE * average + (1 - AVERAGE) * weight_new
    return (weight_new, moment_new, average_new)


def on_device(
    dp_axes,
    mp_axes,
    source_ids,
    target_ids,
    prefix,
    attn_in,
    attn_out,
    ff_in,
    ff_out,
    table,
    gains,
    attn_in_mom,
    attn_out_mom,
    ff_in_mom,
    ff_out_mom,
    table_mom,
    gains_mom,
    attn_in_avg,
    attn_out_avg,
    ff_in_avg,
    ff_out_avg,
    table_avg,
    gains_avg,
):
    every = dp_axes + mp_axes
    core = mp_axes[-1]
    row_axes = mp_axes[1:]
    line = mp_axes[:-1]
    gather_orders = (
        line + dp_axes + (core,),
        line + dp_axes[::-1] + (core,),
        dp_axes + line + (core,),
    )
    sum_orders = tuple(order[::-1] for order in gather_orders)
    last = (line[-1], core)
    three = (gather_orders[0], gather_orders[1], line[:-1] + dp_axes[::-1] + last)
    six_orders = three + three[:2] + (line[:-1] + dp_axes + last,)
    two_dp, two_mp, two_rows = (2,) * len(dp_axes), (2,) * len(mp_axes), (2,) * len(row_axes)

    seq_count, length = source_ids.shape
    rows = length // 2 ** len(row_axes)
    per_item = 2 ** len(row_axes)
    skip = PREFIX_LOW // per_item
    first_row = lax.axis_index(row_axes)

    def by_device(values):
        return values.reshape(values.shape[:-1] + (rows, per_item)).swapaxes(-1, -2)

    def with_skipped(values):
        return jnp.pad(values, ((rows - values.shape[0], 0), (0, 0)))


    vocab_part = table.shape[0]
    offset = lax.axis_index(mp_axes) * vocab_part
    table_bf = table.astype(BF)
    decoder_ids = jnp.concatenate(
        [jnp.zeros((seq_count, 1), jnp.int32), target_ids[:, :-1]], axis=1
    )
    ids_all = by_device(gather_blocks(jnp.stack([source_ids, decoder_ids]), dp_axes, dp_axes))
    ids_all = ids_all.reshape(-1, 2, 2 ** len(mp_axes), rows).transpose(1, 2, 0, 3).reshape(2, -1)
    table_rows = lax.all_gather(table_bf, dp_axes, axis=1, tiled=True)
    local_ids = ids_all - offset
    inside = (local_ids >= 0) & (local_ids < vocab_part)

    def trade(parts):
        for position, axis in enumerate(dp_axes):
            bit = lax.axis_index(axis)
            received = swap(take_bit(parts, 1 - bit, position), axis)
            kept = take_bit(parts, bit, position)
            parts = jnp.stack(
                [jnp.where(bit == 0, kept, received), jnp.where(bit == 0, received, kept)],
                axis=position,
            )
        return parts

    table_zero = jnp.pad(table, ((0, 8), (0, 0)))
    places = jnp.where(inside, local_ids, vocab_part)

    def look_up(which):
        found = rows_of(table_zero, places[which])
        return found.reshape(2 ** len(mp_axes), -1, found.shape[-1])

    def collect(found):
        return lax.psum_scatter(found, mp_axes, scatter_dimension=0)

    def embed(mine):
        width = mine.shape[-1]
        parts = trade(mine.reshape(two_dp + (rows, width))).reshape(-1, rows, width)
        return jnp.moveaxis(parts, 0, 1).reshape(rows, -1).astype(F32)

    found_e = look_up(0)
    mine_e = collect(found_e)
    found_d = look_up(1)
    mine_d = collect(found_d)

    gain_all = gather_blocks(gains.astype(BF).T, every, gather_orders[0])
    gain_all = gain_all.reshape(-1, gains.shape[0]).T.astype(F32)
    shards = [attn_in[0], attn_out[0], ff_in[0], ff_out[0]]
    shards += [attn_in[1], attn_out[1], attn_in[2], attn_out[2], ff_in[1], ff_out[1]]
    shards = [shard.astype(BF) for shard in shards]
    in_kernels = attn_in.shape[1] % 16 == 0
    if in_kernels:
        *shards, found_e, found_d, table_rows, gain_all = lax.optimization_barrier(
            shards + [found_e, found_d, table_rows, gain_all]
        )
        behind = (8, 9,)
        full = [None] * len(shards)
        ahead = [k for k in range(len(shards)) if k not in behind]
        for k, got in zip(ahead, gather_all([shards[k] for k in ahead], every, six_orders)):
            full[k] = got
        full[0], mine_e, mine_d = lax.optimization_barrier((full[0], mine_e, mine_d))
        stream_e, *sent = lax.optimization_barrier(
            [embed(mine_e)] + [shards[k] for k in behind]
        )
        for k, shard in zip(behind, sent):
            full[k] = lax.all_gather(shard, every, axis=0, tiled=True)
    else:
        stream_e = embed(mine_e)
        full = [
            gather_blocks(shard, every, gather_orders[k % 3]) for k, shard in enumerate(shards)
        ]
    full = [got.reshape((-1,) + shard.shape[1:]) for got, shard in zip(full, shards)]
    a_in, a_out = (full[0], full[4], full[6]), (full[1], full[5], full[7])
    f_in, f_out = (full[2], full[8]), (full[3], full[9])
    def spread_keys(own):
        return gather_blocks(own, row_axes, row_axes).reshape(length, -1)

    def attention_forward(stream, source, block, gain_row, start):
        normed = norm_forward(stream, gain_row).astype(BF)
        anchor = normed if source is None else source
        keyvals = spread_keys(mm(anchor, a_in[block][:, QW:]).astype(BF))
        first = 0 if start is None else skip
        queries = mm(normed[first:], a_in[block][:, :QW]).astype(BF)
        position = None if start is None else start + first * per_item
        mixed = attend_forward(queries, keyvals, position, per_item)
        out = stream[first:] + mm(mixed, a_out[block])
        return (out, (stream, normed, anchor, queries, keyvals, mixed))

    def ffn_forward(stream, which, gain_row):
        normed = norm_forward(stream, gain_row).astype(BF)
        both = mm(normed, f_in[which])
        hidden_act = (jax.nn.gelu(both[:, :FF], approximate=True) * both[:, FF:]).astype(BF)
        return (stream + mm(hidden_act, f_out[which]), (stream, normed, both, hidden_act))

    stream_e, enc_attn = attention_forward(stream_e, None, 0, gain_all[0], None)
    stream_e, mine_d = lax.optimization_barrier((stream_e, mine_d))
    stream_d = embed(mine_d)
    stream_d, dec_self = attention_forward(stream_d, None, 1, gain_all[3], first_row)
    stream_e, enc_ffn = ffn_forward(stream_e, 0, gain_all[1])
    encoded = norm_forward(stream_e, gain_all[2]).astype(BF)
    stream_d, dec_cross = attention_forward(stream_d, encoded, 2, gain_all[4], None)
    stream_d, dec_ffn = ffn_forward(stream_d, 1, gain_all[5])
    hidden = norm_forward(stream_d, gain_all[6]).astype(BF)

    hidden_all = gather_blocks(hidden, mp_axes, mp_axes).reshape(-1, hidden.shape[-1])
    targets = by_device(target_ids)[..., skip:].reshape(-1)
    vocab_ids = offset + jnp.arange(vocab_part)
    hits = vocab_ids[None, :] == targets[:, None]
    logits = mm_nt(hidden_all, table_rows) * D ** (-0.5)
    own_max = jnp.max(logits, axis=-1)
    expo = jnp.exp(logits - own_max[:, None])
    stats = jnp.stack(
        [own_max, jnp.sum(expo, axis=-1), jnp.sum(jnp.where(hits, logits, 0.0), axis=-1)]
    )
    expo = expo.astype(BF)
    for axis in mp_axes[::-1]:
        other = swap(stats, axis)
        joint = jnp.maximum(stats[0], other[0])
        stats = jnp.stack(
            [
                joint,
                stats[1] * jnp.exp(stats[0] - joint) + other[1] * jnp.exp(other[0] - joint),
                stats[2] + other[2],
            ]
        )
    log_norm = stats[0] + jnp.log(stats[1])
    prefix_group = lax.dynamic_slice_in_dim(prefix, lax.axis_index(dp_axes) * seq_count, seq_count)
    positions = by_device(jnp.arange(length))[..., skip:].reshape(1, -1)
    scored = (positions >= prefix_group[:, None]).astype(F32).reshape(-1)
    scored_count = jnp.sum((length - prefix).astype(F32))
    scale = jnp.exp(own_max - log_norm)
    d_logits = (
        (expo.astype(F32) * scale[:, None] - hits.astype(F32)) * (scored / scored_count)[:, None]
    ).astype(BF)
    d_final = (mm(d_logits, table_rows) * D ** (-0.5)).astype(BF)

    def table_term(held):
        _, rows_all = lax.optimization_barrier((held, hidden_all))
        return (mm_tn(d_logits, rows_all) * D ** (-0.5)).astype(BF)

    d_final, head_table = sum_blocks(
        d_final.reshape(two_mp + hidden.shape), mp_axes, mp_axes[::-1], F32, table_term
    )

    grad_table = lax.psum_scatter(head_table, dp_axes, scatter_dimension=1, tiled=True)

    def ffn_backward(saved, which, gain_row, d_stream):
        stream, normed, both, hidden_act = saved
        up_part = both[:, FF:]
        activated, gelu_pull = jax.vjp(partial(jax.nn.gelu, approximate=True), both[:, :FF])
        d_branch = d_stream.astype(BF)
        d_hidden = mm_nt(d_branch, f_out[which])
        d_both = jnp.concatenate(
            [gelu_pull(d_hidden * up_part)[0].astype(BF), (d_hidden * activated).astype(BF)], axis=1
        )
        d_normed = mm_nt(d_both, f_in[which])
        d_input, grad_gain = norm_backward(stream, gain_row, d_normed)
        return (d_stream + d_input, (normed, d_both, hidden_act, d_branch), grad_gain)

    def attention_backward(saved, cross, block, gain_row, start, d_stream):
        stream, normed, anchor, queries, keyvals, mixed = saved
        d_branch = d_stream.astype(BF)
        d_mixed = mm_nt(d_branch, a_out[block]).astype(BF)
        queries = with_skipped(queries)
        d_queries, d_keyvals = attend_backward(
            queries, keyvals, start, per_item, with_skipped(d_mixed)
        )
        d_keyvals = sum_blocks(
            d_keyvals.reshape(two_rows + (rows, -1)), row_axes, row_axes[::-1], BF
        )
        d_queries = d_queries[rows - stream.shape[0] :]
        d_normed = mm_nt(d_queries, a_in[block][:, :QW])
        d_anchor = mm_nt(d_keyvals, a_in[block][:, QW:])
        if not cross:
            d_normed = d_normed + d_anchor
        factors = (normed, anchor, d_queries, d_keyvals, mixed, d_branch)
        d_input, grad_gain = norm_backward(stream, gain_row, d_normed)
        if start is not None:
            d_stream = with_skipped(d_stream)
        return (d_stream + d_input, d_anchor, factors, grad_gain)

    d_y, gain6 = norm_backward(stream_d, gain_all[6], d_final)
    d_y, ffn_factors1, gain5 = ffn_backward(dec_ffn, 1, gain_all[5], d_y)
    d_y, d_encoded, attn_factors2, gain4 = attention_backward(
        dec_cross, True, 2, gain_all[4], None, d_y
    )
    d_y, _, attn_factors1, gain3 = attention_backward(
        dec_self, False, 1, gain_all[3], first_row, d_y
    )
    d_encoded, grad_table = lax.optimization_barrier((d_encoded, grad_table))
    d_x, gain2 = norm_backward(stream_e, gain_all[2], d_encoded)
    d_x, ffn_factors0, gain1 = ffn_backward(enc_ffn, 0, gain_all[1], d_x)
    d_x, _, attn_factors0, gain0 = attention_backward(
        enc_attn, False, 0, gain_all[0], None, d_x
    )

    def trade_rows(d_rows):
        width = table.shape[1]
        parts = jnp.moveaxis(d_rows.astype(BF).reshape(rows, -1, width), 1, 0)
        return trade(parts.reshape(two_dp + (rows, width))).reshape(-1, width)

    def look_back(which, spread):
        own_ids = local_ids[which].astype(jnp.int16)
        places = (own_ids[None, :] == jnp.arange(vocab_part, dtype=jnp.int16)[:, None]).astype(BF)
        return mm(places, spread.reshape(-1, spread.shape[-1]))

    traded_y, traded_x = trade_rows(d_y), trade_rows(d_x)
    spread_y, spread_x = (lax.all_gather(traded, mp_axes) for traded in (traded_y, traded_x))

    gain_grads = jnp.stack([gain0, gain1, gain2, gain3, gain4, gain5, gain6])
    gain_blocks = jnp.moveaxis(gain_grads.reshape(gains.shape[0], -1, gains.shape[1]), 1, 0)
    grad_gains = sum_blocks(
        gain_blocks.reshape((2,) * len(every) + gains.shape), every, sum_orders[0]
    )

    if in_kernels:
        traded_x, ffn_left, attn_left = lax.optimization_barrier(
            (traded_x, ffn_factors0[2], attn_factors0[0])
        )
        attn_factors0 = (attn_left, attn_left) + attn_factors0[2:]
        ffn_factors0 = ffn_factors0[:2] + (ffn_left,) + ffn_factors0[3:]
    lefts, rights, spans = [], [], []
    for normed, anchor, d_queries, d_keyvals, mixed, d_branch in (
        attn_factors0,
        attn_factors1,
        attn_factors2,
    ):
        lefts += [normed, mixed] if anchor is normed else [normed, anchor, mixed]
        rights += [d_queries, d_keyvals, d_branch]
        widths = [d_queries.shape[1], d_keyvals.shape[1]]
        spans += ([sum(widths)] if anchor is normed else widths) + [d_branch.shape[1]]
    wide_lefts, wide_rights = [], []
    for normed, d_both, hidden_act, d_branch in (ffn_factors0, ffn_factors1):
        lefts.append(normed)
        rights.append(d_both)
        spans.append(d_both.shape[1])
        wide_lefts.append(hidden_act)
        wide_rights.append(d_branch)
    wide_spans = [right.shape[1] for right in wide_rights]
    if in_kernels:
        back_orders = tuple(order[::-1] for order in three)
        six_back = tuple(order[::-1] for order in six_orders)
        own = grad_sums(lefts, rights, every, six_back, spans, 1, 128)
        wide = grad_sums(wide_lefts, wide_rights, every, back_orders[:2], wide_spans, 2)
        own, wide, spread_x, spread_y = lax.optimization_barrier((own, wide, spread_x, spread_y))
    else:

        def own_sum(left, right, kind):
            product = mm_tn(left, right).astype(BF)
            blocks = product.reshape((2,) * len(every) + (-1,) + product.shape[1:])
            return sum_blocks(blocks, every, sum_orders[kind % 3])

        everything = jnp.concatenate([with_skipped(right) for right in rights], axis=1)
        ends = [sum(spans[: k + 1]) for k in range(len(spans))]
        parts = jnp.split(everything, ends[:-1], axis=1)
        pairs = list(enumerate(zip([with_skipped(left) for left in lefts], parts)))
        own = jnp.concatenate([own_sum(*pair, k) for k, pair in pairs], axis=1)
        pairs = list(enumerate(zip(wide_lefts, wide_rights)))
        wide = jnp.concatenate([own_sum(*pair, k) for k, pair in pairs], axis=1)
    grad_table = grad_table.astype(F32) + look_back(1, spread_y) + look_back(0, spread_x)
    ends = (attn_in.shape[2], attn_in.shape[2] + attn_out.shape[2])
    ffn_from = 3 * ends[1]
    gradients = (
        jnp.stack([own[:, ends[1] * k : ends[1] * k + ends[0]] for k in range(3)]),
        jnp.stack([own[:, ends[1] * k + ends[0] : ends[1] * (k + 1)] for k in range(3)]),
        jnp.stack([own[:, ffn_from + 2 * FF * k : ffn_from + 2 * FF * (k + 1)] for k in range(2)]),
        jnp.stack(jnp.split(wide, 2, axis=1)),
        grad_table,
        grad_gains,
    )

    own_losses = ((log_norm - stats[2]) * scored).reshape(2 ** len(mp_axes), -1)
    loss_part = jnp.sum(take_bit(own_losses, lax.axis_index(mp_axes), 0))
    squares = sum((jnp.sum(gradient * gradient) for gradient in gradients))
    totals = jnp.stack([loss_part, squares])
    totals = total_of(totals, every[::-1], 3)
    loss_sum = totals[0]
    grad_norm = jnp.sqrt(totals[1])
    factor = jnp.minimum(1.0, CLIP / grad_norm)
    weights = (attn_in, attn_out, ff_in, ff_out, table, gains)
    moments = (attn_in_mom, attn_out_mom, ff_in_mom, ff_out_mom, table_mom, gains_mom)
    averages = (attn_in_avg, attn_out_avg, ff_in_avg, ff_out_avg, table_avg, gains_avg)
    results = [
        update(weight, gradient, moment, average, rate, factor)
        for weight, gradient, moment, average, rate in zip(
            weights, gradients, moments, averages, step_rates()
        )
    ]
    return (loss_sum, scored_count, grad_norm) + tuple(
        results[array][kind] for kind in range(3) for array in range(6)
    )


def solution(mesh):
    dp_count, mp_count = mesh.shape["dp"], mesh.shape["mp"]
    dp_axes = tuple(f"d{k}" for k in range(dp_count.bit_length() - 1))
    mp_axes = tuple(f"m{k}" for k in range(mp_count.bit_length() - 1))
    every = dp_axes + mp_axes
    fine = Mesh(mesh.devices.reshape((2,) * len(every)), every)
    rows_split = P(None, every, None)
    params = (rows_split,) * 4 + (P(mp_axes, dp_axes), P(None, every))
    in_specs = (P(dp_axes, None), P(dp_axes, None), P()) + params * 3
    out_specs = (P(), P(), P()) + params * 3
    return jax.shard_map(
        partial(on_device, dp_axes, mp_axes),
        mesh=fine,
        in_specs=in_specs,
        out_specs=out_specs,
        check_vma=False,
    )
```
